512 devices in a mesh: tm: 64 (over z, y), kv: 8 (over x, core).
Axes of the slice: x: 4, y: 8, z: 8, core: 2. Of those that a mesh axis runs over, the one named last changes fastest.
Arguments:
- frames: bfloat16 [12288, 512], P(('tm', 'kv')), may hold values from -6 to 6
- attn_gain: float32 [512], replicated, may hold values from 0.5 to 2
- w_query: bfloat16 [512, 512], replicated, may hold values from -14 to 14
- w_key: bfloat16 [512, 512], replicated, may hold values from -1 to 1
- w_value: bfloat16 [512, 512], replicated, may hold values from -0.25 to 0.25
- w_out: bfloat16 [512, 512], replicated, may hold values from -0.25 to 0.25
- conv_gain: float32 [512], replicated, may hold values from 0.5 to 2
- w_expand: bfloat16 [512, 1024], replicated, may hold values from -0.25 to 0.25
- kernel: float32 [31, 512], replicated, may hold values from -1 to 1
- bn_scale: float32 [512], replicated, may hold values from 0.5 to 2
- bn_shift: float32 [512], replicated, may hold values from -3 to 3
- w_project: bfloat16 [512, 512], replicated, may hold values from -0.25 to 0.25
Outputs:
- attended: bfloat16 [12288, 512], P(('tm', 'kv'))
- layer_out: bfloat16 [12288, 512], P(('tm', 'kv'))
The draws below stay inside these ranges and needn't reach their ends.
All inputs are finite; a program needn't handle non-finite values.
Results may differ from the reference program's by a relative error of at most 0.02.
Values may be sent and summed in bfloat16 or wider, within the bound.
A program may use at most 64 MiB of HBM per device.

```python
import math
import jax
import jax.numpy as jnp
from jax import lax

D = 512
HEADS = 8
HEAD_DIM = 64
KERNEL = 31
HD = 512
FRAMES = 12288


def shared_rows(key):
    return jnp.clip(jax.random.normal(key, (D, HD), jnp.float32), -4.0, 4.0) / math.sqrt(D)


def draw_w_key(key, part):
    shared = shared_rows(key)
    return shared.astype(jnp.bfloat16)


def draw_w_query(key, part):
    key = jax.random.fold_in(key, 5)
    own = jnp.clip(jax.random.normal(key, (D, HD), jnp.float32), -4.0, 4.0) * math.sqrt(6.0 / D)
    return own.astype(jnp.bfloat16)


def levels(stream_key, dims, split, least, largest):
    level = 1.0
    for axis_at, blocks in split:
        heights = jax.random.uniform(jax.random.fold_in(jax.random.fold_in(stream_key, 6), axis_at), (blocks,), jnp.float32, least / len(split), largest / len(split))
        level = level * jnp.repeat(jnp.exp(heights), dims[axis_at] // blocks).reshape((-1,) + (1,) * (len(dims) - 1 - axis_at))
    return level


def normal_values(own_key, dims, scale, most, shards=(), kind=jnp.bfloat16):
    array = jax.random.normal(own_key, dims, jnp.float32) * scale
    if len(shards) > 0:
        array = levels(own_key, dims, shards, -0.22, 0.18) * array
    return jnp.clip(array, min=-most, max=most).astype(kind)


def setup_inputs(seed: int = 0) -> dict:
    key_list = jax.random.split(jax.random.key(seed), 13)
    return {
        "frames": normal_values(key_list[0], (FRAMES, D), 1.0, 6.0, ((0, 512),)),
        "attn_gain": jnp.clip(jnp.exp(jax.random.uniform(key_list[1], (D,), jnp.float32, math.log(0.5), math.log(2.0))), 0.5, 2.0),
        "w_query": draw_w_query(jax.random.fold_in(key_list[12], 71), 0),
        "w_key": draw_w_key(jax.random.fold_in(key_list[12], 71), 0),
        "w_value": normal_values(key_list[4], (D, HD), D ** -0.5, 0.25),
        "w_out": normal_values(key_list[5], (HD, D), HD ** -0.5, 0.25),
        "conv_gain": jnp.clip(jnp.exp(jax.random.uniform(key_list[6], (D,), jnp.float32, math.log(0.5), math.log(2.0))), 0.5, 2.0),
        "w_expand": normal_values(key_list[7], (D, 2 * D), D ** -0.5, 0.25),
        "kernel": normal_values(key_list[8], (KERNEL, D), KERNEL ** -0.5, 1.0, (), jnp.float32),
        "bn_scale": jnp.clip(jnp.exp(jax.random.uniform(key_list[9], (D,), jnp.float32, math.log(0.5), math.log(2.0))), 0.5, 2.0),
        "bn_shift": normal_values(key_list[10], (D,), 0.5, 3.0, (), jnp.float32),
        "w_project": normal_values(key_list[11], (D, D), D ** -0.5, 0.25),
    }


def layer_norm(values, gain):
    mean = lax.optimization_barrier(jnp.mean(values, axis=-1, keepdims=True))
    centered = values - mean
    var = lax.optimization_barrier(jnp.mean(centered * centered, axis=-1, keepdims=True))
    return centered / jnp.sqrt(var + 1e-05) * gain

def rotate(heads_in, positions):
    half = HEAD_DIM // 2
    inverse = 10000.0 ** (-(jnp.arange(half, dtype=jnp.float32) * 2.0) / HEAD_DIM)
    angle = positions.astype(jnp.float32)[:, None] * inverse[None, :]
    cosine = jnp.cos(angle)[:, None, :]
    sine = jnp.sin(angle)[:, None, :]
    first = heads_in[..., :half]
    second = heads_in[..., half:]
    return jnp.concatenate([first * cosine - second * sine, second * cosine + first * sine], axis=-1)

def reference(frames, attn_gain, w_query, w_key, w_value, w_out, conv_gain, w_expand, kernel, bn_scale, bn_shift, w_project):
    inputs = frames.astype(jnp.float32)
    normed = layer_norm(inputs, attn_gain).astype(jnp.bfloat16)
    positions = jnp.arange(FRAMES, dtype=jnp.int32)
    q_full = jnp.dot(normed, w_query, preferred_element_type=jnp.float32).reshape(FRAMES, HEADS, HEAD_DIM)
    queries = (rotate(q_full, positions) * 0.125).astype(jnp.bfloat16)
    k_full = jnp.dot(normed, w_key, preferred_element_type=jnp.float32).reshape(FRAMES, HEADS, HEAD_DIM)
    keys = rotate(k_full, positions).astype(jnp.bfloat16).astype(jnp.float32)
    values = jnp.dot(normed, w_value, preferred_element_type=jnp.float32).astype(jnp.bfloat16)
    values = values.reshape(FRAMES, HEADS, HEAD_DIM).astype(jnp.float32)
    block = math.gcd(FRAMES, 512)

    def attend(query_block):
        score = jnp.einsum('qhd,khd->hqk', query_block.astype(jnp.float32), keys)
        top = lax.optimization_barrier(jnp.max(score, axis=-1, keepdims=True))
        weight = jnp.exp(score - top)
        total = lax.optimization_barrier(jnp.sum(weight, axis=-1))
        rounded = weight.astype(jnp.bfloat16).astype(jnp.float32)
        mixed = jnp.einsum('hqk,khd->qhd', rounded, values)
        mixed = mixed / jnp.transpose(total)[:, :, None]
        return mixed.reshape(query_block.shape[0], HD).astype(jnp.bfloat16)
    context = lax.map(attend, queries.reshape(FRAMES // block, block, HEADS, HEAD_DIM))
    context = context.reshape(FRAMES, HD)
    attended = jnp.dot(context, w_out, preferred_element_type=jnp.float32).astype(jnp.bfloat16)
    mid = inputs + lax.optimization_barrier(attended).astype(jnp.float32)
    conv_in = layer_norm(mid, conv_gain).astype(jnp.bfloat16)
    expanded = jnp.dot(conv_in, w_expand, preferred_element_type=jnp.float32)
    glu = (expanded[:, :D] * jax.nn.sigmoid(expanded[:, D:])).astype(jnp.bfloat16)
    half_width = (KERNEL - 1) // 2
    padded = jnp.pad(lax.optimization_barrier(glu).astype(jnp.float32), ((half_width, half_width), (0, 0)))
    depth = jnp.zeros((FRAMES, D), jnp.float32)
    for tap in range(KERNEL):
        depth = depth + kernel[tap][None, :] * padded[tap:tap + FRAMES]
    act = jax.nn.silu(depth * bn_scale + bn_shift).astype(jnp.bfloat16)
    layer_out = (mid + jnp.dot(act, w_project, preferred_element_type=jnp.float32)).astype(jnp.bfloat16)
    return (attended, layer_out)
```

```python
import functools
import math

import jax
import jax.numpy as jnp
from jax import lax
from jax.experimental import pallas as pl
from jax.experimental.pallas import tpu as pltpu
from jax.sharding import PartitionSpec as P

HEAD_DIM = 64
HALF = HEAD_DIM // 2
LANES = 128
HALO = 16
WINDOW = 64
MESH = pl.DeviceIdType.MESH
BF16 = jnp.bfloat16
F32 = jnp.float32


def layer_norm(values, gain):
    mean = jnp.mean(values, axis=-1, keepdims=True)
    centered = values - mean
    var = jnp.mean(centered * centered, axis=-1, keepdims=True)
    return centered / jnp.sqrt(var + 1e-05) * gain


def matmul(a, b):
    return jnp.dot(a, b, preferred_element_type=F32)


def folded(rows):
    half = rows.shape[0] // 2
    lane = lax.broadcasted_iota(jnp.int32, (half, LANES), 1)
    return jnp.where(lane < HEAD_DIM, pltpu.roll(rows[:half], HEAD_DIM, 1), rows[half:]).astype(BF16)


def all_heads(ref):
    columns = []
    lane = lax.broadcasted_iota(jnp.int32, ref.shape[1:], 1)
    for pair in range(ref.shape[0] // 2):
        even = ref[2 * pair].astype(F32)
        odd = ref[2 * pair + 1].astype(F32)
        top = jnp.where(lane < HEAD_DIM, even, pltpu.roll(odd, HEAD_DIM, 1))
        bottom = jnp.where(lane < HEAD_DIM, pltpu.roll(even, HEAD_DIM, 1), odd)
        columns.append(jnp.concatenate([top, bottom], axis=0))
    return jnp.concatenate(columns, axis=1)


def layer_kernel(
    side,
    frames_hbm,
    attn_gain_hbm,
    conv_gain_hbm,
    taps_hbm,
    scale_hbm,
    shift_hbm,
    w_query_hbm,
    w_key_hbm,
    w_value_hbm,
    w_out_hbm,
    w_expand_hbm,
    w_project_hbm,
    attended_hbm,
    layer_hbm,
    attended_ref,
    layer_ref,
    frames_ref,
    attn_gain_ref,
    conv_gain_ref,
    taps_ref,
    scale_ref,
    shift_ref,
    w_query,
    w_key,
    w_value,
    w_out,
    w_expand,
    w_project,
    head_send,
    head_recv,
    kv_all,
    kv_wide,
    q_all,
    part_send,
    part_recv,
    ctx_send,
    ctx_recv,
    edge_send,
    edge_recv,
    context,
    halo_send,
    halo_recv,
    padded,
    load_sem,
    store_sem,
    head_ssem,
    head_rsem,
    kv_ssem,
    kv_rsem,
    q_ssem,
    q_rsem,
    part_ssem,
    part_rsem,
    ctx_ssem,
    ctx_rsem,
    edge_ssem,
    edge_rsem,
    halo_ssem,
    halo_rsem,
):
    rows, width = frames_ref.shape
    groups = head_send.shape[0]
    block = rows * groups
    half_block = block // 2
    blocks = side * side
    tm = lax.axis_index("tm")
    kv = lax.axis_index("kv")
    core = kv % 2
    slow = tm // side
    fast = tm % side
    key_at = fast + core * (slow - fast)
    key_stride = 1 + core * (side - 1)
    query_at = slow + core * (fast - slow)
    query_stride = side - core * (side - 1)

    def kv_peer(d):
        return (tm, (kv + d) % groups)

    def key_peer(d):
        return (tm + ((key_at + d) % side - key_at) * key_stride, kv)

    def query_peer(d):
        return (tm + ((query_at + d) % side - query_at) * query_stride, kv)

    devices = groups * blocks
    me = tm * groups + kv
    following = (me + 1) % devices
    preceding = (me + devices - 1) % devices
    following = (following // groups, following % groups)
    preceding = (preceding // groups, preceding % groups)
    later = (tm + 1) % blocks
    earlier = (tm + blocks - 1) % blocks
    near = sorted(range(1, side), key=lambda d: min(d, side - d))

    def greet(device):
        pl.semaphore_signal(barrier, inc=1, device_id=device, device_id_type=MESH)

    loads = [
        pltpu.make_async_copy(source, target, load_sem.at[i])
        for i, (source, target) in enumerate(
            (
                (frames_hbm, frames_ref),
                (attn_gain_hbm, attn_gain_ref),
                (w_key_hbm, w_key),
                (w_value_hbm, w_value),
                (w_query_hbm, w_query),
                (w_out_hbm, w_out),
                (conv_gain_hbm, conv_gain_ref),
                (w_expand_hbm, w_expand),
                (taps_hbm, taps_ref),
                (scale_hbm, scale_ref),
                (shift_hbm, shift_ref),
                (w_project_hbm, w_project),
            )
        )
    ]
    for load in loads[:5]:
        load.start()

    barrier = pltpu.get_barrier_semaphore()
    for d in range(1, groups):
        greet(kv_peer(d))
    for d in range(1, side):
        greet(key_peer(d))
        greet(query_peer(d))

    @pl.when(kv == groups - 1)
    def _():
        for head in range(groups):
            greet((later, head))

    @pl.when(kv == 0)
    def _():
        for head in range(groups):
            greet((earlier, head))

    lane = lax.broadcasted_iota(jnp.int32, (rows, LANES), 1)
    low = lane < HEAD_DIM
    first_half = lane % HEAD_DIM < HALF
    which = lax.broadcasted_iota(jnp.int32, (1, LANES), 1) % HALF
    inverse = jnp.zeros((1, LANES), F32)
    for i in range(HALF):
        inverse = jnp.where(which == i, 10000.0 ** (-2.0 * i / HEAD_DIM), inverse)
    positions = me * rows + lax.broadcasted_iota(jnp.int32, (rows, LANES), 0)
    angle = positions.astype(F32) * inverse
    cosine = jnp.cos(angle)
    sine = jnp.sin(angle)
    sine = jnp.where(first_half, -sine, sine)

    def rotated(part):
        swapped = jnp.where(
            first_half, pltpu.roll(part, LANES - HALF, 1), pltpu.roll(part, HALF, 1)
        )
        return part * cosine + swapped * sine

    loads[0].wait()
    loads[1].wait()
    inputs = frames_ref[...].astype(F32)
    halo_send[0] = inputs[:HALO].astype(BF16)
    halo_send[1] = inputs[rows - HALO :].astype(BF16)
    normed = layer_norm(inputs, attn_gain_ref[...]).astype(BF16)
    loads[2].wait()
    keys = matmul(normed, w_key[...])
    loads[3].wait()
    values = matmul(normed, w_value[...])
    loads[4].wait()
    queries = matmul(normed, w_query[...])
    to_log2 = 0.125 / math.log(2.0)
    for pair in range(groups // 2):
        at = slice(pair * LANES, (pair + 1) * LANES)
        key = rotated(keys[:, at])
        query = rotated(queries[:, at]) * to_log2
        value = values[:, at]
        key_value = jnp.where(low, key, pltpu.roll(value, HEAD_DIM, 1))
        head_send[2 * pair] = jnp.concatenate(
            [key_value, jnp.where(low, query, 0.0)], axis=0
        ).astype(BF16)
        key_value = jnp.where(low, pltpu.roll(key, HEAD_DIM, 1), value)
        head_send[2 * pair + 1] = jnp.concatenate(
            [key_value, jnp.where(low, pltpu.roll(query, HEAD_DIM, 1), 0.0)], axis=0
        ).astype(BF16)

    pl.semaphore_wait(barrier, groups - 1 + 2 * (side - 1) + 2)

    head_copies = [
        pltpu.make_async_remote_copy(
            src_ref=head_send.at[(kv + d) % groups],
            dst_ref=head_recv.at[kv],
            send_sem=head_ssem.at[d],
            recv_sem=head_rsem.at[d],
            device_id=kv_peer(d),
            device_id_type=MESH,
        )
        for d in range(1, groups)
    ]
    for copy in head_copies:
        copy.start()
    halo_copies = [
        pltpu.make_async_remote_copy(
            src_ref=halo_send.at[i],
            dst_ref=halo_recv.at[i],
            send_sem=halo_ssem.at[i],
            recv_sem=halo_rsem.at[i],
            device_id=target,
            device_id_type=MESH,
        )
        for i, target in enumerate((preceding, following))
    ]
    for copy in halo_copies:
        copy.start()
    for load in loads[5:]:
        load.start()
    head_recv[kv] = head_send[kv]
    kv_wide[:, LANES:] = jnp.ones((kv_wide.shape[0], LANES), BF16)
    for copy in head_copies:
        copy.wait_recv()
    pieces = [head_recv[head].astype(F32) for head in range(groups)]
    own_block = jnp.concatenate([piece[:rows] for piece in pieces], axis=0).astype(BF16)
    kv_all[0] = own_block

    def kv_copy(d):
        return pltpu.make_async_remote_copy(
            src_ref=kv_all.at[0],
            dst_ref=kv_all.at[d],
            send_sem=kv_ssem.at[d],
            recv_sem=kv_rsem.at[d],
            device_id=key_peer(d),
            device_id_type=MESH,
        )

    def q_copy(d):
        return pltpu.make_async_remote_copy(
            src_ref=q_all.at[0],
            dst_ref=q_all.at[d],
            send_sem=q_ssem.at[d],
            recv_sem=q_rsem.at[d],
            device_id=query_peer(d),
            device_id_type=MESH,
        )

    for d in near:
        kv_copy(d).start()
    own_queries = jnp.concatenate([piece[rows:] for piece in pieces], axis=0)
    q_all[0] = (
        own_queries[:half_block] + pltpu.roll(own_queries[half_block:], HEAD_DIM, 1)
    ).astype(BF16)
    for d in near:
        q_copy(d).start()

    kv_wide[0:block, :LANES] = own_block
    for d in near:
        kv_copy(d).wait_recv()
        kv_wide[d * block : (d + 1) * block, :LANES] = kv_all[d]

    half_lane = lax.broadcasted_iota(jnp.int32, (half_block, LANES), 1)
    block_lane = lax.broadcasted_iota(jnp.int32, (block, LANES), 1)
    step_lane = lax.broadcasted_iota(jnp.int32, (2 * block, LANES), 1)

    def unfolded(d):
        packed = q_all[d].astype(F32)
        return [
            jnp.where(half_lane < HEAD_DIM, packed, 0.0),
            jnp.where(half_lane < HEAD_DIM, pltpu.roll(packed, HEAD_DIM, 1), 0.0),
        ]

    def attend(first, second):
        query = jnp.concatenate(unfolded(first) + unfolded(second), axis=0).astype(BF16)
        score = lax.dot_general(
            query, kv_wide[:, :LANES], (((1,), (1,)), ((), ())), preferred_element_type=F32
        )
        top = jnp.max(score, axis=1, keepdims=True)
        weight = jnp.exp2(score - top).astype(BF16)
        mixed = matmul(weight, kv_wide[...])
        total = mixed[:, LANES:]
        level = top + jnp.log2(total)
        high = level.astype(BF16).astype(F32)
        part = jnp.where(
            step_lane >= HEAD_DIM,
            mixed[:, :LANES] / total,
            jnp.where(step_lane < HALF, high, level - high),
        ).astype(BF16)
        part_send[first] = part[:block]
        part_send[second] = part[block:]

    def part_copy(d):
        return pltpu.make_async_remote_copy(
            src_ref=part_send.at[d],
            dst_ref=part_recv.at[d],
            send_sem=part_ssem.at[d],
            recv_sem=part_rsem.at[d],
            device_id=query_peer(side - d),
            device_id_type=MESH,
        )

    order = [0] + near[2:] + near[:2]

    def in_order(step):
        return sum((step == i).astype(jnp.int32) * d for i, d in enumerate(order))

    @pl.loop(0, side // 2)
    def _(step):
        first = in_order(2 * step)
        second = in_order(2 * step + 1)

        @pl.when(step > 0)
        def _():
            q_copy(first).wait_recv()

        q_copy(second).wait_recv()
        attend(first, second)

        @pl.when(step > 0)
        def _():
            part_copy(first).start()

        part_copy(second).start()

    part_recv[0] = part_send[0]
    for d in range(1, side):
        part_copy(d).wait_recv()

    parts = part_recv[...].reshape(side * block, LANES)
    pick = lax.broadcasted_iota(jnp.int32, (LANES, LANES), 0)
    pick = jnp.where((pick == 0) | (pick == HALF), 1.0, 0.0).astype(BF16)
    levels = matmul(parts, pick).reshape(side, block, LANES)
    parts = parts.astype(F32).reshape(side, block, LANES)
    fades = jnp.exp2(levels - jnp.max(levels, axis=0, keepdims=True))
    merged = jnp.sum(fades * parts, axis=0) / jnp.sum(fades, axis=0)

    edge_send[0] = folded(merged[: 2 * HALO])
    edge_send[1] = folded(merged[block - 2 * HALO :])
    framed = jnp.concatenate(
        [jnp.zeros((HALO, LANES), F32), merged, jnp.zeros((WINDOW - rows - HALO, LANES), F32)],
        axis=0,
    )
    for part in range(groups):
        ctx_send[part] = folded(framed[part * rows : part * rows + WINDOW])

    def edge_copy(i, head):
        return pltpu.make_async_remote_copy(
            src_ref=edge_send.at[i],
            dst_ref=edge_recv.at[head],
            send_sem=edge_ssem.at[i],
            recv_sem=edge_rsem.at[head],
            device_id=((earlier, groups - 1), (later, 0))[i],
            device_id_type=MESH,
        )

    for i in range(2):
        edge_copy(i, kv).start()
    ctx_copies = [
        pltpu.make_async_remote_copy(
            src_ref=ctx_send.at[(kv + d) % groups],
            dst_ref=ctx_recv.at[kv],
            send_sem=ctx_ssem.at[d],
            recv_sem=ctx_rsem.at[d],
            device_id=kv_peer(d),
            device_id_type=MESH,
        )
        for d in range(1, groups)
    ]
    for copy in ctx_copies:
        copy.start()
    ctx_recv[kv] = ctx_send[kv]
    for load in loads[5:]:
        load.wait()
    for copy in halo_copies:
        copy.wait_recv()
    extent = rows + 2 * HALO
    nearby = jnp.concatenate([halo_recv[1].astype(F32), inputs, halo_recv[0].astype(F32)], axis=0)
    for copy in ctx_copies:
        copy.wait_recv()
    context[...] = all_heads(ctx_recv)[:extent]

    @pl.when(kv == 0)
    def _():
        for head in range(groups):
            edge_copy(1, head).wait_recv()
        context[:HALO] = all_heads(edge_recv)[HALO:]

    @pl.when(kv == groups - 1)
    def _():
        for head in range(groups):
            edge_copy(0, head).wait_recv()
        context[extent - HALO :] = all_heads(edge_recv)[:HALO]

    attended = matmul(context[...].astype(BF16), w_out[...]).astype(BF16).astype(F32)
    attended_ref[...] = attended[HALO : HALO + rows].astype(BF16)
    stores = [
        pltpu.make_async_copy(attended_ref, attended_hbm, store_sem.at[0]),
        pltpu.make_async_copy(layer_ref, layer_hbm, store_sem.at[1]),
    ]
    stores[0].start()
    mid = nearby + attended
    conv_in = layer_norm(mid, conv_gain_ref[...]).astype(BF16)
    expanded = matmul(conv_in, w_expand[...])
    gate = expanded[:, width:]
    glu = (expanded[:, :width] / (1.0 + jnp.exp(-gate))).astype(BF16).astype(F32)
    times = me * rows - HALO + lax.broadcasted_iota(jnp.int32, (extent, width), 0)
    padded[...] = jnp.where((times >= 0) & (times < devices * rows), glu, 0.0)

    depth = jnp.zeros((rows, width), F32)
    count = taps_ref.shape[0]
    for turn in range(8):
        shifted = None
        for tap in range(turn - 1, count, 8):
            if tap < 0:
                continue
            term = taps_ref[tap : tap + 1] * padded[tap + 1 - turn : tap + 9 - turn + rows]
            shifted = term if shifted is None else shifted + term
        depth = depth + shifted[turn : turn + rows]
    batch = depth * scale_ref[...] + shift_ref[...]
    act = (batch / (1.0 + jnp.exp(-batch))).astype(BF16)
    layer_ref[...] = (mid[HALO : HALO + rows] + matmul(act, w_project[...])).astype(BF16)
    stores[1].start()

    for copy in head_copies + halo_copies + ctx_copies:
        copy.wait_send()
    for d in range(1, side):
        kv_copy(d).wait_send()
        q_copy(d).wait_send()
        part_copy(d).wait_send()
    for i in range(2):
        edge_copy(i, kv).wait_send()
    for store in stores:
        store.wait()


def copy_kernel(attended_in, layer_in, attended_out, layer_out, sem):
    copies = [
        pltpu.make_async_copy(attended_in, attended_out, sem.at[0]),
        pltpu.make_async_copy(layer_in, layer_out, sem.at[1]),
    ]
    for copy in copies:
        copy.start()
    for copy in copies:
        copy.wait()


def on_device(
    frames,
    attn_gain,
    w_query,
    w_key,
    w_value,
    w_out,
    conv_gain,
    w_expand,
    kernel,
    bn_scale,
    bn_shift,
    w_project,
):
    rows, width = frames.shape
    groups = lax.axis_size("kv")
    side = math.isqrt(lax.axis_size("tm"))
    block = rows * groups
    anywhere = pl.BlockSpec(memory_space=pl.ANY)
    dma = pltpu.SemaphoreType.DMA
    results = pl.pallas_call(
        functools.partial(layer_kernel, side),
        out_shape=(
            jax.ShapeDtypeStruct((rows, width), BF16),
            jax.ShapeDtypeStruct((rows, width), BF16),
        ),
        in_specs=[anywhere] * 12,
        out_specs=(anywhere, anywhere),
        scratch_shapes=[
            pltpu.VMEM((rows, width), BF16),
            pltpu.VMEM((rows, width), BF16),
            pltpu.VMEM((rows, width), BF16),
            pltpu.VMEM((1, width), F32),
            pltpu.VMEM((1, width), F32),
            pltpu.VMEM(kernel.shape, F32),
            pltpu.VMEM((1, width), F32),
            pltpu.VMEM((1, width), F32),
            pltpu.VMEM((width, width), BF16),
            pltpu.VMEM((width, width), BF16),
            pltpu.VMEM((width, width), BF16),
            pltpu.VMEM((width, width), BF16),
            pltpu.VMEM((width, 2 * width), BF16),
            pltpu.VMEM((width, width), BF16),
            pltpu.VMEM((groups, 2 * rows, LANES), BF16),
            pltpu.VMEM((groups, 2 * rows, LANES), BF16),
            pltpu.VMEM((side, block, LANES), BF16),
            pltpu.VMEM((side * block, 2 * LANES), BF16),
            pltpu.VMEM((side, block // 2, LANES), BF16),
            pltpu.VMEM((side, block, LANES), BF16),
            pltpu.VMEM((side, block, LANES), BF16),
            pltpu.VMEM((groups, WINDOW // 2, LANES), BF16),
            pltpu.VMEM((groups, WINDOW // 2, LANES), BF16),
            pltpu.VMEM((2, HALO, LANES), BF16),
            pltpu.VMEM((groups, HALO, LANES), BF16),
            pltpu.VMEM((rows + 2 * HALO, width), F32),
            pltpu.VMEM((2, HALO, width), BF16),
            pltpu.VMEM((2, HALO, width), BF16),
            pltpu.VMEM((rows + 2 * HALO, width), F32),
            dma((12,)),
            dma((2,)),
            dma((groups,)),
            dma((groups,)),
            dma((side,)),
            dma((side,)),
            dma((side,)),
            dma((side,)),
            dma((side,)),
            dma((side,)),
            dma((groups,)),
            dma((groups,)),
            dma((2,)),
            dma((groups,)),
            dma((2,)),
            dma((2,)),
        ],
        compiler_params=pltpu.CompilerParams(
            collective_id=0, has_side_effects=True, vmem_limit_bytes=60 * 1024 * 1024
        ),
    )(
        frames,
        attn_gain.reshape(1, width),
        conv_gain.reshape(1, width),
        kernel,
        bn_scale.reshape(1, width),
        bn_shift.reshape(1, width),
        w_query,
        w_key,
        w_value,
        w_out,
        w_expand,
        w_project,
    )
    return pl.pallas_call(
        copy_kernel,
        out_shape=tuple(jax.ShapeDtypeStruct(r.shape, r.dtype) for r in results),
        in_specs=[anywhere] * 2,
        out_specs=(anywhere, anywhere),
        scratch_shapes=[dma((2,))],
        compiler_params=pltpu.CompilerParams(vmem_limit_bytes=60 * 1024 * 1024),
    )(*results)


def solution(mesh):
    rows = P(("tm", "kv"), None)
    return jax.shard_map(
        on_device,
        mesh=mesh,
        in_specs=(rows,) + (P(),) * 11,
        out_specs=(rows, rows),
        check_vma=False,
    )
```

```python
import functools
import math

import jax
import jax.numpy as jnp
from jax import lax
from jax.experimental import pallas as pl
from jax.experimental.pallas import tpu as pltpu
from jax.sharding import PartitionSpec as P

HEAD_DIM = 64
HALF = HEAD_DIM // 2
LANES = 128
HALO = 16
WINDOW = 64
CHUNK = 32
MESH = pl.DeviceIdType.MESH
BF16 = jnp.bfloat16
F32 = jnp.float32


def layer_norm(values, gain):
    mean = jnp.mean(values, axis=-1, keepdims=True)
    centered = values - mean
    var = jnp.mean(centered * centered, axis=-1, keepdims=True)
    return centered / jnp.sqrt(var + 1e-05) * gain


def matmul(a, b):
    return jnp.dot(a, b, preferred_element_type=F32)


def folded(rows):
    half = rows.shape[0] // 2
    lane = lax.broadcasted_iota(jnp.int32, (half, LANES), 1)
    return jnp.where(lane < HEAD_DIM, pltpu.roll(rows[:half], HEAD_DIM, 1), rows[half:]).astype(BF16)


def all_heads(ref):
    columns = []
    lane = lax.broadcasted_iota(jnp.int32, ref.shape[1:], 1)
    for pair in range(ref.shape[0] // 2):
        even = ref[2 * pair].astype(F32)
        odd = ref[2 * pair + 1].astype(F32)
        top = jnp.where(lane < HEAD_DIM, even, pltpu.roll(odd, HEAD_DIM, 1))
        bottom = jnp.where(lane < HEAD_DIM, pltpu.roll(even, HEAD_DIM, 1), odd)
        columns.append(jnp.concatenate([top, bottom], axis=0))
    return jnp.concatenate(columns, axis=1)


def layer_kernel(
    side,
    frames_hbm,
    gains_hbm,
    taps_hbm,
    w_query_hbm,
    w_key_hbm,
    w_value_hbm,
    w_out_hbm,
    w_expand_hbm,
    w_project_hbm,
    attended_ref,
    layer_ref,
    frames_ref,
    gains_ref,
    taps_ref,
    w_query,
    w_key,
    w_value,
    w_out,
    w_expand,
    w_project,
    head_send,
    head_recv,
    kv_all,
    kv_wide,
    key_rows,
    q_all,
    scores,
    weights,
    tops,
    part_send,
    part_recv,
    ctx_send,
    ctx_recv,
    edge_send,
    edge_recv,
    context,
    halo_send,
    halo_recv,
    padded,
    load_sem,
    head_ssem,
    head_rsem,
    kv_ssem,
    kv_rsem,
    q_ssem,
    q_rsem,
    part_ssem,
    part_rsem,
    ctx_ssem,
    ctx_rsem,
    edge_ssem,
    edge_rsem,
    halo_ssem,
    halo_rsem,
):
    rows, width = frames_ref.shape
    groups = head_send.shape[0]
    block = rows * groups
    half_block = block // 2
    blocks = side * side
    tm = lax.axis_index("tm")
    kv = lax.axis_index("kv")
    core = kv % 2
    slow = tm // side
    fast = tm % side
    key_at = fast + core * (slow - fast)
    key_stride = 1 + core * (side - 1)
    query_at = slow + core * (fast - slow)
    query_stride = side - core * (side - 1)

    def kv_peer(d):
        return (tm, (kv + d) % groups)

    def key_peer(d):
        return (tm + ((key_at + d) % side - key_at) * key_stride, kv)

    def query_peer(d):
        return (tm + ((query_at + d) % side - query_at) * query_stride, kv)

    devices = groups * blocks
    me = tm * groups + kv
    following = (me + 1) % devices
    preceding = (me + devices - 1) % devices
    following = (following // groups, following % groups)
    preceding = (preceding // groups, preceding % groups)
    later = (tm + 1) % blocks
    earlier = (tm + blocks - 1) % blocks
    near = sorted(range(1, side), key=lambda d: min(d, side - d))

    def greet(device):
        pl.semaphore_signal(barrier, inc=1, device_id=device, device_id_type=MESH)

    loads = [
        pltpu.make_async_copy(source, target, load_sem.at[i])
        for i, (source, target) in enumerate(
            (
                (frames_hbm, frames_ref),
                (gains_hbm, gains_ref),
                (w_key_hbm, w_key),
                (w_value_hbm, w_value),
                (w_query_hbm, w_query),
                (w_out_hbm, w_out),
                (w_expand_hbm, w_expand),
                (taps_hbm, taps_ref),
                (w_project_hbm, w_project),
            )
        )
    ]
    for load in loads[:5]:
        load.start()

    barrier = pltpu.get_barrier_semaphore()
    for d in range(1, groups):
        greet(kv_peer(d))
    for d in range(1, side):
        greet(key_peer(d))
        greet(query_peer(d))

    @pl.when(kv == groups - 1)
    def _():
        for head in range(groups):
            greet((later, head))

    @pl.when(kv == 0)
    def _():
        for head in range(groups):
            greet((earlier, head))

    lane = lax.broadcasted_iota(jnp.int32, (rows, LANES), 1)
    low = lane < HEAD_DIM
    first_half = lane % HEAD_DIM < HALF
    which = lax.broadcasted_iota(jnp.int32, (1, LANES), 1) % HALF
    inverse = jnp.zeros((1, LANES), F32)
    for i in range(HALF):
        inverse = jnp.where(which == i, 10000.0 ** (-2.0 * i / HEAD_DIM), inverse)
    positions = me * rows + lax.broadcasted_iota(jnp.int32, (rows, LANES), 0)
    angle = positions.astype(F32) * inverse
    cosine = jnp.cos(angle)
    sine = jnp.sin(angle)
    sine = jnp.where(first_half, -sine, sine)

    def rotated(part):
        swapped = jnp.where(
            first_half, pltpu.roll(part, LANES - HALF, 1), pltpu.roll(part, HALF, 1)
        )
        return part * cosine + swapped * sine

    loads[0].wait()
    loads[1].wait()
    inputs = frames_ref[...].astype(F32)
    halo_send[0] = inputs[:HALO].astype(BF16)
    halo_send[1] = inputs[rows - HALO :].astype(BF16)
    normed = layer_norm(inputs, gains_ref[0:1]).astype(BF16)
    loads[2].wait()
    keys = matmul(normed, w_key[...])
    loads[3].wait()
    values = matmul(normed, w_value[...])
    loads[4].wait()
    queries = matmul(normed, w_query[...])
    to_log2 = 0.125 / math.log(2.0)
    for pair in range(groups // 2):
        at = slice(pair * LANES, (pair + 1) * LANES)
        key = rotated(keys[:, at])
        query = rotated(queries[:, at]) * to_log2
        value = values[:, at]
        key_value = jnp.where(low, key, pltpu.roll(value, HEAD_DIM, 1))
        head_send[2 * pair] = jnp.concatenate(
            [key_value, jnp.where(low, query, 0.0)], axis=0
        ).astype(BF16)
        key_value = jnp.where(low, pltpu.roll(key, HEAD_DIM, 1), value)
        head_send[2 * pair + 1] = jnp.concatenate(
            [key_value, jnp.where(low, pltpu.roll(query, HEAD_DIM, 1), 0.0)], axis=0
        ).astype(BF16)

    pl.semaphore_wait(barrier, groups - 1 + 2 * (side - 1) + 2)

    head_copies = [
        pltpu.make_async_remote_copy(
            src_ref=head_send.at[(kv + d) % groups],
            dst_ref=head_recv.at[kv],
            send_sem=head_ssem.at[d],
            recv_sem=head_rsem.at[d],
            device_id=kv_peer(d),
            device_id_type=MESH,
        )
        for d in range(1, groups)
    ]
    for copy in head_copies:
        copy.start()
    halo_copies = [
        pltpu.make_async_remote_copy(
            src_ref=halo_send.at[i],
            dst_ref=halo_recv.at[i],
            send_sem=halo_ssem.at[i],
            recv_sem=halo_rsem.at[i],
            device_id=target,
            device_id_type=MESH,
        )
        for i, target in enumerate((preceding, following))
    ]
    for copy in halo_copies:
        copy.start()
    for load in loads[5:]:
        load.start()
    head_recv[kv] = head_send[kv]
    kv_wide[:, LANES:] = jnp.ones((kv_wide.shape[0], LANES), BF16)
    for copy in head_copies:
        copy.wait_recv()
    pieces = [head_recv[head].astype(F32) for head in range(groups)]
    own_block = jnp.concatenate([piece[:rows] for piece in pieces], axis=0).astype(BF16)
    kv_all[0] = own_block

    def line_copies(ref, ssem, rsem, peer):
        half = ref.shape[1] // 2
        lower, upper = pl.ds(0, half), pl.ds(half, half)

        def copy(source, target, place, sem):
            return pltpu.make_async_remote_copy(
                src_ref=source,
                dst_ref=target,
                send_sem=ssem.at[sem],
                recv_sem=rsem.at[sem],
                device_id=peer(place),
                device_id_type=MESH,
            )

        if side < 8:
            return {d: copy(ref.at[0], ref.at[d], d, d) for d in near}, {}
        direct = {d: copy(ref.at[0], ref.at[d], d, d) for d in near[:4]}
        relayed = {
            2: {
                3: copy(ref.at[2], ref.at[3], 1, 3),
                4: copy(ref.at[2, lower], ref.at[4, lower], 2, 4),
            },
            6: {
                5: copy(ref.at[6], ref.at[5], 7, 5),
                0: copy(ref.at[6, upper], ref.at[4, upper], 6, 0),
            },
        }
        return direct, relayed

    kv_direct, kv_relayed = line_copies(kv_all, kv_ssem, kv_rsem, key_peer)
    q_direct, q_relayed = line_copies(q_all, q_ssem, q_rsem, query_peer)
    lines = ((kv_direct, kv_relayed), (q_direct, q_relayed))
    for copy in kv_direct.values():
        copy.start()
    own_queries = jnp.concatenate([piece[rows:] for piece in pieces], axis=0)
    q_all[0] = (
        own_queries[:half_block] + pltpu.roll(own_queries[half_block:], HEAD_DIM, 1)
    ).astype(BF16)
    for copy in q_direct.values():
        copy.start()
    for direct, relayed in lines:
        for d, onward in relayed.items():
            direct[d].wait_recv()
            for copy in onward.values():
                copy.start()
    for direct, relayed in lines:
        for d, copy in direct.items():
            if d not in relayed:
                copy.wait_recv()
        for onward in relayed.values():
            for copy in onward.values():
                copy.wait_recv()
    kv_wide[:, :LANES] = kv_all[...].reshape(side * block, LANES)
    for d in range(0, side, 2):
        both = kv_all[d : d + 2].astype(F32).reshape(2 * block, LANES)
        key_rows[:, d * block : (d + 2) * block] = both.T.astype(BF16)

    half_lane = lax.broadcasted_iota(jnp.int32, (half_block, LANES), 1)
    block_lane = lax.broadcasted_iota(jnp.int32, (block, LANES), 1)
    step_lane = lax.broadcasted_iota(jnp.int32, (2 * block, LANES), 1)

    def unfolded(d):
        packed = q_all[d].astype(F32)
        return [
            jnp.where(half_lane < HEAD_DIM, packed, 0.0),
            jnp.where(half_lane < HEAD_DIM, pltpu.roll(packed, HEAD_DIM, 1), 0.0),
        ]

    def attend(first, second):
        query = jnp.concatenate(unfolded(first) + unfolded(second), axis=0).astype(BF16)
        scores[...] = matmul(query, key_rows[...])
        for begin in range(0, 2 * block, CHUNK):
            at = slice(begin, begin + CHUNK)
            score = scores[at]
            top = jnp.max(score, axis=1, keepdims=True)
            weights[at] = jnp.exp2(score - top).astype(BF16)
            tops[at] = jnp.broadcast_to(top, (CHUNK, LANES))
        mixed = matmul(weights[...], kv_wide[...])
        total = mixed[:, LANES:]
        level = tops[...] + jnp.log2(total)
        high = level.astype(BF16).astype(F32)
        part = jnp.where(
            step_lane >= HEAD_DIM,
            mixed[:, :LANES] / total,
            jnp.where(step_lane < HALF, high, level - high),
        ).astype(BF16)
        part_send[first] = part[:block]
        part_send[second] = part[block:]

    def part_copy(d):
        return pltpu.make_async_remote_copy(
            src_ref=part_send.at[d],
            dst_ref=part_recv.at[d],
            send_sem=part_ssem.at[d],
            recv_sem=part_rsem.at[d],
            device_id=query_peer(side - d),
            device_id_type=MESH,
        )

    order = [0] + near[::-1]

    def in_order(step):
        return sum((step == i).astype(jnp.int32) * d for i, d in enumerate(order))

    @pl.loop(0, side // 2)
    def _(step):
        first = in_order(2 * step)
        second = in_order(2 * step + 1)

        attend(first, second)

        @pl.when(step > 0)
        def _():
            part_copy(first).start()

        part_copy(second).start()

    part_recv[0] = part_send[0]
    for d in range(1, side):
        part_copy(d).wait_recv()

    parts = part_recv[...].reshape(side * block, LANES)
    pick = lax.broadcasted_iota(jnp.int32, (LANES, LANES), 0)
    pick = jnp.where((pick == 0) | (pick == HALF), 1.0, 0.0).astype(BF16)
    levels = matmul(parts, pick).reshape(side, block, LANES)
    parts = parts.astype(F32).reshape(side, block, LANES)
    fades = jnp.exp2(levels - jnp.max(levels, axis=0, keepdims=True))
    merged = jnp.sum(fades * parts, axis=0) / jnp.sum(fades, axis=0)

    edge_send[0] = folded(merged[: 2 * HALO])
    edge_send[1] = folded(merged[block - 2 * HALO :])
    framed = jnp.concatenate(
        [jnp.zeros((HALO, LANES), F32), merged, jnp.zeros((WINDOW - rows - HALO, LANES), F32)],
        axis=0,
    )
    for part in range(groups):
        ctx_send[part] = folded(framed[part * rows : part * rows + WINDOW])

    def edge_copy(i, head):
        return pltpu.make_async_remote_copy(
            src_ref=edge_send.at[i],
            dst_ref=edge_recv.at[head],
            send_sem=edge_ssem.at[i],
            recv_sem=edge_rsem.at[head],
            device_id=((earlier, groups - 1), (later, 0))[i],
            device_id_type=MESH,
        )

    for i in range(2):
        edge_copy(i, kv).start()
    ctx_copies = [
        pltpu.make_async_remote_copy(
            src_ref=ctx_send.at[(kv + d) % groups],
            dst_ref=ctx_recv.at[kv],
            send_sem=ctx_ssem.at[d],
            recv_sem=ctx_rsem.at[d],
            device_id=kv_peer(d),
            device_id_type=MESH,
        )
        for d in range(1, groups)
    ]
    for copy in ctx_copies:
        copy.start()
    ctx_recv[kv] = ctx_send[kv]
    for load in loads[5:]:
        load.wait()
    for copy in halo_copies:
        copy.wait_recv()
    extent = rows + 2 * HALO
    nearby = jnp.concatenate([halo_recv[1].astype(F32), inputs, halo_recv[0].astype(F32)], axis=0)
    for copy in ctx_copies:
        copy.wait_recv()
    context[...] = all_heads(ctx_recv)[:extent]

    @pl.when(kv == 0)
    def _():
        for head in range(groups):
            edge_copy(1, head).wait_recv()
        context[:HALO] = all_heads(edge_recv)[HALO:]

    @pl.when(kv == groups - 1)
    def _():
        for head in range(groups):
            edge_copy(0, head).wait_recv()
        context[extent - HALO :] = all_heads(edge_recv)[:HALO]

    attended = matmul(context[...].astype(BF16), w_out[...]).astype(BF16).astype(F32)
    attended_ref[...] = attended[HALO : HALO + rows].astype(BF16)
    mid = nearby + attended
    conv_in = layer_norm(mid, gains_ref[1:2]).astype(BF16)
    expanded = matmul(conv_in, w_expand[...])
    gate = expanded[:, width:]
    glu = (expanded[:, :width] / (1.0 + jnp.exp(-gate))).astype(BF16).astype(F32)
    times = me * rows - HALO + lax.broadcasted_iota(jnp.int32, (extent, width), 0)
    padded[...] = jnp.where((times >= 0) & (times < devices * rows), glu, 0.0)

    depth = jnp.zeros((rows, width), F32)
    count = taps_ref.shape[0]
    for turn in range(8):
        shifted = None
        for tap in range(turn - 1, count, 8):
            if tap < 0:
                continue
            term = taps_ref[tap : tap + 1] * padded[tap + 1 - turn : tap + 9 - turn + rows]
            shifted = term if shifted is None else shifted + term
        depth = depth + shifted[turn : turn + rows]
    batch = depth * gains_ref[2:3] + gains_ref[3:4]
    act = (batch / (1.0 + jnp.exp(-batch))).astype(BF16)
    layer_ref[...] = (mid[HALO : HALO + rows] + matmul(act, w_project[...])).astype(BF16)

    for copy in head_copies + halo_copies + ctx_copies:
        copy.wait_send()
    for d in range(1, side):
        part_copy(d).wait_send()
    for direct, relayed in lines:
        for copy in direct.values():
            copy.wait_send()
        for onward in relayed.values():
            for copy in onward.values():
                copy.wait_send()
    for i in range(2):
        edge_copy(i, kv).wait_send()


def copy_kernel(attended_in, layer_in, attended_out, layer_out, sem):
    copies = [
        pltpu.make_async_copy(attended_in, attended_out, sem.at[0]),
        pltpu.make_async_copy(layer_in, layer_out, sem.at[1]),
    ]
    for copy in copies:
        copy.start()
    for copy in copies:
        copy.wait()


def on_device(
    frames,
    attn_gain,
    w_query,
    w_key,
    w_value,
    w_out,
    conv_gain,
    w_expand,
    kernel,
    bn_scale,
    bn_shift,
    w_project,
):
    rows, width = frames.shape
    groups = lax.axis_size("kv")
    side = math.isqrt(lax.axis_size("tm"))
    block = rows * groups
    vmem = pl.BlockSpec(memory_space=pltpu.VMEM)
    anywhere = pl.BlockSpec(memory_space=pl.ANY)
    dma = pltpu.SemaphoreType.DMA
    results = pl.pallas_call(
        functools.partial(layer_kernel, side),
        out_shape=(
            jax.ShapeDtypeStruct((rows, width), BF16),
            jax.ShapeDtypeStruct((rows, width), BF16),
        ),
        in_specs=[anywhere] * 9,
        out_specs=(vmem, vmem),
        scratch_shapes=[
            pltpu.VMEM((rows, width), BF16),
            pltpu.VMEM((4, width), F32),
            pltpu.VMEM(kernel.shape, F32),
            pltpu.VMEM((width, width), BF16),
            pltpu.VMEM((width, width), BF16),
            pltpu.VMEM((width, width), BF16),
            pltpu.VMEM((width, width), BF16),
            pltpu.VMEM((width, 2 * width), BF16),
            pltpu.VMEM((width, width), BF16),
            pltpu.VMEM((groups, 2 * rows, LANES), BF16),
            pltpu.VMEM((groups, 2 * rows, LANES), BF16),
            pltpu.VMEM((side, block, LANES), BF16),
            pltpu.VMEM((side * block, 2 * LANES), BF16),
            pltpu.VMEM((LANES, side * block), BF16),
            pltpu.VMEM((side, block // 2, LANES), BF16),
            pltpu.VMEM((2 * block, side * block), F32),
            pltpu.VMEM((2 * block, side * block), BF16),
            pltpu.VMEM((2 * block, LANES), F32),
            pltpu.VMEM((side, block, LANES), BF16),
            pltpu.VMEM((side, block, LANES), BF16),
            pltpu.VMEM((groups, WINDOW // 2, LANES), BF16),
            pltpu.VMEM((groups, WINDOW // 2, LANES), BF16),
            pltpu.VMEM((2, HALO, LANES), BF16),
            pltpu.VMEM((groups, HALO, LANES), BF16),
            pltpu.VMEM((rows + 2 * HALO, width), F32),
            pltpu.VMEM((2, HALO, width), BF16),
            pltpu.VMEM((2, HALO, width), BF16),
            pltpu.VMEM((rows + 2 * HALO, width), F32),
            dma((9,)),
            dma((groups,)),
            dma((groups,)),
            dma((side,)),
            dma((side,)),
            dma((side,)),
            dma((side,)),
            dma((side,)),
            dma((side,)),
            dma((groups,)),
            dma((groups,)),
            dma((2,)),
            dma((groups,)),
            dma((2,)),
            dma((2,)),
        ],
        compiler_params=pltpu.CompilerParams(
            collective_id=0, has_side_effects=True, vmem_limit_bytes=55160 * 1024
        ),
    )(
        frames,
        jnp.stack([attn_gain, conv_gain, bn_scale, bn_shift]),
        kernel,
        w_query,
        w_key,
        w_value,
        w_out,
        w_expand,
        w_project,
    )
    return pl.pallas_call(
        copy_kernel,
        out_shape=tuple(jax.ShapeDtypeStruct(r.shape, r.dtype) for r in results),
        in_specs=[vmem] * 2,
        out_specs=(anywhere, anywhere),
        scratch_shapes=[dma((2,))],
        compiler_params=pltpu.CompilerParams(vmem_limit_bytes=4 * 1024 * 1024),
    )(*results)


def solution(mesh):
    rows = P(("tm", "kv"), None)
    return jax.shard_map(
        on_device,
        mesh=mesh,
        in_specs=(rows,) + (P(),) * 11,
        out_specs=(rows, rows),
        check_vma=False,
    )
```

```python
import functools
import math

import jax
import jax.numpy as jnp
from jax import lax
from jax.experimental import pallas as pl
from jax.experimental.pallas import tpu as pltpu
from jax.sharding import PartitionSpec as P

HEAD_DIM = 64
HALF = HEAD_DIM // 2
LANES = 128
HALO = 16
WINDOW = 64
CHUNK = 32
MESH = pl.DeviceIdType.MESH
BF16 = jnp.bfloat16
F32 = jnp.float32


def layer_norm(values, gain):
    mean = jnp.mean(values, axis=-1, keepdims=True)
    centered = values - mean
    var = jnp.mean(centered * centered, axis=-1, keepdims=True)
    return centered / jnp.sqrt(var + 1e-05) * gain


def matmul(a, b):
    return jnp.dot(a, b, preferred_element_type=F32)


def folded(rows):
    half = rows.shape[0] // 2
    lane = lax.broadcasted_iota(jnp.int32, (half, LANES), 1)
    return jnp.where(lane < HEAD_DIM, pltpu.roll(rows[:half], HEAD_DIM, 1), rows[half:]).astype(BF16)


def all_heads(ref):
    columns = []
    lane = lax.broadcasted_iota(jnp.int32, ref.shape[1:], 1)
    for pair in range(ref.shape[0] // 2):
        even = ref[2 * pair].astype(F32)
        odd = ref[2 * pair + 1].astype(F32)
        top = jnp.where(lane < HEAD_DIM, even, pltpu.roll(odd, HEAD_DIM, 1))
        bottom = jnp.where(lane < HEAD_DIM, pltpu.roll(even, HEAD_DIM, 1), odd)
        columns.append(jnp.concatenate([top, bottom], axis=0))
    return jnp.concatenate(columns, axis=1)


def layer_kernel(
    side,
    frames_hbm,
    attn_gain_hbm,
    conv_gain_hbm,
    scale_hbm,
    shift_hbm,
    taps_hbm,
    w_query_hbm,
    w_key_hbm,
    w_value_hbm,
    w_out_hbm,
    w_expand_hbm,
    w_project_hbm,
    attended_hbm,
    layer_hbm,
    attended_ref,
    layer_ref,
    frames_ref,
    gains_ref,
    taps_ref,
    w_query,
    w_key,
    w_value,
    w_out,
    w_expand,
    w_project,
    head_send,
    head_recv,
    kv_all,
    near_wide,
    far_wide,
    near_keys,
    far_keys,
    q_all,
    near_scores,
    far_scores,
    near_weights,
    far_weights,
    tops,
    first_mixed,
    first_tops,
    part_send,
    part_recv,
    ctx_send,
    ctx_recv,
    edge_send,
    edge_recv,
    context,
    halo_send,
    halo_recv,
    padded,
    load_sem,
    store_sem,
    head_ssem,
    head_rsem,
    kv_ssem,
    kv_rsem,
    q_ssem,
    q_rsem,
    part_ssem,
    part_rsem,
    ctx_ssem,
    ctx_rsem,
    edge_ssem,
    edge_rsem,
    halo_ssem,
    halo_rsem,
):
    rows, width = frames_ref.shape
    groups = head_send.shape[0]
    block = rows * groups
    half_block = block // 2
    blocks = side * side
    tm = lax.axis_index("tm")
    kv = lax.axis_index("kv")
    core = kv % 2
    slow = tm // side
    fast = tm % side
    key_at = fast + core * (slow - fast)
    key_stride = 1 + core * (side - 1)
    query_at = slow + core * (fast - slow)
    query_stride = side - core * (side - 1)

    def kv_peer(d):
        return (tm, (kv + d) % groups)

    def key_peer(d):
        return (tm + ((key_at + d) % side - key_at) * key_stride, kv)

    def query_peer(d):
        return (tm + ((query_at + d) % side - query_at) * query_stride, kv)

    devices = groups * blocks
    me = tm * groups + kv
    following = (me + 1) % devices
    preceding = (me + devices - 1) % devices
    following = (following // groups, following % groups)
    preceding = (preceding // groups, preceding % groups)
    later = (tm + 1) % blocks
    earlier = (tm + blocks - 1) % blocks
    near = sorted(range(1, side), key=lambda d: min(d, side - d))

    def greet(device):
        pl.semaphore_signal(barrier, inc=1, device_id=device, device_id_type=MESH)

    loads = [
        pltpu.make_async_copy(source, target, load_sem.at[i])
        for i, (source, target) in enumerate(
            (
                (frames_hbm, frames_ref),
                (attn_gain_hbm, gains_ref.at[0:1]),
                (w_key_hbm, w_key),
                (w_value_hbm, w_value),
                (w_query_hbm, w_query),
                (w_out_hbm, w_out),
                (w_expand_hbm, w_expand),
                (taps_hbm, taps_ref),
                (conv_gain_hbm, gains_ref.at[1:2]),
                (scale_hbm, gains_ref.at[2:3]),
                (shift_hbm, gains_ref.at[3:4]),
                (w_project_hbm, w_project),
            )
        )
    ]
    for load in loads[:5]:
        load.start()

    barrier = pltpu.get_barrier_semaphore()
    for d in range(1, groups):
        greet(kv_peer(d))
    for d in range(1, side):
        greet(key_peer(d))
        greet(query_peer(d))

    @pl.when(kv == groups - 1)
    def _():
        for head in range(groups):
            greet((later, head))

    @pl.when(kv == 0)
    def _():
        for head in range(groups):
            greet((earlier, head))

    lane = lax.broadcasted_iota(jnp.int32, (rows, LANES), 1)
    low = lane < HEAD_DIM
    first_half = lane % HEAD_DIM < HALF
    which = lax.broadcasted_iota(jnp.int32, (1, LANES), 1) % HALF
    inverse = jnp.zeros((1, LANES), F32)
    for i in range(HALF):
        inverse = jnp.where(which == i, 10000.0 ** (-2.0 * i / HEAD_DIM), inverse)
    positions = me * rows + lax.broadcasted_iota(jnp.int32, (rows, LANES), 0)
    angle = positions.astype(F32) * inverse
    cosine = jnp.cos(angle)
    sine = jnp.sin(angle)
    sine = jnp.where(first_half, -sine, sine)

    def rotated(part):
        swapped = jnp.where(
            first_half, pltpu.roll(part, LANES - HALF, 1), pltpu.roll(part, HALF, 1)
        )
        return part * cosine + swapped * sine

    loads[0].wait()
    loads[1].wait()
    inputs = frames_ref[...].astype(F32)
    halo_send[0] = inputs[:HALO].astype(BF16)
    halo_send[1] = inputs[rows - HALO :].astype(BF16)
    normed = layer_norm(inputs, gains_ref[0:1]).astype(BF16)
    loads[2].wait()
    keys = matmul(normed, w_key[...])
    loads[3].wait()
    values = matmul(normed, w_value[...])
    loads[4].wait()
    queries = matmul(normed, w_query[...])
    to_log2 = 0.125 / math.log(2.0)
    for pair in range(groups // 2):
        at = slice(pair * LANES, (pair + 1) * LANES)
        key = rotated(keys[:, at])
        query = rotated(queries[:, at]) * to_log2
        value = values[:, at]
        key_value = jnp.where(low, key, pltpu.roll(value, HEAD_DIM, 1))
        head_send[2 * pair] = jnp.concatenate(
            [key_value, jnp.where(low, query, 0.0)], axis=0
        ).astype(BF16)
        key_value = jnp.where(low, pltpu.roll(key, HEAD_DIM, 1), value)
        head_send[2 * pair + 1] = jnp.concatenate(
            [key_value, jnp.where(low, pltpu.roll(query, HEAD_DIM, 1), 0.0)], axis=0
        ).astype(BF16)

    pl.semaphore_wait(barrier, groups - 1 + 2 * (side - 1) + 2)

    head_copies = [
        pltpu.make_async_remote_copy(
            src_ref=head_send.at[(kv + d) % groups],
            dst_ref=head_recv.at[kv],
            send_sem=head_ssem.at[d],
            recv_sem=head_rsem.at[d],
            device_id=kv_peer(d),
            device_id_type=MESH,
        )
        for d in range(1, groups)
    ]
    for copy in head_copies:
        copy.start()
    halo_copies = [
        pltpu.make_async_remote_copy(
            src_ref=halo_send.at[i],
            dst_ref=halo_recv.at[i],
            send_sem=halo_ssem.at[i],
            recv_sem=halo_rsem.at[i],
            device_id=target,
            device_id_type=MESH,
        )
        for i, target in enumerate((preceding, following))
    ]
    for copy in halo_copies:
        copy.start()
    for load in loads[5:]:
        load.start()
    head_recv[kv] = head_send[kv]
    for wide in (near_wide, far_wide):
        wide[:, LANES:] = jnp.ones((wide.shape[0], LANES), BF16)
    for copy in head_copies:
        copy.wait_recv()
    pieces = [head_recv[head].astype(F32) for head in range(groups)]
    own_block = jnp.concatenate([piece[:rows] for piece in pieces], axis=0).astype(BF16)
    kv_all[0] = own_block

    def line_copies(ref, ssem, rsem, peer):
        half = ref.shape[1] // 2
        lower, upper = pl.ds(0, half), pl.ds(half, half)

        def copy(source, target, place, sem):
            return pltpu.make_async_remote_copy(
                src_ref=source,
                dst_ref=target,
                send_sem=ssem.at[sem],
                recv_sem=rsem.at[sem],
                device_id=peer(place),
                device_id_type=MESH,
            )

        if side < 8:
            return {d: copy(ref.at[0], ref.at[d], d, d) for d in near}, {}
        direct = {d: copy(ref.at[0], ref.at[d], d, d) for d in near[:4]}
        relayed = {
            2: {
                3: copy(ref.at[2], ref.at[3], 1, 3),
                4: copy(ref.at[2, lower], ref.at[4, lower], 2, 4),
            },
            6: {
                5: copy(ref.at[6], ref.at[5], 7, 5),
                0: copy(ref.at[6, upper], ref.at[4, upper], 6, 0),
            },
        }
        return direct, relayed

    kv_direct, kv_relayed = line_copies(kv_all, kv_ssem, kv_rsem, key_peer)
    q_direct, q_relayed = line_copies(q_all, q_ssem, q_rsem, query_peer)
    lines = ((kv_direct, kv_relayed), (q_direct, q_relayed))
    for copy in kv_direct.values():
        copy.start()
    own_queries = jnp.concatenate([piece[rows:] for piece in pieces], axis=0)
    q_all[0] = (
        own_queries[:half_block] + pltpu.roll(own_queries[half_block:], HEAD_DIM, 1)
    ).astype(BF16)
    for copy in q_direct.values():
        copy.start()
    for direct, relayed in lines:
        for d, onward in relayed.items():
            direct[d].wait_recv()
            for copy in onward.values():
                copy.start()
    slots = [0] + near
    near_slots = slots[: near_wide.shape[0] // block]
    far_slots = slots[len(near_slots) :]

    def wait_for(wanted):
        for direct, relayed in lines:
            for d, copy in direct.items():
                if d in wanted and d not in relayed:
                    copy.wait_recv()
            for onward in relayed.values():
                for d, copy in onward.items():
                    if (d or 4) in wanted:
                        copy.wait_recv()

    def lay_out(wanted, wide, keys):
        for i in range(0, len(wanted), 2):
            few = wanted[i : i + 2]
            both = jnp.concatenate([kv_all[d] for d in few], axis=0)
            at = slice(i * block, (i + len(few)) * block)
            wide[at, :LANES] = both
            keys[:, at] = both.astype(F32).T.astype(BF16)

    half_lane = lax.broadcasted_iota(jnp.int32, (half_block, LANES), 1)
    block_lane = lax.broadcasted_iota(jnp.int32, (block, LANES), 1)

    def unfolded(d):
        packed = q_all[d].astype(F32)
        return jnp.concatenate(
            [
                jnp.where(half_lane < HEAD_DIM, packed, 0.0),
                jnp.where(half_lane < HEAD_DIM, pltpu.roll(packed, HEAD_DIM, 1), 0.0),
            ],
            axis=0,
        ).astype(BF16)

    def soften(pieces, floor=None):
        for begin in range(0, block, CHUNK):
            at = slice(begin, begin + CHUNK)
            score = [scores[at] for scores, _ in pieces]
            top = functools.reduce(
                jnp.maximum, [jnp.max(part, axis=1, keepdims=True) for part in score]
            )
            if floor is not None:
                top = jnp.maximum(top, floor[at, :1])
            for part, (_, weights) in zip(score, pieces):
                weights[at] = jnp.exp2(part - top).astype(BF16)
            tops[at] = jnp.broadcast_to(top, (CHUNK, LANES))

    def finish(d, mixed):
        total = mixed[:, LANES:]
        level = tops[...] + jnp.log2(total)
        high = level.astype(BF16).astype(F32)
        part_send[d] = jnp.where(
            block_lane >= HEAD_DIM,
            mixed[:, :LANES] / total,
            jnp.where(block_lane < HALF, high, level - high),
        ).astype(BF16)

    def chosen(step, order):
        return sum((step == i).astype(jnp.int32) * d for i, d in enumerate(order))

    wait_for(near_slots)
    lay_out(near_slots, near_wide, near_keys)

    @pl.loop(0, len(near_slots))
    def _(step):
        near_scores[...] = matmul(unfolded(chosen(step, near_slots)), near_keys[...])
        soften([(near_scores, near_weights)])
        first_mixed[step] = matmul(near_weights[...], near_wide[...])
        first_tops[step] = tops[...]

    wait_for(far_slots)
    lay_out(far_slots, far_wide, far_keys)

    def part_copy(d):
        return pltpu.make_async_remote_copy(
            src_ref=part_send.at[d],
            dst_ref=part_recv.at[d],
            send_sem=part_ssem.at[d],
            recv_sem=part_rsem.at[d],
            device_id=query_peer(side - d),
            device_id_type=MESH,
        )

    @pl.loop(0, len(far_slots))
    def _(step):
        d = chosen(step, far_slots[::-1])
        query = unfolded(d)
        near_scores[...] = matmul(query, near_keys[...])
        far_scores[...] = matmul(query, far_keys[...])
        soften([(near_scores, near_weights), (far_scores, far_weights)])
        mixed = matmul(near_weights[...], near_wide[...])
        finish(d, mixed + matmul(far_weights[...], far_wide[...]))
        part_copy(d).start()

    @pl.loop(0, len(near_slots))
    def _(step):
        at = len(near_slots) - 1 - step
        d = chosen(at, near_slots)
        far_scores[...] = matmul(unfolded(d), far_keys[...])
        soften([(far_scores, far_weights)], first_tops.at[at])
        fade = jnp.exp2(first_tops[at] - tops[...])
        mixed = first_mixed[at] * jnp.concatenate([fade, fade], axis=1)
        finish(d, mixed + matmul(far_weights[...], far_wide[...]))

        @pl.when(at > 0)
        def _():
            part_copy(d).start()

    part_recv[0] = part_send[0]
    for d in range(1, side):
        part_copy(d).wait_recv()

    parts = part_recv[...].reshape(side * block, LANES)
    pick = lax.broadcasted_iota(jnp.int32, (LANES, LANES), 0)
    pick = jnp.where((pick == 0) | (pick == HALF), 1.0, 0.0).astype(BF16)
    levels = matmul(parts, pick).reshape(side, block, LANES)
    parts = parts.astype(F32).reshape(side, block, LANES)
    fades = jnp.exp2(levels - jnp.max(levels, axis=0, keepdims=True))
    merged = jnp.sum(fades * parts, axis=0) / jnp.sum(fades, axis=0)

    edge_send[0] = folded(merged[: 2 * HALO])
    edge_send[1] = folded(merged[block - 2 * HALO :])
    framed = jnp.concatenate(
        [jnp.zeros((HALO, LANES), F32), merged, jnp.zeros((WINDOW - rows - HALO, LANES), F32)],
        axis=0,
    )
    for part in range(groups):
        ctx_send[part] = folded(framed[part * rows : part * rows + WINDOW])

    def edge_copy(i, head):
        return pltpu.make_async_remote_copy(
            src_ref=edge_send.at[i],
            dst_ref=edge_recv.at[head],
            send_sem=edge_ssem.at[i],
            recv_sem=edge_rsem.at[head],
            device_id=((earlier, groups - 1), (later, 0))[i],
            device_id_type=MESH,
        )

    for i in range(2):
        edge_copy(i, kv).start()
    ctx_copies = [
        pltpu.make_async_remote_copy(
            src_ref=ctx_send.at[(kv + d) % groups],
            dst_ref=ctx_recv.at[kv],
            send_sem=ctx_ssem.at[d],
            recv_sem=ctx_rsem.at[d],
            device_id=kv_peer(d),
            device_id_type=MESH,
        )
        for d in range(1, groups)
    ]
    for copy in ctx_copies:
        copy.start()
    ctx_recv[kv] = ctx_send[kv]
    for load in loads[5:]:
        load.wait()
    for copy in halo_copies:
        copy.wait_recv()
    extent = rows + 2 * HALO
    nearby = jnp.concatenate([halo_recv[1].astype(F32), inputs, halo_recv[0].astype(F32)], axis=0)
    for copy in ctx_copies:
        copy.wait_recv()
    context[...] = all_heads(ctx_recv)[:extent]

    @pl.when(kv == 0)
    def _():
        for head in range(groups):
            edge_copy(1, head).wait_recv()
        context[:HALO] = all_heads(edge_recv)[HALO:]

    @pl.when(kv == groups - 1)
    def _():
        for head in range(groups):
            edge_copy(0, head).wait_recv()
        context[extent - HALO :] = all_heads(edge_recv)[:HALO]

    attended = matmul(context[...].astype(BF16), w_out[...]).astype(BF16).astype(F32)
    attended_ref[...] = attended[HALO : HALO + rows].astype(BF16)
    stores = [
        pltpu.make_async_copy(attended_ref, attended_hbm, store_sem.at[0]),
        pltpu.make_async_copy(layer_ref, layer_hbm, store_sem.at[1]),
    ]
    stores[0].start()
    mid = nearby + attended
    conv_in = layer_norm(mid, gains_ref[1:2]).astype(BF16)
    expanded = matmul(conv_in, w_expand[...])
    gate = expanded[:, width:]
    glu = (expanded[:, :width] / (1.0 + jnp.exp(-gate))).astype(BF16).astype(F32)
    times = me * rows - HALO + lax.broadcasted_iota(jnp.int32, (extent, width), 0)
    padded[...] = jnp.where((times >= 0) & (times < devices * rows), glu, 0.0)

    depth = jnp.zeros((rows, width), F32)
    count = taps_ref.shape[0]
    for turn in range(8):
        shifted = None
        for tap in range(turn - 1, count, 8):
            if tap < 0:
                continue
            term = taps_ref[tap : tap + 1] * padded[tap + 1 - turn : tap + 9 - turn + rows]
            shifted = term if shifted is None else shifted + term
        depth = depth + shifted[turn : turn + rows]
    batch = depth * gains_ref[2:3] + gains_ref[3:4]
    act = (batch / (1.0 + jnp.exp(-batch))).astype(BF16)
    layer_ref[...] = (mid[HALO : HALO + rows] + matmul(act, w_project[...])).astype(BF16)
    stores[1].start()

    for copy in head_copies + halo_copies + ctx_copies:
        copy.wait_send()
    for d in range(1, side):
        part_copy(d).wait_send()
    for direct, relayed in lines:
        for copy in direct.values():
            copy.wait_send()
        for onward in relayed.values():
            for copy in onward.values():
                copy.wait_send()
    for i in range(2):
        edge_copy(i, kv).wait_send()
    for store in stores:
        store.wait()


def copy_kernel(attended_in, layer_in, attended_out, layer_out, attended, layer, sem):
    def copies(step, *pairs):
        return [
            pltpu.make_async_copy(source, target, sem.at[2 * step + i])
            for i, (source, target) in enumerate(pairs)
        ]

    inward = copies(0, (attended_in, attended), (layer_in, layer))
    outward = copies(1, (attended, attended_out), (layer, layer_out))
    for copy in inward:
        copy.start()
    for copy, onward in zip(inward, outward):
        copy.wait()
        onward.start()
    for copy in outward:
        copy.wait()


def on_device(
    frames,
    attn_gain,
    w_query,
    w_key,
    w_value,
    w_out,
    conv_gain,
    w_expand,
    kernel,
    bn_scale,
    bn_shift,
    w_project,
):
    rows, width = frames.shape
    groups = lax.axis_size("kv")
    side = math.isqrt(lax.axis_size("tm"))
    block = rows * groups
    near_rows = (5 if side == 8 else side // 2) * block
    far_rows = side * block - near_rows
    anywhere = pl.BlockSpec(memory_space=pl.ANY)
    dma = pltpu.SemaphoreType.DMA
    results = pl.pallas_call(
        functools.partial(layer_kernel, side),
        out_shape=(
            jax.ShapeDtypeStruct((rows, width), BF16),
            jax.ShapeDtypeStruct((rows, width), BF16),
        ),
        in_specs=[anywhere] * 12,
        out_specs=(anywhere, anywhere),
        scratch_shapes=[
            pltpu.VMEM((rows, width), BF16),
            pltpu.VMEM((rows, width), BF16),
            pltpu.VMEM((rows, width), BF16),
            pltpu.VMEM((4, width), F32),
            pltpu.VMEM(kernel.shape, F32),
            pltpu.VMEM((width, width), BF16),
            pltpu.VMEM((width, width), BF16),
            pltpu.VMEM((width, width), BF16),
            pltpu.VMEM((width, width), BF16),
            pltpu.VMEM((width, 2 * width), BF16),
            pltpu.VMEM((width, width), BF16),
            pltpu.VMEM((groups, 2 * rows, LANES), BF16),
            pltpu.VMEM((groups, 2 * rows, LANES), BF16),
            pltpu.VMEM((side, block, LANES), BF16),
            pltpu.VMEM((near_rows, 2 * LANES), BF16),
            pltpu.VMEM((far_rows, 2 * LANES), BF16),
            pltpu.VMEM((LANES, near_rows), BF16),
            pltpu.VMEM((LANES, far_rows), BF16),
            pltpu.VMEM((side, block // 2, LANES), BF16),
            pltpu.VMEM((block, near_rows), F32),
            pltpu.VMEM((block, far_rows), F32),
            pltpu.VMEM((block, near_rows), BF16),
            pltpu.VMEM((block, far_rows), BF16),
            pltpu.VMEM((block, LANES), F32),
            pltpu.VMEM((near_rows // block, block, 2 * LANES), F32),
            pltpu.VMEM((near_rows // block, block, LANES), F32),
            pltpu.VMEM((side, block, LANES), BF16),
            pltpu.VMEM((side, block, LANES), BF16),
            pltpu.VMEM((groups, WINDOW // 2, LANES), BF16),
            pltpu.VMEM((groups, WINDOW // 2, LANES), BF16),
            pltpu.VMEM((2, HALO, LANES), BF16),
            pltpu.VMEM((groups, HALO, LANES), BF16),
            pltpu.VMEM((rows + 2 * HALO, width), F32),
            pltpu.VMEM((2, HALO, width), BF16),
            pltpu.VMEM((2, HALO, width), BF16),
            pltpu.VMEM((rows + 2 * HALO, width), F32),
            dma((12,)),
            dma((2,)),
            dma((groups,)),
            dma((groups,)),
            dma((side,)),
            dma((side,)),
            dma((side,)),
            dma((side,)),
            dma((side,)),
            dma((side,)),
            dma((groups,)),
            dma((groups,)),
            dma((2,)),
            dma((groups,)),
            dma((2,)),
            dma((2,)),
        ],
        compiler_params=pltpu.CompilerParams(
            collective_id=0, has_side_effects=True, vmem_limit_bytes=60 * 1024 * 1024
        ),
    )(
        frames,
        attn_gain.reshape(1, width),
        conv_gain.reshape(1, width),
        bn_scale.reshape(1, width),
        bn_shift.reshape(1, width),
        kernel,
        w_query,
        w_key,
        w_value,
        w_out,
        w_expand,
        w_project,
    )
    return pl.pallas_call(
        copy_kernel,
        out_shape=tuple(jax.ShapeDtypeStruct(r.shape, r.dtype) for r in results),
        in_specs=[anywhere] * 2,
        out_specs=(anywhere, anywhere),
        scratch_shapes=[pltpu.VMEM((rows, width), BF16), pltpu.VMEM((rows, width), BF16), dma((4,))],
        compiler_params=pltpu.CompilerParams(vmem_limit_bytes=60 * 1024 * 1024),
    )(*results)


def solution(mesh):
    rows = P(("tm", "kv"), None)
    return jax.shard_map(
        on_device,
        mesh=mesh,
        in_specs=(rows,) + (P(),) * 11,
        out_specs=(rows, rows),
        check_vma=False,
    )
```

```python
import functools
import math

import jax
import jax.numpy as jnp
from jax import lax
from jax.experimental import pallas as pl
from jax.experimental.pallas import tpu as pltpu
from jax.sharding import PartitionSpec as P

HEAD_DIM = 64
HALF = HEAD_DIM // 2
LANES = 128
HALO = 16
WINDOW = 64
CHUNK = 32
MESH = pl.DeviceIdType.MESH
BF16 = jnp.bfloat16
F32 = jnp.float32


def layer_norm(values, gain):
    mean = jnp.mean(values, axis=-1, keepdims=True)
    centered = values - mean
    var = jnp.mean(centered * centered, axis=-1, keepdims=True)
    return centered / jnp.sqrt(var + 1e-05) * gain


def matmul(a, b):
    return jnp.dot(a, b, preferred_element_type=F32)


def folded(rows):
    half = rows.shape[0] // 2
    lane = lax.broadcasted_iota(jnp.int32, (half, LANES), 1)
    return jnp.where(lane < HEAD_DIM, pltpu.roll(rows[:half], HEAD_DIM, 1), rows[half:])


def all_heads(ref):
    columns = []
    lane = lax.broadcasted_iota(jnp.int32, ref.shape[1:], 1)
    for pair in range(ref.shape[0] // 2):
        even = ref[2 * pair].astype(F32)
        odd = ref[2 * pair + 1].astype(F32)
        top = jnp.where(lane < HEAD_DIM, even, pltpu.roll(odd, HEAD_DIM, 1))
        bottom = jnp.where(lane < HEAD_DIM, pltpu.roll(even, HEAD_DIM, 1), odd)
        columns.append(jnp.concatenate([top, bottom], axis=0))
    return jnp.concatenate(columns, axis=1)


def layer_kernel(
    side,
    frames_hbm,
    attn_gain_hbm,
    conv_gain_hbm,
    scale_hbm,
    shift_hbm,
    taps_hbm,
    w_query_hbm,
    w_key_hbm,
    w_value_hbm,
    w_out_hbm,
    w_expand_hbm,
    w_project_hbm,
    attended_hbm,
    layer_hbm,
    attended_ref,
    layer_ref,
    frames_ref,
    gains_ref,
    taps_ref,
    w_query,
    w_key,
    w_value,
    w_out,
    w_expand,
    w_project,
    head_send,
    head_recv,
    kv_all,
    near_wide,
    far_wide,
    near_keys,
    far_keys,
    q_all,
    near_scores,
    far_scores,
    near_weights,
    far_weights,
    tops,
    first_mixed,
    first_tops,
    part_send,
    part_recv,
    ctx_send,
    ctx_recv,
    edge_send,
    edge_recv,
    context,
    halo_send,
    halo_recv,
    padded,
    load_sem,
    store_sem,
    head_ssem,
    head_rsem,
    kv_ssem,
    kv_rsem,
    q_ssem,
    q_rsem,
    part_ssem,
    part_rsem,
    ctx_ssem,
    ctx_rsem,
    edge_ssem,
    edge_rsem,
    halo_ssem,
    halo_rsem,
):
    rows, width = frames_ref.shape
    groups = head_send.shape[0]
    block = rows * groups
    half_block = block // 2
    level_rows = -(-block // LANES)
    blocks = side * side
    tm = lax.axis_index("tm")
    kv = lax.axis_index("kv")
    bits = side.bit_length() - 1
    core = kv & 1
    slow = tm >> bits
    fast = tm & (side - 1)
    key_at = fast + core * (slow - fast)
    key_stride = 1 + core * (side - 1)
    query_at = slow + core * (fast - slow)
    query_stride = side - core * (side - 1)

    def kv_peer(d):
        return (tm, (kv + d) & (groups - 1))

    def key_peer(d):
        return (tm + (((key_at + d) & (side - 1)) - key_at) * key_stride, kv)

    def query_peer(d):
        return (tm + (((query_at + d) & (side - 1)) - query_at) * query_stride, kv)

    devices = groups * blocks
    me = tm * groups + kv
    following = (me + 1) & (devices - 1)
    preceding = (me - 1) & (devices - 1)
    group_bits = groups.bit_length() - 1
    following = (following >> group_bits, following & (groups - 1))
    preceding = (preceding >> group_bits, preceding & (groups - 1))
    later = (tm + 1) & (blocks - 1)
    earlier = (tm - 1) & (blocks - 1)
    near = sorted(range(1, side), key=lambda d: min(d, side - d))

    def greet(device):
        pl.semaphore_signal(barrier, inc=1, device_id=device, device_id_type=MESH)

    loads = [
        pltpu.make_async_copy(source, target, load_sem.at[i])
        for i, (source, target) in enumerate(
            (
                (frames_hbm, frames_ref),
                (attn_gain_hbm, gains_ref.at[0:1]),
                (w_key_hbm, w_key),
                (w_value_hbm, w_value),
                (w_query_hbm, w_query),
                (w_out_hbm, w_out),
                (w_expand_hbm, w_expand),
                (taps_hbm, taps_ref),
                (conv_gain_hbm, gains_ref.at[1:2]),
                (scale_hbm, gains_ref.at[2:3]),
                (shift_hbm, gains_ref.at[3:4]),
                (w_project_hbm, w_project),
            )
        )
    ]
    for load in loads[:5]:
        load.start()

    barrier = pltpu.get_barrier_semaphore()
    for d in range(1, groups):
        greet(kv_peer(d))
    for d in range(1, side):
        greet(key_peer(d))
        greet(query_peer(d))

    @pl.when(kv == groups - 1)
    def _():
        for head in range(groups):
            greet((later, head))

    @pl.when(kv == 0)
    def _():
        for head in range(groups):
            greet((earlier, head))

    lane = lax.broadcasted_iota(jnp.int32, (rows, LANES), 1)
    low = lane < HEAD_DIM
    first_half = lane % HEAD_DIM < HALF
    which = lax.broadcasted_iota(jnp.int32, (1, LANES), 1) % HALF
    inverse = jnp.zeros((1, LANES), F32)
    for i in range(HALF):
        inverse = jnp.where(which == i, 10000.0 ** (-2.0 * i / HEAD_DIM), inverse)
    positions = me * rows + lax.broadcasted_iota(jnp.int32, (rows, LANES), 0)
    angle = positions.astype(F32) * inverse
    cosine = jnp.cos(angle)
    sine = jnp.sin(angle)
    sine = jnp.where(first_half, -sine, sine)

    def rotated(part):
        swapped = jnp.where(
            first_half, pltpu.roll(part, LANES - HALF, 1), pltpu.roll(part, HALF, 1)
        )
        return part * cosine + swapped * sine

    loads[0].wait()
    loads[1].wait()
    inputs = frames_ref[...].astype(F32)
    halo_send[0] = inputs[:HALO].astype(BF16)
    halo_send[1] = inputs[rows - HALO :].astype(BF16)
    normed = layer_norm(inputs, gains_ref[0:1]).astype(BF16)
    loads[2].wait()
    keys = matmul(normed, w_key[...])
    loads[3].wait()
    values = matmul(normed, w_value[...])
    loads[4].wait()
    queries = matmul(normed, w_query[...])
    to_log2 = 0.125 / math.log(2.0)
    for pair in range(groups // 2):
        at = slice(pair * LANES, (pair + 1) * LANES)
        key = rotated(keys[:, at])
        query = rotated(queries[:, at]) * to_log2
        value = values[:, at]
        key_value = jnp.where(low, key, pltpu.roll(value, HEAD_DIM, 1))
        head_send[2 * pair] = jnp.concatenate(
            [key_value, jnp.where(low, query, 0.0)], axis=0
        ).astype(BF16)
        key_value = jnp.where(low, pltpu.roll(key, HEAD_DIM, 1), value)
        head_send[2 * pair + 1] = jnp.concatenate(
            [key_value, jnp.where(low, pltpu.roll(query, HEAD_DIM, 1), 0.0)], axis=0
        ).astype(BF16)

    pl.semaphore_wait(barrier, groups - 1 + 2 * (side - 1) + 2)

    head_copies = [
        pltpu.make_async_remote_copy(
            src_ref=head_send.at[(kv + d) & (groups - 1)],
            dst_ref=head_recv.at[kv],
            send_sem=head_ssem.at[d],
            recv_sem=head_rsem.at[d],
            device_id=kv_peer(d),
            device_id_type=MESH,
        )
        for d in range(1, groups)
    ]
    for copy in head_copies:
        copy.start()
    halo_copies = [
        pltpu.make_async_remote_copy(
            src_ref=halo_send.at[i],
            dst_ref=halo_recv.at[i],
            send_sem=halo_ssem.at[i],
            recv_sem=halo_rsem.at[i],
            device_id=target,
            device_id_type=MESH,
        )
        for i, target in enumerate((preceding, following))
    ]
    for copy in halo_copies:
        copy.start()
    for load in loads[5:]:
        load.start()
    head_recv[kv] = head_send[kv]
    for wide in (near_wide, far_wide):
        wide[:, LANES:] = jnp.ones((wide.shape[0], LANES), BF16)
    for copy in head_copies:
        copy.wait_recv()
    pieces = [head_recv[head].astype(F32) for head in range(groups)]
    own_block = jnp.concatenate([piece[:rows] for piece in pieces], axis=0).astype(BF16)
    kv_all[0] = own_block

    def line_copies(ref, ssem, rsem, peer):
        half = ref.shape[1] // 2
        lower, upper = pl.ds(0, half), pl.ds(half, half)

        def copy(source, target, place, sem):
            return pltpu.make_async_remote_copy(
                src_ref=source,
                dst_ref=target,
                send_sem=ssem.at[sem],
                recv_sem=rsem.at[sem],
                device_id=peer(place),
                device_id_type=MESH,
            )

        if side < 8:
            return {d: copy(ref.at[0], ref.at[d], d, d) for d in near}, {}
        direct = {d: copy(ref.at[0], ref.at[d], d, d) for d in near[:4]}
        relayed = {
            2: {
                3: copy(ref.at[2], ref.at[3], 1, 3),
                4: copy(ref.at[2, lower], ref.at[4, lower], 2, 4),
            },
            6: {
                5: copy(ref.at[6], ref.at[5], 7, 5),
                0: copy(ref.at[6, upper], ref.at[4, upper], 6, 0),
            },
        }
        return direct, relayed

    kv_direct, kv_relayed = line_copies(kv_all, kv_ssem, kv_rsem, key_peer)
    q_direct, q_relayed = line_copies(q_all, q_ssem, q_rsem, query_peer)
    lines = ((kv_direct, kv_relayed), (q_direct, q_relayed))
    for copy in kv_direct.values():
        copy.start()
    own_queries = jnp.concatenate([piece[rows:] for piece in pieces], axis=0)
    q_all[0] = (
        own_queries[:half_block] + pltpu.roll(own_queries[half_block:], HEAD_DIM, 1)
    ).astype(BF16)
    for copy in q_direct.values():
        copy.start()
    for direct, relayed in lines:
        for d, onward in relayed.items():
            direct[d].wait_recv()
            for copy in onward.values():
                copy.start()
    slots = [0] + near
    near_slots = slots[: near_wide.shape[0] // block]
    far_slots = slots[len(near_slots) :]

    def wait_for(wanted):
        for direct, relayed in lines:
            for d, copy in direct.items():
                if d in wanted and d not in relayed:
                    copy.wait_recv()
            for onward in relayed.values():
                for d, copy in onward.items():
                    if (d or 4) in wanted:
                        copy.wait_recv()

    def lay_out(wanted, wide, keys):
        for i in range(0, len(wanted), 2):
            few = wanted[i : i + 2]
            both = jnp.concatenate([kv_all[d] for d in few], axis=0)
            at = slice(i * block, (i + len(few)) * block)
            wide[at, :LANES] = both
            keys[:, at] = both.astype(F32).T.astype(BF16)

    half_lane = lax.broadcasted_iota(jnp.int32, (half_block, LANES), 1)

    def unfolded(d):
        packed = q_all[d].astype(F32)
        return jnp.concatenate(
            [
                jnp.where(half_lane < HEAD_DIM, packed, 0.0),
                jnp.where(half_lane < HEAD_DIM, pltpu.roll(packed, HEAD_DIM, 1), 0.0),
            ],
            axis=0,
        ).astype(BF16)

    def soften(pieces, floor=None):
        for begin in range(0, block, CHUNK):
            at = slice(begin, begin + CHUNK)
            score = [scores[at] for scores, _ in pieces]
            top = functools.reduce(
                jnp.maximum, [jnp.max(part, axis=1, keepdims=True) for part in score]
            )
            if floor is not None:
                top = jnp.maximum(top, floor[at, :1])
            for part, (_, weights) in zip(score, pieces):
                weights[at] = jnp.exp2(part - top).astype(BF16)
            tops[at] = jnp.broadcast_to(top, (CHUNK, LANES))

    def finish(d, mixed):
        total = mixed[:, LANES:]
        level = tops[...] + jnp.log2(total)
        place = lax.broadcasted_iota(jnp.int32, (HALO, LANES), 0)
        levels = jnp.zeros((HALO, LANES), F32)
        for i in range(level_rows):
            few = level[i * LANES : (i + 1) * LANES]
            row = lax.broadcasted_iota(jnp.int32, few.shape, 0)
            column = lax.broadcasted_iota(jnp.int32, few.shape, 1)
            line = jnp.sum(jnp.where(row == column, few, 0.0), axis=0, keepdims=True)
            high = line.astype(BF16).astype(F32)
            levels = jnp.where(place == i, high, levels)
            levels = jnp.where(place == level_rows + i, line - high, levels)
        part_send[d] = jnp.concatenate(
            [folded(mixed[:, :LANES] / total), levels], axis=0
        ).astype(BF16)

    def chosen(step, order):
        return sum((step == i).astype(jnp.int32) * d for i, d in enumerate(order))

    wait_for(near_slots)
    lay_out(near_slots, near_wide, near_keys)

    @pl.loop(0, len(near_slots))
    def _(step):
        near_scores[...] = matmul(unfolded(chosen(step, near_slots)), near_keys[...])
        soften([(near_scores, near_weights)])
        first_mixed[step] = matmul(near_weights[...], near_wide[...])
        first_tops[step] = tops[...]

    wait_for(far_slots)
    lay_out(far_slots, far_wide, far_keys)

    def part_copy(d):
        return pltpu.make_async_remote_copy(
            src_ref=part_send.at[d],
            dst_ref=part_recv.at[d],
            send_sem=part_ssem.at[d],
            recv_sem=part_rsem.at[d],
            device_id=query_peer(side - d),
            device_id_type=MESH,
        )

    @pl.loop(0, len(far_slots))
    def _(step):
        d = chosen(step, far_slots[::-1])
        query = unfolded(d)
        near_scores[...] = matmul(query, near_keys[...])
        far_scores[...] = matmul(query, far_keys[...])
        soften([(near_scores, near_weights), (far_scores, far_weights)])
        mixed = matmul(near_weights[...], near_wide[...])
        finish(d, mixed + matmul(far_weights[...], far_wide[...]))
        part_copy(d).start()

    @pl.loop(0, len(near_slots))
    def _(step):
        at = len(near_slots) - 1 - step
        d = chosen(at, near_slots)
        far_scores[...] = matmul(unfolded(d), far_keys[...])
        soften([(far_scores, far_weights)], first_tops.at[at])
        fade = jnp.exp2(first_tops[at] - tops[...])
        mixed = first_mixed[at] * jnp.concatenate([fade, fade], axis=1)
        finish(d, mixed + matmul(far_weights[...], far_wide[...]))

        @pl.when(at > 0)
        def _():
            part_copy(d).start()

    part_recv[0] = part_send[0]
    for d in range(1, side):
        part_copy(d).wait_recv()

    levels = []
    for i in range(level_rows):
        levels.append(
            [
                part_recv[d, half_block + i : half_block + i + 1].astype(F32)
                + part_recv[d, half_block + level_rows + i : half_block + level_rows + i + 1].astype(F32)
                for d in range(side)
            ]
        )
    shares = []
    for level in levels:
        level = jnp.concatenate(level, axis=0)
        fade = jnp.exp2(level - jnp.max(level, axis=0, keepdims=True))
        shares.append(fade / jnp.sum(fade, axis=0, keepdims=True))
    shares = jnp.concatenate(
        shares + [jnp.zeros((LANES - side * level_rows, LANES), F32)], axis=0
    ).T
    upper = []
    begin = half_block
    while begin < block:
        i = begin // LANES
        end = min(block, (i + 1) * LANES)
        few = shares[begin - i * LANES : end - i * LANES]
        upper.append(pltpu.roll(few, LANES - i * side, 1) if i else few)
        begin = end
    lower = shares[:half_block]
    upper = jnp.concatenate(upper, axis=0)
    pick = jnp.zeros((half_block, LANES), F32)
    for i, share in enumerate((lower, upper)):
        high = share.astype(BF16).astype(F32)
        for j, piece in enumerate((high, share - high)):
            begin = (2 * i + j) * side
            piece = pltpu.roll(piece, begin, 1) if begin else piece
            pick = jnp.where((half_lane >= begin) & (half_lane < begin + side), piece, pick)
    index = lax.broadcasted_iota(jnp.int32, (LANES, side * LANES), 0)
    lane = lax.broadcasted_iota(jnp.int32, (LANES, side * LANES), 1)
    spread = (
        (index % side == lane // LANES)
        & (index < 4 * side)
        & (index // (2 * side) == lane % LANES // HEAD_DIM)
    )
    spread = matmul(pick.astype(BF16), jnp.where(spread, 1.0, 0.0).astype(BF16))
    merged = jnp.zeros((half_block, LANES), F32)
    for d in range(side):
        part = part_recv[d].astype(F32)[:half_block]
        merged = merged + spread[:, d * LANES : (d + 1) * LANES] * part
    merged = jnp.concatenate([pltpu.roll(merged, HEAD_DIM, 1), merged], axis=0)

    edge_send[0] = folded(merged[: 2 * HALO]).astype(BF16)
    edge_send[1] = folded(merged[block - 2 * HALO :]).astype(BF16)
    framed = jnp.concatenate(
        [jnp.zeros((HALO, LANES), F32), merged, jnp.zeros((WINDOW - rows - HALO, LANES), F32)],
        axis=0,
    )
    for part in range(groups):
        ctx_send[part] = folded(framed[part * rows : part * rows + WINDOW]).astype(BF16)

    def edge_copy(i, head):
        return pltpu.make_async_remote_copy(
            src_ref=edge_send.at[i],
            dst_ref=edge_recv.at[head],
            send_sem=edge_ssem.at[i],
            recv_sem=edge_rsem.at[head],
            device_id=((earlier, groups - 1), (later, 0))[i],
            device_id_type=MESH,
        )

    for i in range(2):
        edge_copy(i, kv).start()
    ctx_copies = [
        pltpu.make_async_remote_copy(
            src_ref=ctx_send.at[(kv + d) & (groups - 1)],
            dst_ref=ctx_recv.at[kv],
            send_sem=ctx_ssem.at[d],
            recv_sem=ctx_rsem.at[d],
            device_id=kv_peer(d),
            device_id_type=MESH,
        )
        for d in range(1, groups)
    ]
    for copy in ctx_copies:
        copy.start()
    ctx_recv[kv] = ctx_send[kv]
    for load in loads[5:]:
        load.wait()
    for copy in halo_copies:
        copy.wait_recv()
    extent = rows + 2 * HALO
    nearby = jnp.concatenate([halo_recv[1].astype(F32), inputs, halo_recv[0].astype(F32)], axis=0)
    for copy in ctx_copies:
        copy.wait_recv()
    context[...] = all_heads(ctx_recv)[:extent]

    @pl.when(kv == 0)
    def _():
        for head in range(groups):
            edge_copy(1, head).wait_recv()
        context[:HALO] = all_heads(edge_recv)[HALO:]

    @pl.when(kv == groups - 1)
    def _():
        for head in range(groups):
            edge_copy(0, head).wait_recv()
        context[extent - HALO :] = all_heads(edge_recv)[:HALO]

    attended = matmul(context[...].astype(BF16), w_out[...]).astype(BF16).astype(F32)
    attended_ref[...] = attended[HALO : HALO + rows].astype(BF16)
    stores = [
        pltpu.make_async_copy(attended_ref, attended_hbm, store_sem.at[0]),
        pltpu.make_async_copy(layer_ref, layer_hbm, store_sem.at[1]),
    ]
    stores[0].start()
    mid = nearby + attended
    conv_in = layer_norm(mid, gains_ref[1:2]).astype(BF16)
    expanded = matmul(conv_in, w_expand[...])
    gate = expanded[:, width:]
    glu = (expanded[:, :width] / (1.0 + jnp.exp(-gate))).astype(BF16).astype(F32)
    times = me * rows - HALO + lax.broadcasted_iota(jnp.int32, (extent, width), 0)
    padded[...] = jnp.where((times >= 0) & (times < devices * rows), glu, 0.0)

    depth = jnp.zeros((rows, width), F32)
    count = taps_ref.shape[0]
    for turn in range(8):
        shifted = None
        for tap in range(turn - 1, count, 8):
            if tap < 0:
                continue
            term = taps_ref[tap : tap + 1] * padded[tap + 1 - turn : tap + 9 - turn + rows]
            shifted = term if shifted is None else shifted + term
        depth = depth + shifted[turn : turn + rows]
    batch = depth * gains_ref[2:3] + gains_ref[3:4]
    act = (batch / (1.0 + jnp.exp(-batch))).astype(BF16)
    layer_ref[...] = (mid[HALO : HALO + rows] + matmul(act, w_project[...])).astype(BF16)
    stores[1].start()

    for copy in head_copies + halo_copies + ctx_copies:
        copy.wait_send()
    for d in range(1, side):
        part_copy(d).wait_send()
    for direct, relayed in lines:
        for copy in direct.values():
            copy.wait_send()
        for onward in relayed.values():
            for copy in onward.values():
                copy.wait_send()
    for i in range(2):
        edge_copy(i, kv).wait_send()
    for store in stores:
        store.wait()


def copy_kernel(attended_in, layer_in, attended_out, layer_out, attended, layer, sem):
    def copies(step, *pairs):
        return [
            pltpu.make_async_copy(source, target, sem.at[2 * step + i])
            for i, (source, target) in enumerate(pairs)
        ]

    inward = copies(0, (attended_in, attended), (layer_in, layer))
    outward = copies(1, (attended, attended_out), (layer, layer_out))
    for copy in inward:
        copy.start()
    for copy, onward in zip(inward, outward):
        copy.wait()
        onward.start()
    for copy in outward:
        copy.wait()


def on_device(
    frames,
    attn_gain,
    w_query,
    w_key,
    w_value,
    w_out,
    conv_gain,
    w_expand,
    kernel,
    bn_scale,
    bn_shift,
    w_project,
):
    rows, width = frames.shape
    groups = lax.axis_size("kv")
    side = math.isqrt(lax.axis_size("tm"))
    block = rows * groups
    near_rows = (5 if side == 8 else side // 2) * block
    far_rows = side * block - near_rows
    anywhere = pl.BlockSpec(memory_space=pl.ANY)
    dma = pltpu.SemaphoreType.DMA
    results = pl.pallas_call(
        functools.partial(layer_kernel, side),
        out_shape=(
            jax.ShapeDtypeStruct((rows, width), BF16),
            jax.ShapeDtypeStruct((rows, width), BF16),
        ),
        in_specs=[anywhere] * 12,
        out_specs=(anywhere, anywhere),
        scratch_shapes=[
            pltpu.VMEM((rows, width), BF16),
            pltpu.VMEM((rows, width), BF16),
            pltpu.VMEM((rows, width), BF16),
            pltpu.VMEM((4, width), F32),
            pltpu.VMEM(kernel.shape, F32),
            pltpu.VMEM((width, width), BF16),
            pltpu.VMEM((width, width), BF16),
            pltpu.VMEM((width, width), BF16),
            pltpu.VMEM((width, width), BF16),
            pltpu.VMEM((width, 2 * width), BF16),
            pltpu.VMEM((width, width), BF16),
            pltpu.VMEM((groups, 2 * rows, LANES), BF16),
            pltpu.VMEM((groups, 2 * rows, LANES), BF16),
            pltpu.VMEM((side, block, LANES), BF16),
            pltpu.VMEM((near_rows, 2 * LANES), BF16),
            pltpu.VMEM((far_rows, 2 * LANES), BF16),
            pltpu.VMEM((LANES, near_rows), BF16),
            pltpu.VMEM((LANES, far_rows), BF16),
            pltpu.VMEM((side, block // 2, LANES), BF16),
            pltpu.VMEM((block, near_rows), F32),
            pltpu.VMEM((block, far_rows), F32),
            pltpu.VMEM((block, near_rows), BF16),
            pltpu.VMEM((block, far_rows), BF16),
            pltpu.VMEM((block, LANES), F32),
            pltpu.VMEM((near_rows // block, block, 2 * LANES), F32),
            pltpu.VMEM((near_rows // block, block, LANES), F32),
            pltpu.VMEM((side, block // 2 + HALO, LANES), BF16),
            pltpu.VMEM((side, block // 2 + HALO, LANES), BF16),
            pltpu.VMEM((groups, WINDOW // 2, LANES), BF16),
            pltpu.VMEM((groups, WINDOW // 2, LANES), BF16),
            pltpu.VMEM((2, HALO, LANES), BF16),
            pltpu.VMEM((groups, HALO, LANES), BF16),
            pltpu.VMEM((rows + 2 * HALO, width), F32),
            pltpu.VMEM((2, HALO, width), BF16),
            pltpu.VMEM((2, HALO, width), BF16),
            pltpu.VMEM((rows + 2 * HALO, width), F32),
            dma((12,)),
            dma((2,)),
            dma((groups,)),
            dma((groups,)),
            dma((side,)),
            dma((side,)),
            dma((side,)),
            dma((side,)),
            dma((side,)),
            dma((side,)),
            dma((groups,)),
            dma((groups,)),
            dma((2,)),
            dma((groups,)),
            dma((2,)),
            dma((2,)),
        ],
        compiler_params=pltpu.CompilerParams(
            collective_id=0, has_side_effects=True, vmem_limit_bytes=60 * 1024 * 1024
        ),
    )(
        frames,
        attn_gain.reshape(1, width),
        conv_gain.reshape(1, width),
        bn_scale.reshape(1, width),
        bn_shift.reshape(1, width),
        kernel,
        w_query,
        w_key,
        w_value,
        w_out,
        w_expand,
        w_project,
    )
    return pl.pallas_call(
        copy_kernel,
        out_shape=tuple(jax.ShapeDtypeStruct(r.shape, r.dtype) for r in results),
        in_specs=[anywhere] * 2,
        out_specs=(anywhere, anywhere),
        scratch_shapes=[pltpu.VMEM((rows, width), BF16), pltpu.VMEM((rows, width), BF16), dma((4,))],
        compiler_params=pltpu.CompilerParams(vmem_limit_bytes=60 * 1024 * 1024),
    )(*results)


def solution(mesh):
    rows = P(("tm", "kv"), None)
    return jax.shard_map(
        on_device,
        mesh=mesh,
        in_specs=(rows,) + (P(),) * 11,
        out_specs=(rows, rows),
        check_vma=False,
    )
```

```python
import functools
import math

import jax
import jax.numpy as jnp
from jax import lax
from jax.experimental import pallas as pl
from jax.experimental.pallas import tpu as pltpu
from jax.sharding import PartitionSpec as P

HEAD_DIM = 64
HALF = HEAD_DIM // 2
LANES = 128
HALO = 16
WINDOW = 64
CHUNK = 32
MESH = pl.DeviceIdType.MESH
BF16 = jnp.bfloat16
F32 = jnp.float32


def layer_norm(values, gain):
    mean = jnp.mean(values, axis=-1, keepdims=True)
    centered = values - mean
    var = jnp.mean(centered * centered, axis=-1, keepdims=True)
    return centered / jnp.sqrt(var + 1e-05) * gain


def matmul(a, b):
    return jnp.dot(a, b, preferred_element_type=F32)


def folded(rows):
    half = rows.shape[0] // 2
    lane = lax.broadcasted_iota(jnp.int32, (half, LANES), 1)
    return jnp.where(lane < HEAD_DIM, pltpu.roll(rows[:half], HEAD_DIM, 1), rows[half:])


def all_heads(ref):
    columns = []
    lane = lax.broadcasted_iota(jnp.int32, ref.shape[1:], 1)
    for pair in range(ref.shape[0] // 2):
        even = ref[2 * pair].astype(F32)
        odd = ref[2 * pair + 1].astype(F32)
        top = jnp.where(lane < HEAD_DIM, even, pltpu.roll(odd, HEAD_DIM, 1))
        bottom = jnp.where(lane < HEAD_DIM, pltpu.roll(even, HEAD_DIM, 1), odd)
        columns.append(jnp.concatenate([top, bottom], axis=0))
    return jnp.concatenate(columns, axis=1)


def layer_kernel(
    side,
    frames_hbm,
    attn_gain_hbm,
    conv_gain_hbm,
    scale_hbm,
    shift_hbm,
    taps_hbm,
    w_query_hbm,
    w_key_hbm,
    w_value_hbm,
    w_out_hbm,
    w_expand_hbm,
    w_project_hbm,
    attended_ref,
    layer_ref,
    frames_ref,
    gains_ref,
    taps_ref,
    w_query,
    w_key,
    w_value,
    w_out,
    w_expand,
    w_project,
    head_send,
    head_recv,
    kv_all,
    near_wide,
    far_wide,
    near_keys,
    far_keys,
    q_all,
    near_scores,
    far_scores,
    near_weights,
    far_weights,
    tops,
    first_mixed,
    first_tops,
    part_send,
    part_recv,
    ctx_send,
    ctx_recv,
    edge_send,
    edge_recv,
    context,
    halo_send,
    halo_recv,
    padded,
    load_sem,
    head_ssem,
    head_rsem,
    kv_ssem,
    kv_rsem,
    q_ssem,
    q_rsem,
    part_ssem,
    part_rsem,
    ctx_ssem,
    ctx_rsem,
    edge_ssem,
    edge_rsem,
    halo_ssem,
    halo_rsem,
):
    rows, width = frames_ref.shape
    groups = head_send.shape[0]
    block = rows * groups
    half_block = block // 2
    level_rows = -(-block // LANES)
    blocks = side * side
    tm = lax.axis_index("tm")
    kv = lax.axis_index("kv")
    bits = side.bit_length() - 1
    core = kv & 1
    slow = tm >> bits
    fast = tm & (side - 1)
    key_at = fast + core * (slow - fast)
    key_stride = 1 + core * (side - 1)
    query_at = slow + core * (fast - slow)
    query_stride = side - core * (side - 1)

    def kv_peer(d):
        return (tm, (kv + d) & (groups - 1))

    def key_peer(d):
        return (tm + (((key_at + d) & (side - 1)) - key_at) * key_stride, kv)

    def query_peer(d):
        return (tm + (((query_at + d) & (side - 1)) - query_at) * query_stride, kv)

    devices = groups * blocks
    me = tm * groups + kv
    following = (me + 1) & (devices - 1)
    preceding = (me - 1) & (devices - 1)
    group_bits = groups.bit_length() - 1
    following = (following >> group_bits, following & (groups - 1))
    preceding = (preceding >> group_bits, preceding & (groups - 1))
    later = (tm + 1) & (blocks - 1)
    earlier = (tm - 1) & (blocks - 1)
    near = sorted(range(1, side), key=lambda d: min(d, side - d))

    def greet(device):
        pl.semaphore_signal(barrier, inc=1, device_id=device, device_id_type=MESH)

    loads = [
        pltpu.make_async_copy(source, target, load_sem.at[i])
        for i, (source, target) in enumerate(
            (
                (frames_hbm, frames_ref),
                (attn_gain_hbm, gains_ref.at[0:1]),
                (w_key_hbm, w_key),
                (w_value_hbm, w_value),
                (w_query_hbm, w_query),
                (w_out_hbm, w_out),
                (w_expand_hbm, w_expand),
                (taps_hbm, taps_ref),
                (conv_gain_hbm, gains_ref.at[1:2]),
                (scale_hbm, gains_ref.at[2:3]),
                (shift_hbm, gains_ref.at[3:4]),
                (w_project_hbm, w_project),
            )
        )
    ]
    for load in loads[:5]:
        load.start()

    barrier = pltpu.get_barrier_semaphore()
    for d in range(1, groups):
        greet(kv_peer(d))
    for d in near[:4]:
        greet(key_peer(d))
        greet(query_peer(d))

    lane = lax.broadcasted_iota(jnp.int32, (rows, LANES), 1)
    low = lane < HEAD_DIM
    first_half = lane % HEAD_DIM < HALF
    which = lax.broadcasted_iota(jnp.int32, (1, LANES), 1) % HALF
    inverse = jnp.zeros((1, LANES), F32)
    for i in range(HALF):
        inverse = jnp.where(which == i, 10000.0 ** (-2.0 * i / HEAD_DIM), inverse)
    positions = me * rows + lax.broadcasted_iota(jnp.int32, (rows, LANES), 0)
    angle = positions.astype(F32) * inverse
    cosine = jnp.cos(angle)
    sine = jnp.sin(angle)
    sine = jnp.where(first_half, -sine, sine)

    def rotated(part):
        swapped = jnp.where(
            first_half, pltpu.roll(part, LANES - HALF, 1), pltpu.roll(part, HALF, 1)
        )
        return part * cosine + swapped * sine

    loads[0].wait()
    loads[1].wait()
    inputs = frames_ref[...].astype(F32)
    halo_send[0] = inputs[:HALO].astype(BF16)
    halo_send[1] = inputs[rows - HALO :].astype(BF16)
    normed = layer_norm(inputs, gains_ref[0:1]).astype(BF16)
    loads[2].wait()
    keys = matmul(normed, w_key[...])
    loads[3].wait()
    values = matmul(normed, w_value[...])
    loads[4].wait()
    queries = matmul(normed, w_query[...])
    to_log2 = 0.125 / math.log(2.0)
    for pair in range(groups // 2):
        at = slice(pair * LANES, (pair + 1) * LANES)
        key = rotated(keys[:, at])
        query = rotated(queries[:, at]) * to_log2
        value = values[:, at]
        key_value = jnp.where(low, key, pltpu.roll(value, HEAD_DIM, 1))
        head_send[2 * pair] = jnp.concatenate(
            [key_value, jnp.where(low, query, 0.0)], axis=0
        ).astype(BF16)
        key_value = jnp.where(low, pltpu.roll(key, HEAD_DIM, 1), value)
        head_send[2 * pair + 1] = jnp.concatenate(
            [key_value, jnp.where(low, pltpu.roll(query, HEAD_DIM, 1), 0.0)], axis=0
        ).astype(BF16)

    pl.semaphore_wait(barrier, groups - 1 + 2 * len(near[:4]))

    head_copies = [
        pltpu.make_async_remote_copy(
            src_ref=head_send.at[(kv + d) & (groups - 1)],
            dst_ref=head_recv.at[kv],
            send_sem=head_ssem.at[d],
            recv_sem=head_rsem.at[d],
            device_id=kv_peer(d),
            device_id_type=MESH,
        )
        for d in range(1, groups)
    ]
    for copy in head_copies:
        copy.start()
    for load in loads[5:]:
        load.start()
    head_recv[kv] = head_send[kv]
    for wide in (near_wide, far_wide):
        wide[:, LANES:] = jnp.ones((wide.shape[0], LANES), BF16)
    for copy in head_copies:
        copy.wait_recv()
    pieces = [head_recv[head].astype(F32) for head in range(groups)]
    own_block = jnp.concatenate([piece[:rows] for piece in pieces], axis=0).astype(BF16)
    kv_all[0] = own_block

    def line_copies(ref, ssem, rsem, peer):
        half = ref.shape[1] // 2
        lower, upper = pl.ds(0, half), pl.ds(half, half)

        def copy(source, target, place, sem):
            return pltpu.make_async_remote_copy(
                src_ref=source,
                dst_ref=target,
                send_sem=ssem.at[sem],
                recv_sem=rsem.at[sem],
                device_id=peer(place),
                device_id_type=MESH,
            )

        if side < 8:
            return {d: copy(ref.at[0], ref.at[d], d, d) for d in near}, {}
        direct = {d: copy(ref.at[0], ref.at[d], d, d) for d in near[:4]}
        relayed = {
            2: {
                3: copy(ref.at[2], ref.at[3], 1, 3),
                4: copy(ref.at[2, lower], ref.at[4, lower], 2, 4),
            },
            6: {
                5: copy(ref.at[6], ref.at[5], 7, 5),
                0: copy(ref.at[6, upper], ref.at[4, upper], 6, 0),
            },
        }
        return direct, relayed

    kv_direct, kv_relayed = line_copies(kv_all, kv_ssem, kv_rsem, key_peer)
    q_direct, q_relayed = line_copies(q_all, q_ssem, q_rsem, query_peer)
    lines = ((kv_direct, kv_relayed), (q_direct, q_relayed))
    for copy in kv_direct.values():
        copy.start()
    own_queries = jnp.concatenate([piece[rows:] for piece in pieces], axis=0)
    q_all[0] = (
        own_queries[:half_block] + pltpu.roll(own_queries[half_block:], HEAD_DIM, 1)
    ).astype(BF16)
    for copy in q_direct.values():
        copy.start()
    for direct, relayed in lines:
        for d, onward in relayed.items():
            direct[d].wait_recv()
            for copy in onward.values():
                copy.start()
    slots = [0] + near
    near_slots = slots[: near_wide.shape[0] // block]
    far_slots = slots[len(near_slots) :]

    def wait_for(wanted):
        for direct, relayed in lines:
            for d, copy in direct.items():
                if d in wanted and d not in relayed:
                    copy.wait_recv()
            for onward in relayed.values():
                for d, copy in onward.items():
                    if (d or 4) in wanted:
                        copy.wait_recv()

    def lay_out(wanted, wide, keys):
        for i in range(0, len(wanted), 2):
            few = wanted[i : i + 2]
            both = jnp.concatenate([kv_all[d] for d in few], axis=0)
            at = slice(i * block, (i + len(few)) * block)
            wide[at, :LANES] = both
            keys[:, at] = both.astype(F32).T.astype(BF16)

    half_lane = lax.broadcasted_iota(jnp.int32, (half_block, LANES), 1)

    def unfolded(d):
        packed = q_all[d].astype(F32)
        return jnp.concatenate(
            [
                jnp.where(half_lane < HEAD_DIM, packed, 0.0),
                jnp.where(half_lane < HEAD_DIM, pltpu.roll(packed, HEAD_DIM, 1), 0.0),
            ],
            axis=0,
        ).astype(BF16)

    def soften(pieces, floor=None):
        for begin in range(0, block, CHUNK):
            at = slice(begin, begin + CHUNK)
            score = [scores[at] for scores, _ in pieces]
            top = functools.reduce(
                jnp.maximum, [jnp.max(part, axis=1, keepdims=True) for part in score]
            )
            if floor is not None:
                top = jnp.maximum(top, floor[at, :1])
            for part, (_, weights) in zip(score, pieces):
                weights[at] = jnp.exp2(part - top).astype(BF16)
            tops[at] = jnp.broadcast_to(top, (CHUNK, LANES))

    def finish(d, mixed):
        total = mixed[:, LANES:]
        level = tops[...] + jnp.log2(total)
        place = lax.broadcasted_iota(jnp.int32, (HALO, LANES), 0)
        levels = jnp.zeros((HALO, LANES), F32)
        for i in range(level_rows):
            few = level[i * LANES : (i + 1) * LANES]
            row = lax.broadcasted_iota(jnp.int32, few.shape, 0)
            column = lax.broadcasted_iota(jnp.int32, few.shape, 1)
            line = jnp.sum(jnp.where(row == column, few, 0.0), axis=0, keepdims=True)
            high = line.astype(BF16).astype(F32)
            levels = jnp.where(place == i, high, levels)
            levels = jnp.where(place == level_rows + i, line - high, levels)
        part_send[d] = jnp.concatenate(
            [folded(mixed[:, :LANES] / total), levels], axis=0
        ).astype(BF16)

    def chosen(step, order):
        return sum((step == i).astype(jnp.int32) * d for i, d in enumerate(order))

    wait_for(near_slots)
    lay_out(near_slots, near_wide, near_keys)

    @pl.loop(0, len(near_slots))
    def _(step):
        near_scores[...] = matmul(unfolded(chosen(step, near_slots)), near_keys[...])
        soften([(near_scores, near_weights)])
        first_mixed[step] = matmul(near_weights[...], near_wide[...])
        first_tops[step] = tops[...]

    wait_for(far_slots)
    lay_out(far_slots, far_wide, far_keys)

    def part_copy(d):
        return pltpu.make_async_remote_copy(
            src_ref=part_send.at[d],
            dst_ref=part_recv.at[d],
            send_sem=part_ssem.at[d],
            recv_sem=part_rsem.at[d],
            device_id=query_peer(side - d),
            device_id_type=MESH,
        )

    @pl.loop(0, len(far_slots))
    def _(step):
        d = chosen(step, far_slots[::-1])
        query = unfolded(d)
        near_scores[...] = matmul(query, near_keys[...])
        far_scores[...] = matmul(query, far_keys[...])
        soften([(near_scores, near_weights), (far_scores, far_weights)])
        mixed = matmul(near_weights[...], near_wide[...])
        finish(d, mixed + matmul(far_weights[...], far_wide[...]))
        part_copy(d).start()

    @pl.loop(0, len(near_slots))
    def _(step):
        at = len(near_slots) - 1 - step
        d = chosen(at, near_slots)
        far_scores[...] = matmul(unfolded(d), far_keys[...])
        soften([(far_scores, far_weights)], first_tops.at[at])
        fade = jnp.exp2(first_tops[at] - tops[...])
        mixed = first_mixed[at] * jnp.concatenate([fade, fade], axis=1)
        finish(d, mixed + matmul(far_weights[...], far_wide[...]))

        @pl.when(at > 0)
        def _():
            part_copy(d).start()

    part_recv[0] = part_send[0]
    for d in range(1, side):
        part_copy(d).wait_recv()

    levels = []
    for i in range(level_rows):
        levels.append(
            [
                part_recv[d, half_block + i : half_block + i + 1].astype(F32)
                + part_recv[d, half_block + level_rows + i : half_block + level_rows + i + 1].astype(F32)
                for d in range(side)
            ]
        )
    shares = []
    for level in levels:
        level = jnp.concatenate(level, axis=0)
        fade = jnp.exp2(level - jnp.max(level, axis=0, keepdims=True))
        shares.append(fade / jnp.sum(fade, axis=0, keepdims=True))
    shares = jnp.concatenate(
        shares + [jnp.zeros((LANES - side * level_rows, LANES), F32)], axis=0
    ).T
    upper = []
    begin = half_block
    while begin < block:
        i = begin // LANES
        end = min(block, (i + 1) * LANES)
        few = shares[begin - i * LANES : end - i * LANES]
        upper.append(pltpu.roll(few, LANES - i * side, 1) if i else few)
        begin = end
    lower = shares[:half_block]
    upper = jnp.concatenate(upper, axis=0)
    pick = jnp.zeros((half_block, LANES), F32)
    for i, share in enumerate((lower, upper)):
        high = share.astype(BF16).astype(F32)
        for j, piece in enumerate((high, share - high)):
            begin = (2 * i + j) * side
            piece = pltpu.roll(piece, begin, 1) if begin else piece
            pick = jnp.where((half_lane >= begin) & (half_lane < begin + side), piece, pick)
    index = lax.broadcasted_iota(jnp.int32, (LANES, side * LANES), 0)
    lane = lax.broadcasted_iota(jnp.int32, (LANES, side * LANES), 1)
    spread = (
        (index % side == lane // LANES)
        & (index < 4 * side)
        & (index // (2 * side) == lane % LANES // HEAD_DIM)
    )
    spread = matmul(pick.astype(BF16), jnp.where(spread, 1.0, 0.0).astype(BF16))
    merged = jnp.zeros((half_block, LANES), F32)
    for d in range(side):
        part = part_recv[d].astype(F32)[:half_block]
        merged = merged + spread[:, d * LANES : (d + 1) * LANES] * part
    merged = jnp.concatenate([pltpu.roll(merged, HEAD_DIM, 1), merged], axis=0)

    edge_send[0] = folded(merged[: 2 * HALO]).astype(BF16)
    edge_send[1] = folded(merged[block - 2 * HALO :]).astype(BF16)
    framed = jnp.concatenate(
        [jnp.zeros((HALO, LANES), F32), merged, jnp.zeros((WINDOW - rows - HALO, LANES), F32)],
        axis=0,
    )
    for part in range(groups):
        ctx_send[part] = folded(framed[part * rows : part * rows + WINDOW]).astype(BF16)

    def edge_copy(i, head):
        return pltpu.make_async_remote_copy(
            src_ref=edge_send.at[i],
            dst_ref=edge_recv.at[head],
            send_sem=edge_ssem.at[i],
            recv_sem=edge_rsem.at[head],
            device_id=((earlier, groups - 1), (later, 0))[i],
            device_id_type=MESH,
        )

    for i in range(2):
        edge_copy(i, kv).start()
    ctx_copies = [
        pltpu.make_async_remote_copy(
            src_ref=ctx_send.at[(kv + d) & (groups - 1)],
            dst_ref=ctx_recv.at[kv],
            send_sem=ctx_ssem.at[d],
            recv_sem=ctx_rsem.at[d],
            device_id=kv_peer(d),
            device_id_type=MESH,
        )
        for d in range(1, groups)
    ]
    for copy in ctx_copies:
        copy.start()
    halo_copies = [
        pltpu.make_async_remote_copy(
            src_ref=halo_send.at[i],
            dst_ref=halo_recv.at[i],
            send_sem=halo_ssem.at[i],
            recv_sem=halo_rsem.at[i],
            device_id=target,
            device_id_type=MESH,
        )
        for i, target in enumerate((preceding, following))
    ]
    for copy in halo_copies:
        copy.start()
    ctx_recv[kv] = ctx_send[kv]
    for copy in head_copies:
        copy.wait_send()
    for direct, relayed in lines:
        for copy in direct.values():
            copy.wait_send()
        for onward in relayed.values():
            for copy in onward.values():
                copy.wait_send()
    for d in range(1, side):
        part_copy(d).wait_send()
    for load in loads[5:]:
        load.wait()
    for copy in halo_copies:
        copy.wait_recv()
    extent = rows + 2 * HALO
    nearby = jnp.concatenate([halo_recv[1].astype(F32), inputs, halo_recv[0].astype(F32)], axis=0)
    for copy in ctx_copies:
        copy.wait_recv()
    for copy in ctx_copies + halo_copies:
        copy.wait_send()
    for i in range(2):
        edge_copy(i, kv).wait_send()
    context[...] = all_heads(ctx_recv)[:extent]

    @pl.when(kv == 0)
    def _():
        for head in range(groups):
            edge_copy(1, head).wait_recv()
        context[:HALO] = all_heads(edge_recv)[HALO:]

    @pl.when(kv == groups - 1)
    def _():
        for head in range(groups):
            edge_copy(0, head).wait_recv()
        context[extent - HALO :] = all_heads(edge_recv)[:HALO]

    attended = matmul(context[...].astype(BF16), w_out[...]).astype(BF16).astype(F32)
    attended_ref[...] = attended[HALO : HALO + rows].astype(BF16)
    mid = nearby + attended
    conv_in = layer_norm(mid, gains_ref[1:2]).astype(BF16)
    expanded = matmul(conv_in, w_expand[...])
    gate = expanded[:, width:]
    glu = (expanded[:, :width] / (1.0 + jnp.exp(-gate))).astype(BF16).astype(F32)
    times = me * rows - HALO + lax.broadcasted_iota(jnp.int32, (extent, width), 0)
    padded[...] = jnp.where((times >= 0) & (times < devices * rows), glu, 0.0)

    depth = jnp.zeros((rows, width), F32)
    count = taps_ref.shape[0]
    for turn in range(8):
        shifted = None
        for tap in range(turn - 1, count, 8):
            if tap < 0:
                continue
            term = taps_ref[tap : tap + 1] * padded[tap + 1 - turn : tap + 9 - turn + rows]
            shifted = term if shifted is None else shifted + term
        depth = depth + shifted[turn : turn + rows]
    batch = depth * gains_ref[2:3] + gains_ref[3:4]
    act = (batch / (1.0 + jnp.exp(-batch))).astype(BF16)
    layer_ref[...] = (mid[HALO : HALO + rows] + matmul(act, w_project[...])).astype(BF16)


def copy_kernel(attended_in, layer_in, attended_out, layer_out, sem):
    copies = [
        pltpu.make_async_copy(attended_in, attended_out, sem.at[0]),
        pltpu.make_async_copy(layer_in, layer_out, sem.at[1]),
    ]
    for copy in copies:
        copy.start()
    for copy in copies:
        copy.wait()


def on_device(
    frames,
    attn_gain,
    w_query,
    w_key,
    w_value,
    w_out,
    conv_gain,
    w_expand,
    kernel,
    bn_scale,
    bn_shift,
    w_project,
):
    rows, width = frames.shape
    groups = lax.axis_size("kv")
    side = math.isqrt(lax.axis_size("tm"))
    block = rows * groups
    near_rows = (5 if side == 8 else side // 2) * block
    far_rows = side * block - near_rows
    vmem = pl.BlockSpec(memory_space=pltpu.VMEM)
    anywhere = pl.BlockSpec(memory_space=pl.ANY)
    dma = pltpu.SemaphoreType.DMA
    results = pl.pallas_call(
        functools.partial(layer_kernel, side),
        out_shape=(pltpu.VMEM((rows, width), BF16), pltpu.VMEM((rows, width), BF16)),
        in_specs=[anywhere] * 12,
        out_specs=(vmem, vmem),
        scratch_shapes=[
            pltpu.VMEM((rows, width), BF16),
            pltpu.VMEM((4, width), F32),
            pltpu.VMEM(kernel.shape, F32),
            pltpu.VMEM((width, width), BF16),
            pltpu.VMEM((width, width), BF16),
            pltpu.VMEM((width, width), BF16),
            pltpu.VMEM((width, width), BF16),
            pltpu.VMEM((width, 2 * width), BF16),
            pltpu.VMEM((width, width), BF16),
            pltpu.VMEM((groups, 2 * rows, LANES), BF16),
            pltpu.VMEM((groups, 2 * rows, LANES), BF16),
            pltpu.VMEM((side, block, LANES), BF16),
            pltpu.VMEM((near_rows, 2 * LANES), BF16),
            pltpu.VMEM((far_rows, 2 * LANES), BF16),
            pltpu.VMEM((LANES, near_rows), BF16),
            pltpu.VMEM((LANES, far_rows), BF16),
            pltpu.VMEM((side, block // 2, LANES), BF16),
            pltpu.VMEM((block, near_rows), F32),
            pltpu.VMEM((block, far_rows), F32),
            pltpu.VMEM((block, near_rows), BF16),
            pltpu.VMEM((block, far_rows), BF16),
            pltpu.VMEM((block, LANES), F32),
            pltpu.VMEM((near_rows // block, block, 2 * LANES), F32),
            pltpu.VMEM((near_rows // block, block, LANES), F32),
            pltpu.VMEM((side, block // 2 + HALO, LANES), BF16),
            pltpu.VMEM((side, block // 2 + HALO, LANES), BF16),
            pltpu.VMEM((groups, WINDOW // 2, LANES), BF16),
            pltpu.VMEM((groups, WINDOW // 2, LANES), BF16),
            pltpu.VMEM((2, HALO, LANES), BF16),
            pltpu.VMEM((groups, HALO, LANES), BF16),
            pltpu.VMEM((rows + 2 * HALO, width), F32),
            pltpu.VMEM((2, HALO, width), BF16),
            pltpu.VMEM((2, HALO, width), BF16),
            pltpu.VMEM((rows + 2 * HALO, width), F32),
            dma((12,)),
            dma((groups,)),
            dma((groups,)),
            dma((side,)),
            dma((side,)),
            dma((side,)),
            dma((side,)),
            dma((side,)),
            dma((side,)),
            dma((groups,)),
            dma((groups,)),
            dma((2,)),
            dma((groups,)),
            dma((2,)),
            dma((2,)),
        ],
        compiler_params=pltpu.CompilerParams(
            collective_id=0, has_side_effects=True, vmem_limit_bytes=60 * 1024 * 1024
        ),
    )(
        frames,
        attn_gain.reshape(1, width),
        conv_gain.reshape(1, width),
        bn_scale.reshape(1, width),
        bn_shift.reshape(1, width),
        kernel,
        w_query,
        w_key,
        w_value,
        w_out,
        w_expand,
        w_project,
    )
    return pl.pallas_call(
        copy_kernel,
        out_shape=(jax.ShapeDtypeStruct((rows, width), BF16),) * 2,
        in_specs=[vmem] * 2,
        out_specs=(anywhere, anywhere),
        scratch_shapes=[dma((2,))],
        compiler_params=pltpu.CompilerParams(vmem_limit_bytes=4 * 1024 * 1024),
    )(*results)


def solution(mesh):
    rows = P(("tm", "kv"), None)
    return jax.shard_map(
        on_device,
        mesh=mesh,
        in_specs=(rows,) + (P(),) * 11,
        out_specs=(rows, rows),
        check_vma=False,
    )
```

```python
import functools
import math

import jax
import jax.numpy as jnp
from jax import lax
from jax.experimental import pallas as pl
from jax.experimental.pallas import tpu as pltpu
from jax.sharding import PartitionSpec as P

HEAD_DIM = 64
HALF = HEAD_DIM // 2
LANES = 128
HALO = 16
WINDOW = 64
CHUNK = 32
MESH = pl.DeviceIdType.MESH
BF16 = jnp.bfloat16
F32 = jnp.float32


def layer_norm(values, gain):
    mean = jnp.mean(values, axis=-1, keepdims=True)
    centered = values - mean
    var = jnp.mean(centered * centered, axis=-1, keepdims=True)
    return centered / jnp.sqrt(var + 1e-05) * gain


def matmul(a, b):
    return jnp.dot(a, b, preferred_element_type=F32)


def folded(rows):
    half = rows.shape[0] // 2
    lane = lax.broadcasted_iota(jnp.int32, (half, LANES), 1)
    return jnp.where(lane < HEAD_DIM, pltpu.roll(rows[:half], HEAD_DIM, 1), rows[half:])


def all_heads(ref):
    columns = []
    lane = lax.broadcasted_iota(jnp.int32, ref.shape[1:], 1)
    for pair in range(ref.shape[0] // 2):
        even = ref[2 * pair].astype(F32)
        odd = ref[2 * pair + 1].astype(F32)
        top = jnp.where(lane < HEAD_DIM, even, pltpu.roll(odd, HEAD_DIM, 1))
        bottom = jnp.where(lane < HEAD_DIM, pltpu.roll(even, HEAD_DIM, 1), odd)
        columns.append(jnp.concatenate([top, bottom], axis=0))
    return jnp.concatenate(columns, axis=1)


def layer_kernel(
    side,
    frames_hbm,
    attn_gain_hbm,
    conv_gain_hbm,
    scale_hbm,
    shift_hbm,
    taps_hbm,
    w_query_hbm,
    w_key_hbm,
    w_value_hbm,
    w_out_hbm,
    w_expand_hbm,
    w_project_hbm,
    attended_ref,
    layer_ref,
    frames_ref,
    gains_ref,
    taps_ref,
    w_query,
    w_key,
    w_value,
    w_out,
    w_expand,
    w_project,
    head_send,
    head_recv,
    kv_all,
    near_wide,
    far_wide,
    near_keys,
    far_keys,
    q_all,
    near_scores,
    far_scores,
    near_weights,
    far_weights,
    tops,
    first_mixed,
    first_tops,
    part_send,
    part_recv,
    ctx_send,
    ctx_recv,
    edge_send,
    edge_recv,
    context,
    halo_send,
    halo_recv,
    padded,
    load_sem,
    head_ssem,
    head_rsem,
    kv_ssem,
    kv_rsem,
    q_ssem,
    q_rsem,
    part_ssem,
    part_rsem,
    ctx_ssem,
    ctx_rsem,
    edge_ssem,
    edge_rsem,
    halo_ssem,
    halo_rsem,
):
    rows, width = frames_ref.shape
    groups = head_send.shape[0]
    block = rows * groups
    half_block = block // 2
    level_rows = -(-block // LANES)
    blocks = side * side
    tm = lax.axis_index("tm")
    kv = lax.axis_index("kv")
    bits = side.bit_length() - 1
    core = kv & 1
    slow = tm >> bits
    fast = tm & (side - 1)
    key_at = fast + core * (slow - fast)
    key_stride = 1 + core * (side - 1)
    query_at = slow + core * (fast - slow)
    query_stride = side - core * (side - 1)

    def kv_peer(d):
        return (tm, (kv + d) & (groups - 1))

    def key_peer(d):
        return (tm + (((key_at + d) & (side - 1)) - key_at) * key_stride, kv)

    def query_peer(d):
        return (tm + (((query_at + d) & (side - 1)) - query_at) * query_stride, kv)

    devices = groups * blocks
    me = tm * groups + kv
    following = (me + 1) & (devices - 1)
    preceding = (me - 1) & (devices - 1)
    group_bits = groups.bit_length() - 1
    following = (following >> group_bits, following & (groups - 1))
    preceding = (preceding >> group_bits, preceding & (groups - 1))
    later = (tm + 1) & (blocks - 1)
    earlier = (tm - 1) & (blocks - 1)
    near = sorted(range(1, side), key=lambda d: min(d, side - d))

    def greet(device):
        pl.semaphore_signal(barrier, inc=1, device_id=device, device_id_type=MESH)

    loads = [
        pltpu.make_async_copy(source, target, load_sem.at[i])
        for i, (source, target) in enumerate(
            (
                (frames_hbm, frames_ref),
                (attn_gain_hbm, gains_ref.at[0:1]),
                (w_key_hbm, w_key),
                (w_value_hbm, w_value),
                (w_query_hbm, w_query),
                (w_out_hbm, w_out),
                (w_expand_hbm, w_expand),
                (taps_hbm, taps_ref),
                (conv_gain_hbm, gains_ref.at[1:2]),
                (scale_hbm, gains_ref.at[2:3]),
                (shift_hbm, gains_ref.at[3:4]),
                (w_project_hbm, w_project),
            )
        )
    ]
    for load in loads[:5]:
        load.start()

    barrier = pltpu.get_barrier_semaphore()
    for d in range(1, groups):
        greet(kv_peer(d))
    for d in near[:4]:
        greet(key_peer(d))
        greet(query_peer(d))

    lane = lax.broadcasted_iota(jnp.int32, (rows, LANES), 1)
    low = lane < HEAD_DIM
    first_half = lane % HEAD_DIM < HALF
    which = lax.broadcasted_iota(jnp.int32, (1, LANES), 1) % HALF
    inverse = jnp.zeros((1, LANES), F32)
    for i in range(HALF):
        inverse = jnp.where(which == i, 10000.0 ** (-2.0 * i / HEAD_DIM), inverse)
    positions = me * rows + lax.broadcasted_iota(jnp.int32, (rows, LANES), 0)
    angle = positions.astype(F32) * inverse
    cosine = jnp.cos(angle)
    sine = jnp.sin(angle)
    sine = jnp.where(first_half, -sine, sine)

    def rotated(part):
        swapped = jnp.where(
            first_half, pltpu.roll(part, LANES - HALF, 1), pltpu.roll(part, HALF, 1)
        )
        return part * cosine + swapped * sine

    loads[0].wait()
    loads[1].wait()
    inputs = frames_ref[...].astype(F32)
    halo_send[0] = inputs[:HALO].astype(BF16)
    halo_send[1] = inputs[rows - HALO :].astype(BF16)
    normed = layer_norm(inputs, gains_ref[0:1]).astype(BF16)
    loads[2].wait()
    keys = matmul(normed, w_key[...])
    loads[3].wait()
    values = matmul(normed, w_value[...])
    loads[4].wait()
    queries = matmul(normed, w_query[...])
    to_log2 = 0.125 / math.log(2.0)
    for pair in range(groups // 2):
        at = slice(pair * LANES, (pair + 1) * LANES)
        key = rotated(keys[:, at])
        query = rotated(queries[:, at]) * to_log2
        value = values[:, at]
        key_value = jnp.where(low, key, pltpu.roll(value, HEAD_DIM, 1))
        head_send[2 * pair] = jnp.concatenate(
            [key_value, jnp.where(low, query, 0.0)], axis=0
        ).astype(BF16)
        key_value = jnp.where(low, pltpu.roll(key, HEAD_DIM, 1), value)
        head_send[2 * pair + 1] = jnp.concatenate(
            [key_value, jnp.where(low, pltpu.roll(query, HEAD_DIM, 1), 0.0)], axis=0
        ).astype(BF16)

    pl.semaphore_wait(barrier, groups - 1 + 2 * len(near[:4]))

    head_copies = [
        pltpu.make_async_remote_copy(
            src_ref=head_send.at[(kv + d) & (groups - 1)],
            dst_ref=head_recv.at[kv],
            send_sem=head_ssem.at[d],
            recv_sem=head_rsem.at[d],
            device_id=kv_peer(d),
            device_id_type=MESH,
        )
        for d in range(1, groups)
    ]
    for copy in head_copies:
        copy.start()
    for load in loads[5:]:
        load.start()
    head_recv[kv] = head_send[kv]
    for copy in head_copies:
        copy.wait_recv()
    pieces = [head_recv[head].astype(F32) for head in range(groups)]
    own_block = jnp.concatenate([piece[:rows] for piece in pieces], axis=0).astype(BF16)
    kv_all[0] = own_block

    def line_copies(ref, ssem, rsem, peer):
        half = ref.shape[1] // 2
        lower, upper = pl.ds(0, half), pl.ds(half, half)

        def copy(source, target, place, sem):
            return pltpu.make_async_remote_copy(
                src_ref=source,
                dst_ref=target,
                send_sem=ssem.at[sem],
                recv_sem=rsem.at[sem],
                device_id=peer(place),
                device_id_type=MESH,
            )

        if side < 8:
            return {d: copy(ref.at[0], ref.at[d], d, d) for d in near}, {}
        direct = {d: copy(ref.at[0], ref.at[d], d, d) for d in near[:4]}
        relayed = {
            2: {
                3: copy(ref.at[2], ref.at[3], 1, 3),
                4: copy(ref.at[2, lower], ref.at[4, lower], 2, 4),
            },
            6: {
                5: copy(ref.at[6], ref.at[5], 7, 5),
                0: copy(ref.at[6, upper], ref.at[4, upper], 6, 0),
            },
        }
        return direct, relayed

    kv_direct, kv_relayed = line_copies(kv_all, kv_ssem, kv_rsem, key_peer)
    q_direct, q_relayed = line_copies(q_all, q_ssem, q_rsem, query_peer)
    lines = ((kv_direct, kv_relayed), (q_direct, q_relayed))
    for copy in kv_direct.values():
        copy.start()
    own_queries = jnp.concatenate([piece[rows:] for piece in pieces], axis=0)
    q_all[0] = (
        own_queries[:half_block] + pltpu.roll(own_queries[half_block:], HEAD_DIM, 1)
    ).astype(BF16)
    for copy in q_direct.values():
        copy.start()
    for direct, relayed in lines:
        for d, onward in relayed.items():
            direct[d].wait_recv()
            for copy in onward.values():
                copy.start()
    slots = [0] + near
    near_slots = slots[: near_wide.shape[0] // block]
    far_slots = slots[len(near_slots) :]

    def wait_for(wanted):
        for direct, relayed in lines:
            for d, copy in direct.items():
                if d in wanted and d not in relayed:
                    copy.wait_recv()
            for onward in relayed.values():
                for d, copy in onward.items():
                    if (d or 4) in wanted:
                        copy.wait_recv()

    def lay_out(wanted, wide, keys):
        for i in range(0, len(wanted), 2):
            few = wanted[i : i + 2]
            both = jnp.concatenate([kv_all[d] for d in few], axis=0)
            at = slice(i * block, (i + len(few)) * block)
            both = both.astype(F32)
            keys[:, at] = both.T.astype(BF16)
            lane = lax.broadcasted_iota(jnp.int32, both.shape, 1)
            wide[at] = jnp.where(lane < HEAD_DIM, 1.0, both).astype(BF16)

    half_lane = lax.broadcasted_iota(jnp.int32, (half_block, LANES), 1)
    block_lane = lax.broadcasted_iota(jnp.int32, (block, LANES), 1)

    def unfolded(d):
        packed = q_all[d].astype(F32)
        return jnp.concatenate(
            [
                jnp.where(half_lane < HEAD_DIM, packed, 0.0),
                jnp.where(half_lane < HEAD_DIM, pltpu.roll(packed, HEAD_DIM, 1), 0.0),
            ],
            axis=0,
        ).astype(BF16)

    def soften(pieces, floor=None):
        for begin in range(0, block, CHUNK):
            at = slice(begin, begin + CHUNK)
            score = [scores[at] for scores, _ in pieces]
            top = functools.reduce(
                jnp.maximum, [jnp.max(part, axis=1, keepdims=True) for part in score]
            )
            if floor is not None:
                top = jnp.maximum(top, floor[at, :1])
            for part, (_, weights) in zip(score, pieces):
                weights[at] = jnp.exp2(part - top).astype(BF16)
            tops[at] = jnp.broadcast_to(top, (CHUNK, LANES))

    def finish(d, mixed):
        total = jnp.where(block_lane < HEAD_DIM, mixed, pltpu.roll(mixed, HEAD_DIM, 1))
        level = tops[...] + jnp.log2(total)
        place = lax.broadcasted_iota(jnp.int32, (HALO, LANES), 0)
        levels = jnp.zeros((HALO, LANES), F32)
        for i in range(level_rows):
            few = level[i * LANES : (i + 1) * LANES]
            row = lax.broadcasted_iota(jnp.int32, few.shape, 0)
            column = lax.broadcasted_iota(jnp.int32, few.shape, 1)
            line = jnp.sum(jnp.where(row == column, few, 0.0), axis=0, keepdims=True)
            high = line.astype(BF16).astype(F32)
            levels = jnp.where(place == i, high, levels)
            levels = jnp.where(place == level_rows + i, line - high, levels)
        part_send[d] = jnp.concatenate(
            [folded(mixed / total), levels], axis=0
        ).astype(BF16)

    def chosen(step, order):
        return sum((step == i).astype(jnp.int32) * d for i, d in enumerate(order))

    wait_for(near_slots)
    lay_out(near_slots, near_wide, near_keys)

    @pl.loop(0, len(near_slots))
    def _(step):
        near_scores[...] = matmul(unfolded(chosen(step, near_slots)), near_keys[...])
        soften([(near_scores, near_weights)])
        first_mixed[step] = matmul(near_weights[...], near_wide[...])
        first_tops[step] = tops[...]

    wait_for(far_slots)
    lay_out(far_slots, far_wide, far_keys)

    def part_copy(d):
        return pltpu.make_async_remote_copy(
            src_ref=part_send.at[d],
            dst_ref=part_recv.at[d],
            send_sem=part_ssem.at[d],
            recv_sem=part_rsem.at[d],
            device_id=query_peer(side - d),
            device_id_type=MESH,
        )

    @pl.loop(0, len(far_slots))
    def _(step):
        d = chosen(step, far_slots[::-1])
        query = unfolded(d)
        near_scores[...] = matmul(query, near_keys[...])
        far_scores[...] = matmul(query, far_keys[...])
        soften([(near_scores, near_weights), (far_scores, far_weights)])
        mixed = matmul(near_weights[...], near_wide[...])
        finish(d, mixed + matmul(far_weights[...], far_wide[...]))
        part_copy(d).start()

    @pl.loop(0, len(near_slots))
    def _(step):
        at = len(near_slots) - 1 - step
        d = chosen(at, near_slots)
        far_scores[...] = matmul(unfolded(d), far_keys[...])
        soften([(far_scores, far_weights)], first_tops.at[at])
        mixed = first_mixed[at] * jnp.exp2(first_tops[at] - tops[...])
        finish(d, mixed + matmul(far_weights[...], far_wide[...]))

        @pl.when(at > 0)
        def _():
            part_copy(d).start()

    part_recv[0] = part_send[0]
    for d in range(1, side):
        part_copy(d).wait_recv()

    levels = []
    for i in range(level_rows):
        levels.append(
            [
                part_recv[d, half_block + i : half_block + i + 1].astype(F32)
                + part_recv[d, half_block + level_rows + i : half_block + level_rows + i + 1].astype(F32)
                for d in range(side)
            ]
        )
    shares = []
    for level in levels:
        level = jnp.concatenate(level, axis=0)
        fade = jnp.exp2(level - jnp.max(level, axis=0, keepdims=True))
        shares.append(fade / jnp.sum(fade, axis=0, keepdims=True))
    shares = jnp.concatenate(
        shares + [jnp.zeros((LANES - side * level_rows, LANES), F32)], axis=0
    ).T
    upper = []
    begin = half_block
    while begin < block:
        i = begin // LANES
        end = min(block, (i + 1) * LANES)
        few = shares[begin - i * LANES : end - i * LANES]
        upper.append(pltpu.roll(few, LANES - i * side, 1) if i else few)
        begin = end
    lower = shares[:half_block]
    upper = jnp.concatenate(upper, axis=0)
    pick = jnp.zeros((half_block, LANES), F32)
    for i, share in enumerate((lower, upper)):
        high = share.astype(BF16).astype(F32)
        for j, piece in enumerate((high, share - high)):
            begin = (2 * i + j) * side
            piece = pltpu.roll(piece, begin, 1) if begin else piece
            pick = jnp.where((half_lane >= begin) & (half_lane < begin + side), piece, pick)
    index = lax.broadcasted_iota(jnp.int32, (LANES, side * LANES), 0)
    lane = lax.broadcasted_iota(jnp.int32, (LANES, side * LANES), 1)
    spread = (
        (index % side == lane // LANES)
        & (index < 4 * side)
        & (index // (2 * side) == lane % LANES // HEAD_DIM)
    )
    spread = matmul(pick.astype(BF16), jnp.where(spread, 1.0, 0.0).astype(BF16))
    merged = jnp.zeros((half_block, LANES), F32)
    for d in range(side):
        part = part_recv[d].astype(F32)[:half_block]
        merged = merged + spread[:, d * LANES : (d + 1) * LANES] * part
    merged = jnp.concatenate([pltpu.roll(merged, HEAD_DIM, 1), merged], axis=0)

    edge_send[0] = folded(merged[: 2 * HALO]).astype(BF16)
    edge_send[1] = folded(merged[block - 2 * HALO :]).astype(BF16)
    framed = jnp.concatenate(
        [jnp.zeros((HALO, LANES), F32), merged, jnp.zeros((WINDOW - rows - HALO, LANES), F32)],
        axis=0,
    )
    for part in range(groups):
        ctx_send[part] = folded(framed[part * rows : part * rows + WINDOW]).astype(BF16)

    def edge_copy(i, head):
        return pltpu.make_async_remote_copy(
            src_ref=edge_send.at[i],
            dst_ref=edge_recv.at[head],
            send_sem=edge_ssem.at[i],
            recv_sem=edge_rsem.at[head],
            device_id=((earlier, groups - 1), (later, 0))[i],
            device_id_type=MESH,
        )

    for i in range(2):
        edge_copy(i, kv).start()
    ctx_copies = [
        pltpu.make_async_remote_copy(
            src_ref=ctx_send.at[(kv + d) & (groups - 1)],
            dst_ref=ctx_recv.at[kv],
            send_sem=ctx_ssem.at[d],
            recv_sem=ctx_rsem.at[d],
            device_id=kv_peer(d),
            device_id_type=MESH,
        )
        for d in range(1, groups)
    ]
    for copy in ctx_copies:
        copy.start()
    halo_copies = [
        pltpu.make_async_remote_copy(
            src_ref=halo_send.at[i],
            dst_ref=halo_recv.at[i],
            send_sem=halo_ssem.at[i],
            recv_sem=halo_rsem.at[i],
            device_id=target,
            device_id_type=MESH,
        )
        for i, target in enumerate((preceding, following))
    ]
    for copy in halo_copies:
        copy.start()
    ctx_recv[kv] = ctx_send[kv]
    for copy in head_copies:
        copy.wait_send()
    for direct, relayed in lines:
        for copy in direct.values():
            copy.wait_send()
        for onward in relayed.values():
            for copy in onward.values():
                copy.wait_send()
    for d in range(1, side):
        part_copy(d).wait_send()
    for copy in ctx_copies + halo_copies:
        copy.wait_send()
    for i in range(2):
        edge_copy(i, kv).wait_send()
    for load in loads[5:]:
        load.wait()
    for copy in halo_copies:
        copy.wait_recv()
    extent = rows + 2 * HALO
    nearby = jnp.concatenate([halo_recv[1].astype(F32), inputs, halo_recv[0].astype(F32)], axis=0)
    for copy in ctx_copies:
        copy.wait_recv()
    context[...] = all_heads(ctx_recv)[:extent]

    @pl.when(kv == 0)
    def _():
        for head in range(groups):
            edge_copy(1, head).wait_recv()
        context[:HALO] = all_heads(edge_recv)[HALO:]

    @pl.when(kv == groups - 1)
    def _():
        for head in range(groups):
            edge_copy(0, head).wait_recv()
        context[extent - HALO :] = all_heads(edge_recv)[:HALO]

    attended = matmul(context[...].astype(BF16), w_out[...]).astype(BF16).astype(F32)
    attended_ref[...] = attended[HALO : HALO + rows].astype(BF16)
    mid = nearby + attended
    conv_in = layer_norm(mid, gains_ref[1:2]).astype(BF16)
    expanded = matmul(conv_in, w_expand[...])
    gate = expanded[:, width:]
    glu = (expanded[:, :width] / (1.0 + jnp.exp(-gate))).astype(BF16).astype(F32)
    times = me * rows - HALO + lax.broadcasted_iota(jnp.int32, (extent, width), 0)
    padded[...] = jnp.where((times >= 0) & (times < devices * rows), glu, 0.0)

    depth = jnp.zeros((rows, width), F32)
    count = taps_ref.shape[0]
    for turn in range(8):
        shifted = None
        for tap in range(turn - 1, count, 8):
            if tap < 0:
                continue
            term = taps_ref[tap : tap + 1] * padded[tap + 1 - turn : tap + 9 - turn + rows]
            shifted = term if shifted is None else shifted + term
        depth = depth + shifted[turn : turn + rows]
    batch = depth * gains_ref[2:3] + gains_ref[3:4]
    act = (batch / (1.0 + jnp.exp(-batch))).astype(BF16)
    layer_ref[...] = (mid[HALO : HALO + rows] + matmul(act, w_project[...])).astype(BF16)


def copy_kernel(attended_in, layer_in, attended_out, layer_out, sem):
    copies = [
        pltpu.make_async_copy(attended_in, attended_out, sem.at[0]),
        pltpu.make_async_copy(layer_in, layer_out, sem.at[1]),
    ]
    for copy in copies:
        copy.start()
    for copy in copies:
        copy.wait()


def on_device(
    frames,
    attn_gain,
    w_query,
    w_key,
    w_value,
    w_out,
    conv_gain,
    w_expand,
    kernel,
    bn_scale,
    bn_shift,
    w_project,
):
    rows, width = frames.shape
    groups = lax.axis_size("kv")
    side = math.isqrt(lax.axis_size("tm"))
    block = rows * groups
    near_rows = (5 if side == 8 else side // 2) * block
    far_rows = side * block - near_rows
    vmem = pl.BlockSpec(memory_space=pltpu.VMEM)
    anywhere = pl.BlockSpec(memory_space=pl.ANY)
    dma = pltpu.SemaphoreType.DMA
    results = pl.pallas_call(
        functools.partial(layer_kernel, side),
        out_shape=(pltpu.VMEM((rows, width), BF16), pltpu.VMEM((rows, width), BF16)),
        in_specs=[anywhere] * 12,
        out_specs=(vmem, vmem),
        scratch_shapes=[
            pltpu.VMEM((rows, width), BF16),
            pltpu.VMEM((4, width), F32),
            pltpu.VMEM(kernel.shape, F32),
            pltpu.VMEM((width, width), BF16),
            pltpu.VMEM((width, width), BF16),
            pltpu.VMEM((width, width), BF16),
            pltpu.VMEM((width, width), BF16),
            pltpu.VMEM((width, 2 * width), BF16),
            pltpu.VMEM((width, width), BF16),
            pltpu.VMEM((groups, 2 * rows, LANES), BF16),
            pltpu.VMEM((groups, 2 * rows, LANES), BF16),
            pltpu.VMEM((side, block, LANES), BF16),
            pltpu.VMEM((near_rows, LANES), BF16),
            pltpu.VMEM((far_rows, LANES), BF16),
            pltpu.VMEM((LANES, near_rows), BF16),
            pltpu.VMEM((LANES, far_rows), BF16),
            pltpu.VMEM((side, block // 2, LANES), BF16),
            pltpu.VMEM((block, near_rows), F32),
            pltpu.VMEM((block, far_rows), F32),
            pltpu.VMEM((block, near_rows), BF16),
            pltpu.VMEM((block, far_rows), BF16),
            pltpu.VMEM((block, LANES), F32),
            pltpu.VMEM((near_rows // block, block, LANES), F32),
            pltpu.VMEM((near_rows // block, block, LANES), F32),
            pltpu.VMEM((side, block // 2 + HALO, LANES), BF16),
            pltpu.VMEM((side, block // 2 + HALO, LANES), BF16),
            pltpu.VMEM((groups, WINDOW // 2, LANES), BF16),
            pltpu.VMEM((groups, WINDOW // 2, LANES), BF16),
            pltpu.VMEM((2, HALO, LANES), BF16),
            pltpu.VMEM((groups, HALO, LANES), BF16),
            pltpu.VMEM((rows + 2 * HALO, width), F32),
            pltpu.VMEM((2, HALO, width), BF16),
            pltpu.VMEM((2, HALO, width), BF16),
            pltpu.VMEM((rows + 2 * HALO, width), F32),
            dma((12,)),
            dma((groups,)),
            dma((groups,)),
            dma((side,)),
            dma((side,)),
            dma((side,)),
            dma((side,)),
            dma((side,)),
            dma((side,)),
            dma((groups,)),
            dma((groups,)),
            dma((2,)),
            dma((groups,)),
            dma((2,)),
            dma((2,)),
        ],
        compiler_params=pltpu.CompilerParams(
            collective_id=0, has_side_effects=True, vmem_limit_bytes=60 * 1024 * 1024
        ),
    )(
        frames,
        attn_gain.reshape(1, width),
        conv_gain.reshape(1, width),
        bn_scale.reshape(1, width),
        bn_shift.reshape(1, width),
        kernel,
        w_query,
        w_key,
        w_value,
        w_out,
        w_expand,
        w_project,
    )
    return pl.pallas_call(
        copy_kernel,
        out_shape=(jax.ShapeDtypeStruct((rows, width), BF16),) * 2,
        in_specs=[vmem] * 2,
        out_specs=(anywhere, anywhere),
        scratch_shapes=[dma((2,))],
        compiler_params=pltpu.CompilerParams(vmem_limit_bytes=4 * 1024 * 1024),
    )(*results)


def solution(mesh):
    rows = P(("tm", "kv"), None)
    return jax.shard_map(
        on_device,
        mesh=mesh,
        in_specs=(rows,) + (P(),) * 11,
        out_specs=(rows, rows),
        check_vma=False,
    )
```

```python
import functools
import math

import jax
import jax.numpy as jnp
from jax import lax
from jax.experimental import pallas as pl
from jax.experimental.pallas import tpu as pltpu
from jax.sharding import PartitionSpec as P

HEAD_DIM = 64
HALF = HEAD_DIM // 2
LANES = 128
HALO = 16
WINDOW = 64
CHUNK = 32
MESH = pl.DeviceIdType.MESH
BF16 = jnp.bfloat16
F32 = jnp.float32


def layer_norm(values, gain):
    mean = jnp.mean(values, axis=-1, keepdims=True)
    centered = values - mean
    var = jnp.mean(centered * centered, axis=-1, keepdims=True)
    return centered / jnp.sqrt(var + 1e-05) * gain


def matmul(a, b):
    return jnp.dot(a, b, preferred_element_type=F32)


def folded(rows):
    half = rows.shape[0] // 2
    lane = lax.broadcasted_iota(jnp.int32, (half, LANES), 1)
    return jnp.where(lane < HEAD_DIM, pltpu.roll(rows[:half], HEAD_DIM, 1), rows[half:])


def all_heads(ref):
    columns = []
    lane = lax.broadcasted_iota(jnp.int32, ref.shape[1:], 1)
    for pair in range(ref.shape[0] // 2):
        even = ref[2 * pair].astype(F32)
        odd = ref[2 * pair + 1].astype(F32)
        top = jnp.where(lane < HEAD_DIM, even, pltpu.roll(odd, HEAD_DIM, 1))
        bottom = jnp.where(lane < HEAD_DIM, pltpu.roll(even, HEAD_DIM, 1), odd)
        columns.append(jnp.concatenate([top, bottom], axis=0))
    return jnp.concatenate(columns, axis=1)


def layer_kernel(
    side,
    frames_hbm,
    attn_gain_hbm,
    conv_gain_hbm,
    scale_hbm,
    shift_hbm,
    taps_hbm,
    w_query_hbm,
    w_key_hbm,
    w_value_hbm,
    w_out_hbm,
    w_expand_hbm,
    w_project_hbm,
    attended_ref,
    layer_ref,
    frames_ref,
    gains_ref,
    taps_ref,
    w_query,
    w_key,
    w_value,
    w_out,
    w_expand,
    w_project,
    head_send,
    head_recv,
    kv_all,
    near_wide,
    far_wide,
    near_keys,
    far_keys,
    q_all,
    near_scores,
    far_scores,
    near_weights,
    far_weights,
    tops,
    first_mixed,
    first_tops,
    part_send,
    part_recv,
    ctx_send,
    ctx_recv,
    edge_send,
    edge_recv,
    context,
    halo_send,
    halo_recv,
    padded,
    load_sem,
    head_ssem,
    head_rsem,
    kv_ssem,
    kv_rsem,
    q_ssem,
    q_rsem,
    part_ssem,
    part_rsem,
    ctx_ssem,
    ctx_rsem,
    edge_ssem,
    edge_rsem,
    halo_ssem,
    halo_rsem,
):
    rows, width = frames_ref.shape
    groups = head_send.shape[0]
    block = rows * groups
    half_block = block // 2
    level_rows = -(-block // LANES)
    blocks = side * side
    tm = lax.axis_index("tm")
    kv = lax.axis_index("kv")
    bits = side.bit_length() - 1
    core = kv & 1
    slow = tm >> bits
    fast = tm & (side - 1)
    key_at = fast + core * (slow - fast)
    key_stride = 1 + core * (side - 1)
    query_at = slow + core * (fast - slow)
    query_stride = side - core * (side - 1)

    def kv_peer(d):
        return (tm, (kv + d) & (groups - 1))

    def key_peer(d):
        return (tm + (((key_at + d) & (side - 1)) - key_at) * key_stride, kv)

    def query_peer(d):
        return (tm + (((query_at + d) & (side - 1)) - query_at) * query_stride, kv)

    devices = groups * blocks
    me = tm * groups + kv
    following = (me + 1) & (devices - 1)
    preceding = (me - 1) & (devices - 1)
    group_bits = groups.bit_length() - 1
    following = (following >> group_bits, following & (groups - 1))
    preceding = (preceding >> group_bits, preceding & (groups - 1))
    later = (tm + 1) & (blocks - 1)
    earlier = (tm - 1) & (blocks - 1)
    near = sorted(range(1, side), key=lambda d: min(d, side - d))

    def greet(device):
        pl.semaphore_signal(barrier, inc=1, device_id=device, device_id_type=MESH)

    loads = [
        pltpu.make_async_copy(source, target, load_sem.at[i])
        for i, (source, target) in enumerate(
            (
                (frames_hbm, frames_ref),
                (attn_gain_hbm, gains_ref.at[0:1]),
                (w_key_hbm, w_key),
                (w_value_hbm, w_value),
                (w_query_hbm, w_query),
                (w_out_hbm, w_out),
                (w_expand_hbm, w_expand),
                (taps_hbm, taps_ref),
                (conv_gain_hbm, gains_ref.at[1:2]),
                (scale_hbm, gains_ref.at[2:3]),
                (shift_hbm, gains_ref.at[3:4]),
                (w_project_hbm, w_project),
            )
        )
    ]
    for load in loads[:5]:
        load.start()

    barrier = pltpu.get_barrier_semaphore()
    for d in range(1, groups):
        greet(kv_peer(d))
    for d in near[:4]:
        greet(key_peer(d))
        greet(query_peer(d))

    lane = lax.broadcasted_iota(jnp.int32, (rows, LANES), 1)
    low = lane < HEAD_DIM
    first_half = lane % HEAD_DIM < HALF
    which = lax.broadcasted_iota(jnp.int32, (1, LANES), 1) % HALF
    inverse = jnp.zeros((1, LANES), F32)
    for i in range(HALF):
        inverse = jnp.where(which == i, 10000.0 ** (-2.0 * i / HEAD_DIM), inverse)
    positions = me * rows + lax.broadcasted_iota(jnp.int32, (rows, LANES), 0)
    angle = positions.astype(F32) * inverse
    cosine = jnp.cos(angle)
    sine = jnp.sin(angle)
    sine = jnp.where(first_half, -sine, sine)

    def rotated(part):
        swapped = jnp.where(
            first_half, pltpu.roll(part, LANES - HALF, 1), pltpu.roll(part, HALF, 1)
        )
        return part * cosine + swapped * sine

    loads[0].wait()
    loads[1].wait()
    inputs = frames_ref[...].astype(F32)
    halo_send[0] = inputs[:HALO].astype(BF16)
    halo_send[1] = inputs[rows - HALO :].astype(BF16)
    normed = layer_norm(inputs, gains_ref[0:1]).astype(BF16)
    loads[2].wait()
    keys = matmul(normed, w_key[...])
    loads[3].wait()
    values = matmul(normed, w_value[...])
    loads[4].wait()
    queries = matmul(normed, w_query[...])
    to_log2 = 0.125 / math.log(2.0)
    for pair in range(groups // 2):
        at = slice(pair * LANES, (pair + 1) * LANES)
        key = rotated(keys[:, at])
        query = rotated(queries[:, at]) * to_log2
        value = values[:, at]
        key_value = jnp.where(low, key, pltpu.roll(value, HEAD_DIM, 1))
        head_send[2 * pair] = jnp.concatenate(
            [key_value, jnp.where(low, query, 0.0)], axis=0
        ).astype(BF16)
        key_value = jnp.where(low, pltpu.roll(key, HEAD_DIM, 1), value)
        head_send[2 * pair + 1] = jnp.concatenate(
            [key_value, jnp.where(low, pltpu.roll(query, HEAD_DIM, 1), 0.0)], axis=0
        ).astype(BF16)

    pl.semaphore_wait(barrier, groups - 1 + 2 * len(near[:4]))

    head_copies = [
        pltpu.make_async_remote_copy(
            src_ref=head_send.at[(kv + d) & (groups - 1)],
            dst_ref=head_recv.at[kv],
            send_sem=head_ssem.at[d],
            recv_sem=head_rsem.at[d],
            device_id=kv_peer(d),
            device_id_type=MESH,
        )
        for d in range(1, groups)
    ]
    for copy in head_copies:
        copy.start()
    for load in loads[5:]:
        load.start()
    head_recv[kv] = head_send[kv]
    for copy in head_copies:
        copy.wait_recv()
    pieces = [head_recv[head].astype(F32) for head in range(groups)]
    own_block = jnp.concatenate([piece[:rows] for piece in pieces], axis=0).astype(BF16)
    kv_all[0] = own_block

    def line_copies(ref, ssem, rsem, peer):
        half = ref.shape[1] // 2
        lower, upper = pl.ds(0, half), pl.ds(half, half)

        def copy(source, target, place, sem):
            return pltpu.make_async_remote_copy(
                src_ref=source,
                dst_ref=target,
                send_sem=ssem.at[sem],
                recv_sem=rsem.at[sem],
                device_id=peer(place),
                device_id_type=MESH,
            )

        if side < 8:
            return {d: copy(ref.at[0], ref.at[d], d, d) for d in near}, {}
        direct = {d: copy(ref.at[0], ref.at[d], d, d) for d in near[:4]}
        relayed = {
            2: {
                3: copy(ref.at[2], ref.at[3], 1, 3),
                4: copy(ref.at[2, lower], ref.at[4, lower], 2, 4),
            },
            6: {
                5: copy(ref.at[6], ref.at[5], 7, 5),
                0: copy(ref.at[6, upper], ref.at[4, upper], 6, 0),
            },
        }
        return direct, relayed

    kv_direct, kv_relayed = line_copies(kv_all, kv_ssem, kv_rsem, key_peer)
    q_direct, q_relayed = line_copies(q_all, q_ssem, q_rsem, query_peer)
    lines = ((kv_direct, kv_relayed), (q_direct, q_relayed))
    for copy in kv_direct.values():
        copy.start()
    own_queries = jnp.concatenate([piece[rows:] for piece in pieces], axis=0)
    q_all[0] = (
        own_queries[:half_block] + pltpu.roll(own_queries[half_block:], HEAD_DIM, 1)
    ).astype(BF16)
    for copy in q_direct.values():
        copy.start()
    for direct, relayed in lines[::-1]:
        for d, onward in relayed.items():
            direct[d].wait_recv()
            for copy in onward.values():
                copy.start()
    slots = [0] + near
    near_slots = slots[: near_wide.shape[0] // block]
    far_slots = slots[len(near_slots) :]

    def wait_for(line, wanted):
        direct, relayed = line
        for d, copy in direct.items():
            if d in wanted and d not in relayed:
                copy.wait_recv()
        for onward in relayed.values():
            for d, copy in onward.items():
                if (d or 4) in wanted:
                    copy.wait_recv()

    def lay_out(wanted, wide, keys):
        for i in range(0, len(wanted), 2):
            few = wanted[i : i + 2]
            both = jnp.concatenate([kv_all[d] for d in few], axis=0)
            at = slice(i * block, (i + len(few)) * block)
            both = both.astype(F32)
            keys[:, at] = both.T.astype(BF16)
            lane = lax.broadcasted_iota(jnp.int32, both.shape, 1)
            wide[at] = jnp.where(lane < HEAD_DIM, 1.0, both).astype(BF16)

    half_lane = lax.broadcasted_iota(jnp.int32, (half_block, LANES), 1)
    block_lane = lax.broadcasted_iota(jnp.int32, (block, LANES), 1)

    def unfolded(d):
        packed = q_all[d].astype(F32)
        return jnp.concatenate(
            [
                jnp.where(half_lane < HEAD_DIM, packed, 0.0),
                jnp.where(half_lane < HEAD_DIM, pltpu.roll(packed, HEAD_DIM, 1), 0.0),
            ],
            axis=0,
        ).astype(BF16)

    def soften(pieces, floor=None):
        for begin in range(0, 2 * block, CHUNK):
            at = slice(begin, begin + CHUNK)
            score = [scores[at] for scores, _ in pieces]
            top = functools.reduce(
                jnp.maximum, [jnp.max(part, axis=1, keepdims=True) for part in score]
            )
            if floor is not None:
                top = jnp.maximum(top, floor[at, :1])
            for part, (_, weights) in zip(score, pieces):
                weights[at] = jnp.exp2(part - top).astype(BF16)
            tops[at] = jnp.broadcast_to(top, (CHUNK, LANES))

    def finish(d, mixed, top):
        total = jnp.where(block_lane < HEAD_DIM, mixed, pltpu.roll(mixed, HEAD_DIM, 1))
        level = top + jnp.log2(total)
        place = lax.broadcasted_iota(jnp.int32, (HALO, LANES), 0)
        levels = jnp.zeros((HALO, LANES), F32)
        for i in range(level_rows):
            few = level[i * LANES : (i + 1) * LANES]
            row = lax.broadcasted_iota(jnp.int32, few.shape, 0)
            column = lax.broadcasted_iota(jnp.int32, few.shape, 1)
            line = jnp.sum(jnp.where(row == column, few, 0.0), axis=0, keepdims=True)
            high = line.astype(BF16).astype(F32)
            levels = jnp.where(place == i, high, levels)
            levels = jnp.where(place == level_rows + i, line - high, levels)
        part_send[d] = jnp.concatenate(
            [folded(mixed / total), levels], axis=0
        ).astype(BF16)

    def chosen(step, order):
        return sum((step == i).astype(jnp.int32) * d for i, d in enumerate(order))

    steps = side // 2
    early_steps = len(near_slots) // 2

    def pair_of(step):
        return chosen(2 * step, slots), chosen(2 * step + 1, slots)

    for line in lines:
        wait_for(line, near_slots)
    lay_out(near_slots, near_wide, near_keys)

    @pl.loop(0, steps)
    def _(step):
        @pl.when(step == early_steps)
        def _():
            wait_for(lines[1], far_slots)

        first, second = pair_of(step)
        query = jnp.concatenate([unfolded(first), unfolded(second)], axis=0)
        near_scores[...] = matmul(query, near_keys[...])
        soften([(near_scores, near_weights)])
        first_mixed[step] = matmul(near_weights[...], near_wide[...])
        first_tops[step] = tops[...]

    wait_for(lines[0], far_slots)
    lay_out(far_slots, far_wide, far_keys)

    def part_copy(d):
        return pltpu.make_async_remote_copy(
            src_ref=part_send.at[d],
            dst_ref=part_recv.at[d],
            send_sem=part_ssem.at[d],
            recv_sem=part_rsem.at[d],
            device_id=query_peer(side - d),
            device_id_type=MESH,
        )

    @pl.loop(0, steps)
    def _(turn):
        step = steps - 1 - turn
        first, second = pair_of(step)
        query = jnp.concatenate([unfolded(first), unfolded(second)], axis=0)
        far_scores[...] = matmul(query, far_keys[...])
        soften([(far_scores, far_weights)], first_tops.at[step])
        mixed = first_mixed[step] * jnp.exp2(first_tops[step] - tops[...])
        mixed = mixed + matmul(far_weights[...], far_wide[...])
        finish(second, mixed[block:], tops[block:])
        part_copy(second).start()
        finish(first, mixed[:block], tops[:block])

        @pl.when(step > 0)
        def _():
            part_copy(first).start()

    part_recv[0] = part_send[0]
    for d in range(1, side):
        part_copy(d).wait_recv()

    levels = []
    for i in range(level_rows):
        levels.append(
            [
                part_recv[d, half_block + i : half_block + i + 1].astype(F32)
                + part_recv[d, half_block + level_rows + i : half_block + level_rows + i + 1].astype(F32)
                for d in range(side)
            ]
        )
    shares = []
    for level in levels:
        level = jnp.concatenate(level, axis=0)
        fade = jnp.exp2(level - jnp.max(level, axis=0, keepdims=True))
        shares.append(fade / jnp.sum(fade, axis=0, keepdims=True))
    shares = jnp.concatenate(
        shares + [jnp.zeros((LANES - side * level_rows, LANES), F32)], axis=0
    ).T
    upper = []
    begin = half_block
    while begin < block:
        i = begin // LANES
        end = min(block, (i + 1) * LANES)
        few = shares[begin - i * LANES : end - i * LANES]
        upper.append(pltpu.roll(few, LANES - i * side, 1) if i else few)
        begin = end
    lower = shares[:half_block]
    upper = jnp.concatenate(upper, axis=0)
    pick = jnp.zeros((half_block, LANES), F32)
    for i, share in enumerate((lower, upper)):
        high = share.astype(BF16).astype(F32)
        for j, piece in enumerate((high, share - high)):
            begin = (2 * i + j) * side
            piece = pltpu.roll(piece, begin, 1) if begin else piece
            pick = jnp.where((half_lane >= begin) & (half_lane < begin + side), piece, pick)
    index = lax.broadcasted_iota(jnp.int32, (LANES, side * LANES), 0)
    lane = lax.broadcasted_iota(jnp.int32, (LANES, side * LANES), 1)
    spread = (
        (index % side == lane // LANES)
        & (index < 4 * side)
        & (index // (2 * side) == lane % LANES // HEAD_DIM)
    )
    spread = matmul(pick.astype(BF16), jnp.where(spread, 1.0, 0.0).astype(BF16))
    merged = jnp.zeros((half_block, LANES), F32)
    for d in range(side):
        part = part_recv[d].astype(F32)[:half_block]
        merged = merged + spread[:, d * LANES : (d + 1) * LANES] * part
    merged = jnp.concatenate([pltpu.roll(merged, HEAD_DIM, 1), merged], axis=0)

    edge_send[0] = folded(merged[: 2 * HALO]).astype(BF16)
    edge_send[1] = folded(merged[block - 2 * HALO :]).astype(BF16)
    framed = jnp.concatenate(
        [jnp.zeros((HALO, LANES), F32), merged, jnp.zeros((WINDOW - rows - HALO, LANES), F32)],
        axis=0,
    )
    for part in range(groups):
        ctx_send[part] = folded(framed[part * rows : part * rows + WINDOW]).astype(BF16)

    def edge_copy(i, head):
        return pltpu.make_async_remote_copy(
            src_ref=edge_send.at[i],
            dst_ref=edge_recv.at[head],
            send_sem=edge_ssem.at[i],
            recv_sem=edge_rsem.at[head],
            device_id=((earlier, groups - 1), (later, 0))[i],
            device_id_type=MESH,
        )

    for i in range(2):
        edge_copy(i, kv).start()
    ctx_copies = [
        pltpu.make_async_remote_copy(
            src_ref=ctx_send.at[(kv + d) & (groups - 1)],
            dst_ref=ctx_recv.at[kv],
            send_sem=ctx_ssem.at[d],
            recv_sem=ctx_rsem.at[d],
            device_id=kv_peer(d),
            device_id_type=MESH,
        )
        for d in range(1, groups)
    ]
    for copy in ctx_copies:
        copy.start()
    halo_copies = [
        pltpu.make_async_remote_copy(
            src_ref=halo_send.at[i],
            dst_ref=halo_recv.at[i],
            send_sem=halo_ssem.at[i],
            recv_sem=halo_rsem.at[i],
            device_id=target,
            device_id_type=MESH,
        )
        for i, target in enumerate((preceding, following))
    ]
    for copy in halo_copies:
        copy.start()
    ctx_recv[kv] = ctx_send[kv]
    for copy in head_copies:
        copy.wait_send()
    for direct, relayed in lines:
        for copy in direct.values():
            copy.wait_send()
        for onward in relayed.values():
            for copy in onward.values():
                copy.wait_send()
    for d in range(1, side):
        part_copy(d).wait_send()
    for copy in ctx_copies + halo_copies:
        copy.wait_send()
    for i in range(2):
        edge_copy(i, kv).wait_send()
    for load in loads[5:]:
        load.wait()
    for copy in halo_copies:
        copy.wait_recv()
    extent = rows + 2 * HALO
    nearby = jnp.concatenate([halo_recv[1].astype(F32), inputs, halo_recv[0].astype(F32)], axis=0)
    for copy in ctx_copies:
        copy.wait_recv()
    context[...] = all_heads(ctx_recv)[:extent]

    @pl.when(kv == 0)
    def _():
        for head in range(groups):
            edge_copy(1, head).wait_recv()
        context[:HALO] = all_heads(edge_recv)[HALO:]

    @pl.when(kv == groups - 1)
    def _():
        for head in range(groups):
            edge_copy(0, head).wait_recv()
        context[extent - HALO :] = all_heads(edge_recv)[:HALO]

    attended = matmul(context[...].astype(BF16), w_out[...]).astype(BF16).astype(F32)
    attended_ref[...] = attended[HALO : HALO + rows].astype(BF16)
    mid = nearby + attended
    conv_in = layer_norm(mid, gains_ref[1:2]).astype(BF16)
    expanded = matmul(conv_in, w_expand[...])
    gate = expanded[:, width:]
    glu = (expanded[:, :width] / (1.0 + jnp.exp(-gate))).astype(BF16).astype(F32)
    times = me * rows - HALO + lax.broadcasted_iota(jnp.int32, (extent, width), 0)
    padded[...] = jnp.where((times >= 0) & (times < devices * rows), glu, 0.0)

    depth = jnp.zeros((rows, width), F32)
    count = taps_ref.shape[0]
    for turn in range(8):
        shifted = None
        for tap in range(turn - 1, count, 8):
            if tap < 0:
                continue
            term = taps_ref[tap : tap + 1] * padded[tap + 1 - turn : tap + 9 - turn + rows]
            shifted = term if shifted is None else shifted + term
        depth = depth + shifted[turn : turn + rows]
    batch = depth * gains_ref[2:3] + gains_ref[3:4]
    act = (batch / (1.0 + jnp.exp(-batch))).astype(BF16)
    layer_ref[...] = (mid[HALO : HALO + rows] + matmul(act, w_project[...])).astype(BF16)


def copy_kernel(attended_in, layer_in, attended_out, layer_out, sem):
    copies = [
        pltpu.make_async_copy(attended_in, attended_out, sem.at[0]),
        pltpu.make_async_copy(layer_in, layer_out, sem.at[1]),
    ]
    for copy in copies:
        copy.start()
    for copy in copies:
        copy.wait()


def on_device(
    frames,
    attn_gain,
    w_query,
    w_key,
    w_value,
    w_out,
    conv_gain,
    w_expand,
    kernel,
    bn_scale,
    bn_shift,
    w_project,
):
    rows, width = frames.shape
    groups = lax.axis_size("kv")
    side = math.isqrt(lax.axis_size("tm"))
    block = rows * groups
    near_rows = (5 if side == 8 else side // 2) * block
    far_rows = side * block - near_rows
    vmem = pl.BlockSpec(memory_space=pltpu.VMEM)
    anywhere = pl.BlockSpec(memory_space=pl.ANY)
    dma = pltpu.SemaphoreType.DMA
    results = pl.pallas_call(
        functools.partial(layer_kernel, side),
        out_shape=(pltpu.VMEM((rows, width), BF16), pltpu.VMEM((rows, width), BF16)),
        in_specs=[anywhere] * 12,
        out_specs=(vmem, vmem),
        scratch_shapes=[
            pltpu.VMEM((rows, width), BF16),
            pltpu.VMEM((4, width), F32),
            pltpu.VMEM(kernel.shape, F32),
            pltpu.VMEM((width, width), BF16),
            pltpu.VMEM((width, width), BF16),
            pltpu.VMEM((width, width), BF16),
            pltpu.VMEM((width, width), BF16),
            pltpu.VMEM((width, 2 * width), BF16),
            pltpu.VMEM((width, width), BF16),
            pltpu.VMEM((groups, 2 * rows, LANES), BF16),
            pltpu.VMEM((groups, 2 * rows, LANES), BF16),
            pltpu.VMEM((side, block, LANES), BF16),
            pltpu.VMEM((near_rows, LANES), BF16),
            pltpu.VMEM((far_rows, LANES), BF16),
            pltpu.VMEM((LANES, near_rows), BF16),
            pltpu.VMEM((LANES, far_rows), BF16),
            pltpu.VMEM((side, block // 2, LANES), BF16),
            pltpu.VMEM((2 * block, near_rows), F32),
            pltpu.VMEM((2 * block, far_rows), F32),
            pltpu.VMEM((2 * block, near_rows), BF16),
            pltpu.VMEM((2 * block, far_rows), BF16),
            pltpu.VMEM((2 * block, LANES), F32),
            pltpu.VMEM((side // 2, 2 * block, LANES), F32),
            pltpu.VMEM((side // 2, 2 * block, LANES), F32),
            pltpu.VMEM((side, block // 2 + HALO, LANES), BF16),
            pltpu.VMEM((side, block // 2 + HALO, LANES), BF16),
            pltpu.VMEM((groups, WINDOW // 2, LANES), BF16),
            pltpu.VMEM((groups, WINDOW // 2, LANES), BF16),
            pltpu.VMEM((2, HALO, LANES), BF16),
            pltpu.VMEM((groups, HALO, LANES), BF16),
            pltpu.VMEM((rows + 2 * HALO, width), F32),
            pltpu.VMEM((2, HALO, width), BF16),
            pltpu.VMEM((2, HALO, width), BF16),
            pltpu.VMEM((rows + 2 * HALO, width), F32),
            dma((12,)),
            dma((groups,)),
            dma((groups,)),
            dma((side,)),
            dma((side,)),
            dma((side,)),
            dma((side,)),
            dma((side,)),
            dma((side,)),
            dma((groups,)),
            dma((groups,)),
            dma((2,)),
            dma((groups,)),
            dma((2,)),
            dma((2,)),
        ],
        compiler_params=pltpu.CompilerParams(
            collective_id=0, has_side_effects=True, vmem_limit_bytes=60 * 1024 * 1024
        ),
    )(
        frames,
        attn_gain.reshape(1, width),
        conv_gain.reshape(1, width),
        bn_scale.reshape(1, width),
        bn_shift.reshape(1, width),
        kernel,
        w_query,
        w_key,
        w_value,
        w_out,
        w_expand,
        w_project,
    )
    return pl.pallas_call(
        copy_kernel,
        out_shape=(jax.ShapeDtypeStruct((rows, width), BF16),) * 2,
        in_specs=[vmem] * 2,
        out_specs=(anywhere, anywhere),
        scratch_shapes=[dma((2,))],
        compiler_params=pltpu.CompilerParams(vmem_limit_bytes=4 * 1024 * 1024),
    )(*results)


def solution(mesh):
    rows = P(("tm", "kv"), None)
    return jax.shard_map(
        on_device,
        mesh=mesh,
        in_specs=(rows,) + (P(),) * 11,
        out_specs=(rows, rows),
        check_vma=False,
    )
```

```python
import functools
import math

import jax
import jax.numpy as jnp
from jax import lax
from jax.experimental import pallas as pl
from jax.experimental.pallas import tpu as pltpu
from jax.sharding import PartitionSpec as P

HEAD_DIM = 64
HALF = HEAD_DIM // 2
LANES = 128
HALO = 16
WINDOW = 64
CHUNK = 32
MESH = pl.DeviceIdType.MESH
BF16 = jnp.bfloat16
F32 = jnp.float32


def layer_norm(values, gain):
    mean = jnp.mean(values, axis=-1, keepdims=True)
    centered = values - mean
    var = jnp.mean(centered * centered, axis=-1, keepdims=True)
    return centered / jnp.sqrt(var + 1e-05) * gain


def matmul(a, b):
    return jnp.dot(a, b, preferred_element_type=F32)


def folded(rows):
    half = rows.shape[0] // 2
    lane = lax.broadcasted_iota(jnp.int32, (half, LANES), 1)
    return jnp.where(lane < HEAD_DIM, pltpu.roll(rows[:half], HEAD_DIM, 1), rows[half:])


def all_heads(ref):
    columns = []
    lane = lax.broadcasted_iota(jnp.int32, ref.shape[1:], 1)
    for pair in range(ref.shape[0] // 2):
        even = ref[2 * pair].astype(F32)
        odd = ref[2 * pair + 1].astype(F32)
        top = jnp.where(lane < HEAD_DIM, even, pltpu.roll(odd, HEAD_DIM, 1))
        bottom = jnp.where(lane < HEAD_DIM, pltpu.roll(even, HEAD_DIM, 1), odd)
        columns.append(jnp.concatenate([top, bottom], axis=0))
    return jnp.concatenate(columns, axis=1)


def layer_kernel(
    side,
    frames_hbm,
    attn_gain_hbm,
    conv_gain_hbm,
    scale_hbm,
    shift_hbm,
    taps_hbm,
    w_query_hbm,
    w_key_hbm,
    w_value_hbm,
    w_out_hbm,
    w_expand_hbm,
    w_project_hbm,
    attended_ref,
    layer_ref,
    frames_ref,
    gains_ref,
    taps_ref,
    w_query,
    w_key,
    w_value,
    w_out,
    w_expand,
    w_project,
    head_send,
    head_recv,
    kv_all,
    near_wide,
    far_wide,
    near_keys,
    far_keys,
    q_all,
    near_scores,
    far_scores,
    near_weights,
    far_weights,
    far_tops,
    first_mixed,
    first_tops,
    part_send,
    part_recv,
    ctx_send,
    ctx_recv,
    edge_send,
    edge_recv,
    context,
    halo_send,
    halo_recv,
    padded,
    load_sem,
    head_ssem,
    head_rsem,
    kv_ssem,
    kv_rsem,
    q_ssem,
    q_rsem,
    part_ssem,
    part_rsem,
    ctx_ssem,
    ctx_rsem,
    edge_ssem,
    edge_rsem,
    halo_ssem,
    halo_rsem,
):
    rows, width = frames_ref.shape
    groups = head_send.shape[0]
    block = rows * groups
    half_block = block // 2
    level_rows = -(-block // LANES)
    blocks = side * side
    tm = lax.axis_index("tm")
    kv = lax.axis_index("kv")
    bits = side.bit_length() - 1
    core = kv & 1
    slow = tm >> bits
    fast = tm & (side - 1)
    key_at = fast + core * (slow - fast)
    key_stride = 1 + core * (side - 1)
    query_at = slow + core * (fast - slow)
    query_stride = side - core * (side - 1)

    def kv_peer(d):
        return (tm, (kv + d) & (groups - 1))

    def key_peer(d):
        return (tm + (((key_at + d) & (side - 1)) - key_at) * key_stride, kv)

    def query_peer(d):
        return (tm + (((query_at + d) & (side - 1)) - query_at) * query_stride, kv)

    devices = groups * blocks
    me = tm * groups + kv
    following = (me + 1) & (devices - 1)
    preceding = (me - 1) & (devices - 1)
    group_bits = groups.bit_length() - 1
    following = (following >> group_bits, following & (groups - 1))
    preceding = (preceding >> group_bits, preceding & (groups - 1))
    later = (tm + 1) & (blocks - 1)
    earlier = (tm - 1) & (blocks - 1)
    far_first = sorted(range(1, groups), key=lambda d: -min(d, groups - d))
    near = sorted(range(1, side), key=lambda d: min(d, side - d))

    def greet(device):
        pl.semaphore_signal(barrier, inc=1, device_id=device, device_id_type=MESH)

    loads = [
        pltpu.make_async_copy(source, target, load_sem.at[i])
        for i, (source, target) in enumerate(
            (
                (frames_hbm, frames_ref),
                (attn_gain_hbm, gains_ref.at[0:1]),
                (w_key_hbm, w_key),
                (w_value_hbm, w_value),
                (w_query_hbm, w_query),
                (w_out_hbm, w_out),
                (w_expand_hbm, w_expand),
                (taps_hbm, taps_ref),
                (conv_gain_hbm, gains_ref.at[1:2]),
                (scale_hbm, gains_ref.at[2:3]),
                (shift_hbm, gains_ref.at[3:4]),
                (w_project_hbm, w_project),
            )
        )
    ]
    for load in loads[:5]:
        load.start()

    barrier = pltpu.get_barrier_semaphore()
    for d in range(1, groups):
        greet(kv_peer(d))
    for d in near[:4]:
        greet(key_peer(d))
        greet(query_peer(d))

    lane = lax.broadcasted_iota(jnp.int32, (rows, LANES), 1)
    low = lane < HEAD_DIM
    first_half = lane % HEAD_DIM < HALF
    which = lax.broadcasted_iota(jnp.int32, (1, LANES), 1) % HALF
    inverse = jnp.zeros((1, LANES), F32)
    for i in range(HALF):
        inverse = jnp.where(which == i, 10000.0 ** (-2.0 * i / HEAD_DIM), inverse)
    positions = me * rows + lax.broadcasted_iota(jnp.int32, (rows, LANES), 0)
    angle = positions.astype(F32) * inverse
    cosine = jnp.cos(angle)
    sine = jnp.sin(angle)
    sine = jnp.where(first_half, -sine, sine)

    def rotated(part):
        swapped = jnp.where(
            first_half, pltpu.roll(part, LANES - HALF, 1), pltpu.roll(part, HALF, 1)
        )
        return part * cosine + swapped * sine

    loads[0].wait()
    loads[1].wait()
    inputs = frames_ref[...].astype(F32)
    halo_send[0] = inputs[:HALO].astype(BF16)
    halo_send[1] = inputs[rows - HALO :].astype(BF16)
    normed = layer_norm(inputs, gains_ref[0:1]).astype(BF16)
    loads[2].wait()
    keys = matmul(normed, w_key[...])
    loads[3].wait()
    values = matmul(normed, w_value[...])
    loads[4].wait()
    queries = matmul(normed, w_query[...])
    to_log2 = 0.125 / math.log(2.0)
    for pair in range(groups // 2):
        at = slice(pair * LANES, (pair + 1) * LANES)
        key = rotated(keys[:, at])
        query = rotated(queries[:, at]) * to_log2
        value = values[:, at]
        key_value = jnp.where(low, key, pltpu.roll(value, HEAD_DIM, 1))
        head_send[2 * pair] = jnp.concatenate(
            [key_value, jnp.where(low, query, 0.0)], axis=0
        ).astype(BF16)
        key_value = jnp.where(low, pltpu.roll(key, HEAD_DIM, 1), value)
        head_send[2 * pair + 1] = jnp.concatenate(
            [key_value, jnp.where(low, pltpu.roll(query, HEAD_DIM, 1), 0.0)], axis=0
        ).astype(BF16)

    pl.semaphore_wait(barrier, groups - 1 + 2 * len(near[:4]))

    head_copies = [
        pltpu.make_async_remote_copy(
            src_ref=head_send.at[(kv + d) & (groups - 1)],
            dst_ref=head_recv.at[kv],
            send_sem=head_ssem.at[d],
            recv_sem=head_rsem.at[d],
            device_id=kv_peer(d),
            device_id_type=MESH,
        )
        for d in far_first
    ]
    for copy in head_copies:
        copy.start()
    for load in loads[5:]:
        load.start()
    head_recv[kv] = head_send[kv]
    for copy in head_copies:
        copy.wait_recv()
    pieces = [head_recv[head].astype(F32) for head in range(groups)]
    own_block = jnp.concatenate([piece[:rows] for piece in pieces], axis=0).astype(BF16)
    kv_all[0] = own_block

    def line_copies(ref, ssem, rsem, peer):
        half = ref.shape[1] // 2
        lower, upper = pl.ds(0, half), pl.ds(half, half)

        def copy(source, target, place, sem):
            return pltpu.make_async_remote_copy(
                src_ref=source,
                dst_ref=target,
                send_sem=ssem.at[sem],
                recv_sem=rsem.at[sem],
                device_id=peer(place),
                device_id_type=MESH,
            )

        if side < 8:
            return {d: copy(ref.at[0], ref.at[d], d, d) for d in near}, {}
        direct = {d: copy(ref.at[0], ref.at[d], d, d) for d in (2, 6, 1, 7)}
        relayed = {
            2: {
                3: copy(ref.at[2], ref.at[3], 1, 3),
                4: copy(ref.at[2, lower], ref.at[4, lower], 2, 4),
            },
            6: {
                5: copy(ref.at[6], ref.at[5], 7, 5),
                0: copy(ref.at[6, upper], ref.at[4, upper], 6, 0),
            },
        }
        return direct, relayed

    kv_direct, kv_relayed = line_copies(kv_all, kv_ssem, kv_rsem, key_peer)
    q_direct, q_relayed = line_copies(q_all, q_ssem, q_rsem, query_peer)
    lines = ((kv_direct, kv_relayed), (q_direct, q_relayed))
    for copy in kv_direct.values():
        copy.start()
    own_queries = jnp.concatenate([piece[rows:] for piece in pieces], axis=0)
    q_all[0] = (
        own_queries[:half_block] + pltpu.roll(own_queries[half_block:], HEAD_DIM, 1)
    ).astype(BF16)
    for copy in q_direct.values():
        copy.start()
    for direct, relayed in lines[::-1]:
        for d, onward in relayed.items():
            direct[d].wait_recv()
            for copy in onward.values():
                copy.start()
    slots = [0] + near
    near_slots = slots[: near_wide.shape[0] // block]
    far_slots = slots[len(near_slots) :]

    def wait_for(line, wanted):
        direct, relayed = line
        for d, copy in direct.items():
            if d in wanted and d not in relayed:
                copy.wait_recv()
        for onward in relayed.values():
            for d, copy in onward.items():
                if (d or 4) in wanted:
                    copy.wait_recv()

    def lay_out(wanted, wide, keys):
        for i in range(0, len(wanted), 2):
            few = wanted[i : i + 2]
            both = jnp.concatenate([kv_all[d] for d in few], axis=0)
            at = slice(i * block, (i + len(few)) * block)
            both = both.astype(F32)
            keys[:, at] = both.T.astype(BF16)
            lane = lax.broadcasted_iota(jnp.int32, both.shape, 1)
            wide[at] = jnp.where(lane < HEAD_DIM, 1.0, both).astype(BF16)

    half_lane = lax.broadcasted_iota(jnp.int32, (half_block, LANES), 1)
    block_lane = lax.broadcasted_iota(jnp.int32, (block, LANES), 1)

    def unfolded(d):
        packed = q_all[d].astype(F32)
        return jnp.concatenate(
            [
                jnp.where(half_lane < HEAD_DIM, packed, 0.0),
                jnp.where(half_lane < HEAD_DIM, pltpu.roll(packed, HEAD_DIM, 1), 0.0),
            ],
            axis=0,
        ).astype(BF16)

    def soften(scores, weights, tops, floor=None):
        for begin in range(0, 2 * block, CHUNK):
            at = slice(begin, begin + CHUNK)
            score = scores[at]
            top = jnp.max(score, axis=1, keepdims=True)
            if floor is not None:
                top = jnp.maximum(top, floor[at, :1])
            weights[at] = jnp.exp2(score - top).astype(BF16)
            tops[at] = jnp.broadcast_to(top, (CHUNK, LANES))

    def finish(d, mixed, top):
        total = jnp.where(block_lane < HEAD_DIM, mixed, pltpu.roll(mixed, HEAD_DIM, 1))
        level = top + jnp.log2(total)
        place = lax.broadcasted_iota(jnp.int32, (HALO, LANES), 0)
        levels = jnp.zeros((HALO, LANES), F32)
        for i in range(level_rows):
            few = level[i * LANES : (i + 1) * LANES]
            row = lax.broadcasted_iota(jnp.int32, few.shape, 0)
            column = lax.broadcasted_iota(jnp.int32, few.shape, 1)
            line = jnp.sum(jnp.where(row == column, few, 0.0), axis=0, keepdims=True)
            high = line.astype(BF16).astype(F32)
            levels = jnp.where(place == i, high, levels)
            levels = jnp.where(place == level_rows + i, line - high, levels)
        part_send[d] = jnp.concatenate(
            [folded(mixed / total), levels], axis=0
        ).astype(BF16)

    def chosen(step, order):
        return sum((step == i).astype(jnp.int32) * d for i, d in enumerate(order))

    steps = side // 2
    early_steps = len(near_slots) // 2

    def pair_of(step):
        return chosen(2 * step, slots), chosen(2 * step + 1, slots)

    for line in lines:
        wait_for(line, near_slots)
    lay_out(near_slots, near_wide, near_keys)

    @pl.loop(0, steps)
    def _(step):
        @pl.when(step == early_steps)
        def _():
            wait_for(lines[1], far_slots)

        first, second = pair_of(step)
        query = jnp.concatenate([unfolded(first), unfolded(second)], axis=0)
        near_scores[...] = matmul(query, near_keys[...])
        soften(near_scores, near_weights, first_tops.at[step])
        first_mixed[step] = matmul(near_weights[...], near_wide[...])

    wait_for(lines[0], far_slots)
    lay_out(far_slots, far_wide, far_keys)

    def part_copy(d):
        return pltpu.make_async_remote_copy(
            src_ref=part_send.at[d],
            dst_ref=part_recv.at[d],
            send_sem=part_ssem.at[d],
            recv_sem=part_rsem.at[d],
            device_id=query_peer(side - d),
            device_id_type=MESH,
        )

    pairs = [tuple(slots[2 * step : 2 * step + 2]) for step in range(steps)]

    def score_far(step):
        query = jnp.concatenate([unfolded(d) for d in pairs[step]], axis=0)
        far_scores[step] = matmul(query, far_keys[...])

    score_far(steps - 1)
    for step in range(steps - 1, -1, -1):
        if step > 0:
            score_far(step - 1)
        soften(far_scores.at[step], far_weights.at[step], far_tops.at[step], first_tops.at[step])
        top = far_tops[step]
        mixed = first_mixed[step] * jnp.exp2(first_tops[step] - top)
        mixed = mixed + matmul(far_weights[step], far_wide[...])
        for i in (1, 0):
            d = pairs[step][i]
            at = slice(i * block, (i + 1) * block)
            finish(d, mixed[at], top[at])
            if d > 0:
                part_copy(d).start()

    part_recv[0] = part_send[0]
    for d in range(1, side):
        part_copy(d).wait_recv()

    levels = []
    for i in range(level_rows):
        levels.append(
            [
                part_recv[d, half_block + i : half_block + i + 1].astype(F32)
                + part_recv[d, half_block + level_rows + i : half_block + level_rows + i + 1].astype(F32)
                for d in range(side)
            ]
        )
    shares = []
    for level in levels:
        level = jnp.concatenate(level, axis=0)
        fade = jnp.exp2(level - jnp.max(level, axis=0, keepdims=True))
        shares.append(fade / jnp.sum(fade, axis=0, keepdims=True))
    shares = jnp.concatenate(
        shares + [jnp.zeros((LANES - side * level_rows, LANES), F32)], axis=0
    ).T
    upper = []
    begin = half_block
    while begin < block:
        i = begin // LANES
        end = min(block, (i + 1) * LANES)
        few = shares[begin - i * LANES : end - i * LANES]
        upper.append(pltpu.roll(few, LANES - i * side, 1) if i else few)
        begin = end
    lower = shares[:half_block]
    upper = jnp.concatenate(upper, axis=0)
    pick = jnp.zeros((half_block, LANES), F32)
    for i, share in enumerate((lower, upper)):
        high = share.astype(BF16).astype(F32)
        for j, piece in enumerate((high, share - high)):
            begin = (2 * i + j) * side
            piece = pltpu.roll(piece, begin, 1) if begin else piece
            pick = jnp.where((half_lane >= begin) & (half_lane < begin + side), piece, pick)
    index = lax.broadcasted_iota(jnp.int32, (LANES, side * LANES), 0)
    lane = lax.broadcasted_iota(jnp.int32, (LANES, side * LANES), 1)
    spread = (
        (index % side == lane // LANES)
        & (index < 4 * side)
        & (index // (2 * side) == lane % LANES // HEAD_DIM)
    )
    spread = matmul(pick.astype(BF16), jnp.where(spread, 1.0, 0.0).astype(BF16))
    merged = jnp.zeros((half_block, LANES), F32)
    for d in range(side):
        part = part_recv[d].astype(F32)[:half_block]
        merged = merged + spread[:, d * LANES : (d + 1) * LANES] * part
    merged = jnp.concatenate([pltpu.roll(merged, HEAD_DIM, 1), merged], axis=0)

    edge_send[0] = folded(merged[: 2 * HALO]).astype(BF16)
    edge_send[1] = folded(merged[block - 2 * HALO :]).astype(BF16)
    framed = jnp.concatenate(
        [jnp.zeros((HALO, LANES), F32), merged, jnp.zeros((WINDOW - rows - HALO, LANES), F32)],
        axis=0,
    )
    for part in range(groups):
        ctx_send[part] = folded(framed[part * rows : part * rows + WINDOW]).astype(BF16)

    def edge_copy(i, head):
        return pltpu.make_async_remote_copy(
            src_ref=edge_send.at[i],
            dst_ref=edge_recv.at[head],
            send_sem=edge_ssem.at[i],
            recv_sem=edge_rsem.at[head],
            device_id=((earlier, groups - 1), (later, 0))[i],
            device_id_type=MESH,
        )

    for i in range(2):
        edge_copy(i, kv).start()
    ctx_copies = [
        pltpu.make_async_remote_copy(
            src_ref=ctx_send.at[(kv + d) & (groups - 1)],
            dst_ref=ctx_recv.at[kv],
            send_sem=ctx_ssem.at[d],
            recv_sem=ctx_rsem.at[d],
            device_id=kv_peer(d),
            device_id_type=MESH,
        )
        for d in far_first
    ]
    for copy in ctx_copies:
        copy.start()
    halo_copies = [
        pltpu.make_async_remote_copy(
            src_ref=halo_send.at[i],
            dst_ref=halo_recv.at[i],
            send_sem=halo_ssem.at[i],
            recv_sem=halo_rsem.at[i],
            device_id=target,
            device_id_type=MESH,
        )
        for i, target in enumerate((preceding, following))
    ]
    for copy in halo_copies:
        copy.start()
    ctx_recv[kv] = ctx_send[kv]
    for copy in head_copies:
        copy.wait_send()
    for direct, relayed in lines:
        for copy in direct.values():
            copy.wait_send()
        for onward in relayed.values():
            for copy in onward.values():
                copy.wait_send()
    for d in range(1, side):
        part_copy(d).wait_send()
    for copy in ctx_copies + halo_copies:
        copy.wait_send()
    for i in range(2):
        edge_copy(i, kv).wait_send()
    for load in loads[5:]:
        load.wait()
    for copy in halo_copies:
        copy.wait_recv()
    extent = rows + 2 * HALO
    nearby = jnp.concatenate([halo_recv[1].astype(F32), inputs, halo_recv[0].astype(F32)], axis=0)
    for copy in ctx_copies:
        copy.wait_recv()
    context[...] = all_heads(ctx_recv)[:extent]

    @pl.when(kv == 0)
    def _():
        for head in range(groups):
            edge_copy(1, head).wait_recv()
        context[:HALO] = all_heads(edge_recv)[HALO:]

    @pl.when(kv == groups - 1)
    def _():
        for head in range(groups):
            edge_copy(0, head).wait_recv()
        context[extent - HALO :] = all_heads(edge_recv)[:HALO]

    attended = matmul(context[...].astype(BF16), w_out[...]).astype(BF16).astype(F32)
    attended_ref[...] = attended[HALO : HALO + rows].astype(BF16)
    mid = nearby + attended
    conv_in = layer_norm(mid, gains_ref[1:2]).astype(BF16)
    expanded = matmul(conv_in, w_expand[...])
    gate = expanded[:, width:]
    glu = (expanded[:, :width] / (1.0 + jnp.exp(-gate))).astype(BF16).astype(F32)
    times = me * rows - HALO + lax.broadcasted_iota(jnp.int32, (extent, width), 0)
    padded[...] = jnp.where((times >= 0) & (times < devices * rows), glu, 0.0)

    depth = jnp.zeros((rows, width), F32)
    count = taps_ref.shape[0]
    for turn in range(8):
        shifted = None
        for tap in range(turn - 1, count, 8):
            if tap < 0:
                continue
            term = taps_ref[tap : tap + 1] * padded[tap + 1 - turn : tap + 9 - turn + rows]
            shifted = term if shifted is None else shifted + term
        depth = depth + shifted[turn : turn + rows]
    batch = depth * gains_ref[2:3] + gains_ref[3:4]
    act = (batch / (1.0 + jnp.exp(-batch))).astype(BF16)
    layer_ref[...] = (mid[HALO : HALO + rows] + matmul(act, w_project[...])).astype(BF16)


def copy_kernel(attended_in, layer_in, attended_out, layer_out, sem):
    copies = [
        pltpu.make_async_copy(attended_in, attended_out, sem.at[0]),
        pltpu.make_async_copy(layer_in, layer_out, sem.at[1]),
    ]
    for copy in copies:
        copy.start()
    for copy in copies:
        copy.wait()


def on_device(
    frames,
    attn_gain,
    w_query,
    w_key,
    w_value,
    w_out,
    conv_gain,
    w_expand,
    kernel,
    bn_scale,
    bn_shift,
    w_project,
):
    rows, width = frames.shape
    groups = lax.axis_size("kv")
    side = math.isqrt(lax.axis_size("tm"))
    block = rows * groups
    near_rows = (5 if side == 8 else side // 2) * block
    far_rows = side * block - near_rows
    vmem = pl.BlockSpec(memory_space=pltpu.VMEM)
    anywhere = pl.BlockSpec(memory_space=pl.ANY)
    dma = pltpu.SemaphoreType.DMA
    results = pl.pallas_call(
        functools.partial(layer_kernel, side),
        out_shape=(pltpu.VMEM((rows, width), BF16), pltpu.VMEM((rows, width), BF16)),
        in_specs=[anywhere] * 12,
        out_specs=(vmem, vmem),
        scratch_shapes=[
            pltpu.VMEM((rows, width), BF16),
            pltpu.VMEM((4, width), F32),
            pltpu.VMEM(kernel.shape, F32),
            pltpu.VMEM((width, width), BF16),
            pltpu.VMEM((width, width), BF16),
            pltpu.VMEM((width, width), BF16),
            pltpu.VMEM((width, width), BF16),
            pltpu.VMEM((width, 2 * width), BF16),
            pltpu.VMEM((width, width), BF16),
            pltpu.VMEM((groups, 2 * rows, LANES), BF16),
            pltpu.VMEM((groups, 2 * rows, LANES), BF16),
            pltpu.VMEM((side, block, LANES), BF16),
            pltpu.VMEM((near_rows, LANES), BF16),
            pltpu.VMEM((far_rows, LANES), BF16),
            pltpu.VMEM((LANES, near_rows), BF16),
            pltpu.VMEM((LANES, far_rows), BF16),
            pltpu.VMEM((side, block // 2, LANES), BF16),
            pltpu.VMEM((2 * block, near_rows), F32),
            pltpu.VMEM((side // 2, 2 * block, far_rows), F32),
            pltpu.VMEM((2 * block, near_rows), BF16),
            pltpu.VMEM((side // 2, 2 * block, far_rows), BF16),
            pltpu.VMEM((side // 2, 2 * block, LANES), F32),
            pltpu.VMEM((side // 2, 2 * block, LANES), F32),
            pltpu.VMEM((side // 2, 2 * block, LANES), F32),
            pltpu.VMEM((side, block // 2 + HALO, LANES), BF16),
            pltpu.VMEM((side, block // 2 + HALO, LANES), BF16),
            pltpu.VMEM((groups, WINDOW // 2, LANES), BF16),
            pltpu.VMEM((groups, WINDOW // 2, LANES), BF16),
            pltpu.VMEM((2, HALO, LANES), BF16),
            pltpu.VMEM((groups, HALO, LANES), BF16),
            pltpu.VMEM((rows + 2 * HALO, width), F32),
            pltpu.VMEM((2, HALO, width), BF16),
            pltpu.VMEM((2, HALO, width), BF16),
            pltpu.VMEM((rows + 2 * HALO, width), F32),
            dma((12,)),
            dma((groups,)),
            dma((groups,)),
            dma((side,)),
            dma((side,)),
            dma((side,)),
            dma((side,)),
            dma((side,)),
            dma((side,)),
            dma((groups,)),
            dma((groups,)),
            dma((2,)),
            dma((groups,)),
            dma((2,)),
            dma((2,)),
        ],
        compiler_params=pltpu.CompilerParams(
            collective_id=0, has_side_effects=True, vmem_limit_bytes=60 * 1024 * 1024
        ),
    )(
        frames,
        attn_gain.reshape(1, width),
        conv_gain.reshape(1, width),
        bn_scale.reshape(1, width),
        bn_shift.reshape(1, width),
        kernel,
        w_query,
        w_key,
        w_value,
        w_out,
        w_expand,
        w_project,
    )
    return pl.pallas_call(
        copy_kernel,
        out_shape=(jax.ShapeDtypeStruct((rows, width), BF16),) * 2,
        in_specs=[vmem] * 2,
        out_specs=(anywhere, anywhere),
        scratch_shapes=[dma((2,))],
        compiler_params=pltpu.CompilerParams(vmem_limit_bytes=4 * 1024 * 1024),
    )(*results)


def solution(mesh):
    rows = P(("tm", "kv"), None)
    return jax.shard_map(
        on_device,
        mesh=mesh,
        in_specs=(rows,) + (P(),) * 11,
        out_specs=(rows, rows),
        check_vma=False,
    )
```

```python
import functools
import math

import jax
import jax.numpy as jnp
from jax import lax
from jax.experimental import pallas as pl
from jax.experimental.pallas import tpu as pltpu
from jax.sharding import PartitionSpec as P

HEAD_DIM = 64
HALF = HEAD_DIM // 2
LANES = 128
HALO = 16
WINDOW = 64
CHUNK = 32
MESH = pl.DeviceIdType.MESH
BF16 = jnp.bfloat16
F32 = jnp.float32


def layer_norm(values, gain):
    mean = jnp.mean(values, axis=-1, keepdims=True)
    centered = values - mean
    var = jnp.mean(centered * centered, axis=-1, keepdims=True)
    return centered / jnp.sqrt(var + 1e-05) * gain


def matmul(a, b):
    return jnp.dot(a, b, preferred_element_type=F32)


def folded(rows):
    half = rows.shape[0] // 2
    lane = lax.broadcasted_iota(jnp.int32, (half, LANES), 1)
    return jnp.where(lane < HEAD_DIM, pltpu.roll(rows[:half], HEAD_DIM, 1), rows[half:])


def all_heads(ref):
    columns = []
    lane = lax.broadcasted_iota(jnp.int32, ref.shape[1:], 1)
    for pair in range(ref.shape[0] // 2):
        even = ref[2 * pair].astype(F32)
        odd = ref[2 * pair + 1].astype(F32)
        top = jnp.where(lane < HEAD_DIM, even, pltpu.roll(odd, HEAD_DIM, 1))
        bottom = jnp.where(lane < HEAD_DIM, pltpu.roll(even, HEAD_DIM, 1), odd)
        columns.append(jnp.concatenate([top, bottom], axis=0))
    return jnp.concatenate(columns, axis=1)


def layer_kernel(
    side,
    frames_hbm,
    attn_gain_hbm,
    conv_gain_hbm,
    scale_hbm,
    shift_hbm,
    taps_hbm,
    w_query_hbm,
    w_key_hbm,
    w_value_hbm,
    w_out_hbm,
    w_expand_hbm,
    w_project_hbm,
    attended_ref,
    layer_ref,
    frames_ref,
    gains_ref,
    taps_ref,
    w_query,
    w_key,
    w_value,
    w_out,
    w_expand,
    w_project,
    head_send,
    head_recv,
    kv_all,
    near_wide,
    far_wide,
    near_keys,
    far_keys,
    q_all,
    near_scores,
    far_scores,
    near_weights,
    far_weights,
    far_tops,
    first_mixed,
    first_tops,
    part_send,
    part_recv,
    ctx_send,
    ctx_recv,
    edge_send,
    edge_recv,
    context,
    halo_send,
    halo_recv,
    padded,
    load_sem,
    head_ssem,
    head_rsem,
    kv_ssem,
    kv_rsem,
    q_ssem,
    q_rsem,
    part_ssem,
    part_rsem,
    ctx_ssem,
    ctx_rsem,
    edge_ssem,
    edge_rsem,
    halo_ssem,
    halo_rsem,
):
    rows, width = frames_ref.shape
    groups = head_send.shape[0]
    block = rows * groups
    half_block = block // 2
    level_rows = -(-block // LANES)
    blocks = side * side
    tm = lax.axis_index("tm")
    kv = lax.axis_index("kv")
    bits = side.bit_length() - 1
    core = kv & 1
    slow = tm >> bits
    fast = tm & (side - 1)
    key_at = fast + core * (slow - fast)
    key_stride = 1 + core * (side - 1)
    query_at = slow + core * (fast - slow)
    query_stride = side - core * (side - 1)

    def kv_peer(d):
        return (tm, (kv + d) & (groups - 1))

    def key_peer(d):
        return (tm + (((key_at + d) & (side - 1)) - key_at) * key_stride, kv)

    def query_peer(d):
        return (tm + (((query_at + d) & (side - 1)) - query_at) * query_stride, kv)

    devices = groups * blocks
    me = tm * groups + kv
    following = (me + 1) & (devices - 1)
    preceding = (me - 1) & (devices - 1)
    group_bits = groups.bit_length() - 1
    following = (following >> group_bits, following & (groups - 1))
    preceding = (preceding >> group_bits, preceding & (groups - 1))
    later = (tm + 1) & (blocks - 1)
    earlier = (tm - 1) & (blocks - 1)
    far_first = sorted(range(1, groups), key=lambda d: -min(d, groups - d))
    near = sorted(range(1, side), key=lambda d: min(d, side - d))

    def greet(device):
        pl.semaphore_signal(barrier, inc=1, device_id=device, device_id_type=MESH)

    loads = [
        pltpu.make_async_copy(source, target, load_sem.at[i])
        for i, (source, target) in enumerate(
            (
                (frames_hbm, frames_ref),
                (attn_gain_hbm, gains_ref.at[0:1]),
                (w_key_hbm, w_key),
                (w_value_hbm, w_value),
                (w_query_hbm, w_query),
                (w_out_hbm, w_out),
                (w_expand_hbm, w_expand),
                (taps_hbm, taps_ref),
                (conv_gain_hbm, gains_ref.at[1:2]),
                (scale_hbm, gains_ref.at[2:3]),
                (shift_hbm, gains_ref.at[3:4]),
                (w_project_hbm, w_project),
            )
        )
    ]
    for load in loads[:5]:
        load.start()

    barrier = pltpu.get_barrier_semaphore()
    for d in range(1, groups):
        greet(kv_peer(d))
    for d in near[:4]:
        greet(key_peer(d))
        greet(query_peer(d))

    lane = lax.broadcasted_iota(jnp.int32, (rows, LANES), 1)
    low = lane < HEAD_DIM
    first_half = lane % HEAD_DIM < HALF
    which = lax.broadcasted_iota(jnp.int32, (1, LANES), 1) % HALF
    inverse = jnp.zeros((1, LANES), F32)
    for i in range(HALF):
        inverse = jnp.where(which == i, 10000.0 ** (-2.0 * i / HEAD_DIM), inverse)
    positions = me * rows + lax.broadcasted_iota(jnp.int32, (rows, LANES), 0)
    angle = positions.astype(F32) * inverse
    cosine = jnp.cos(angle)
    sine = jnp.sin(angle)
    sine = jnp.where(first_half, -sine, sine)

    def rotated(part):
        swapped = jnp.where(
            first_half, pltpu.roll(part, LANES - HALF, 1), pltpu.roll(part, HALF, 1)
        )
        return part * cosine + swapped * sine

    loads[0].wait()
    loads[1].wait()
    inputs = frames_ref[...].astype(F32)
    halo_send[0] = inputs[:HALO].astype(BF16)
    halo_send[1] = inputs[rows - HALO :].astype(BF16)
    normed = layer_norm(inputs, gains_ref[0:1]).astype(BF16)
    loads[2].wait()
    keys = matmul(normed, w_key[...])
    loads[3].wait()
    values = matmul(normed, w_value[...])
    loads[4].wait()
    queries = matmul(normed, w_query[...])
    to_log2 = 0.125 / math.log(2.0)
    for pair in range(groups // 2):
        at = slice(pair * LANES, (pair + 1) * LANES)
        key = rotated(keys[:, at])
        query = rotated(queries[:, at]) * to_log2
        value = values[:, at]
        key_value = jnp.where(low, key, pltpu.roll(value, HEAD_DIM, 1))
        head_send[2 * pair] = jnp.concatenate(
            [key_value, jnp.where(low, query, 0.0)], axis=0
        ).astype(BF16)
        key_value = jnp.where(low, pltpu.roll(key, HEAD_DIM, 1), value)
        head_send[2 * pair + 1] = jnp.concatenate(
            [key_value, jnp.where(low, pltpu.roll(query, HEAD_DIM, 1), 0.0)], axis=0
        ).astype(BF16)

    pl.semaphore_wait(barrier, groups - 1 + 2 * len(near[:4]))

    head_copies = [
        pltpu.make_async_remote_copy(
            src_ref=head_send.at[(kv + d) & (groups - 1)],
            dst_ref=head_recv.at[kv],
            send_sem=head_ssem.at[d],
            recv_sem=head_rsem.at[d],
            device_id=kv_peer(d),
            device_id_type=MESH,
        )
        for d in far_first
    ]
    for copy in head_copies:
        copy.start()
    for load in loads[5:]:
        load.start()
    head_recv[kv] = head_send[kv]
    for copy in head_copies:
        copy.wait_recv()
    pieces = [head_recv[head].astype(F32) for head in range(groups)]
    own_block = jnp.concatenate([piece[:rows] for piece in pieces], axis=0).astype(BF16)
    kv_all[0] = own_block

    def line_copies(ref, ssem, rsem, peer, halved):
        half = ref.shape[1] // 2
        lower, upper, whole = pl.ds(0, half), pl.ds(half, half), pl.ds(0, 2 * half)
        used = []

        def copy(source, target, rows, place):
            sem = len(used)
            used.append(sem)
            return pltpu.make_async_remote_copy(
                src_ref=ref.at[source, rows],
                dst_ref=ref.at[target, rows],
                send_sem=ssem.at[sem],
                recv_sem=rsem.at[sem],
                device_id=peer(place),
                device_id_type=MESH,
            )

        def entry(place, rows, onward=()):
            return place, copy(0, place, rows, place), [
                (target, copy(place, target, rows, step)) for target, rows, step in onward
            ]

        if side < 8:
            return [entry(d, whole) for d in near]
        if halved:
            return [
                entry(2, lower, [(4, lower, 2), (3, lower, 1)]),
                entry(6, upper, [(4, upper, 6), (5, upper, 7)]),
                entry(2, upper, [(3, upper, 1)]),
                entry(6, lower, [(5, lower, 7)]),
                entry(1, whole),
                entry(7, whole),
            ]
        return [
            entry(2, whole, [(4, lower, 2), (3, whole, 1)]),
            entry(6, whole, [(4, upper, 6), (5, whole, 7)]),
            entry(1, whole),
            entry(7, whole),
        ]

    kv_line = line_copies(kv_all, kv_ssem, kv_rsem, key_peer, True)
    q_line = line_copies(q_all, q_ssem, q_rsem, query_peer, False)
    for _, copy, _ in kv_line:
        copy.start()
    own_queries = jnp.concatenate([piece[rows:] for piece in pieces], axis=0)
    q_all[0] = (
        own_queries[:half_block] + pltpu.roll(own_queries[half_block:], HEAD_DIM, 1)
    ).astype(BF16)
    for _, copy, _ in q_line:
        copy.start()
    for line in (q_line, kv_line):
        for _, copy, onward in line:
            if onward:
                copy.wait_recv()
            for _, relay in onward:
                relay.start()

    slots = [0] + near
    near_count = near_wide.shape[0] // block

    def wait_for(line, wanted):
        for slot, copy, onward in line:
            if slot in wanted and not onward:
                copy.wait_recv()
            for target, relay in onward:
                if target in wanted:
                    relay.wait_recv()

    def lay_out(few, at, wide, keys):
        both = jnp.concatenate([kv_all[d] for d in few], axis=0).astype(F32)
        at = slice(at * block, (at + len(few)) * block)
        keys[:, at] = both.T.astype(BF16)
        lane = lax.broadcasted_iota(jnp.int32, both.shape, 1)
        wide[at] = jnp.where(lane < HEAD_DIM, 1.0, both).astype(BF16)

    def lay_out_line(kv_slots, wide, keys):
        for i in range(0, len(kv_slots), 2):
            wait_for(kv_line, kv_slots[i : i + 2])
            lay_out(kv_slots[i : i + 2], i, wide, keys)

    half_lane = lax.broadcasted_iota(jnp.int32, (half_block, LANES), 1)
    block_lane = lax.broadcasted_iota(jnp.int32, (block, LANES), 1)

    def unfolded(d):
        packed = q_all[d].astype(F32)
        return jnp.concatenate(
            [
                jnp.where(half_lane < HEAD_DIM, packed, 0.0),
                jnp.where(half_lane < HEAD_DIM, pltpu.roll(packed, HEAD_DIM, 1), 0.0),
            ],
            axis=0,
        ).astype(BF16)

    def soften(scores, weights, tops, floor=None):
        for begin in range(0, 2 * block, CHUNK):
            at = slice(begin, begin + CHUNK)
            score = scores[at]
            top = jnp.max(score, axis=1, keepdims=True)
            if floor is not None:
                top = jnp.maximum(top, floor[at, :1])
            weights[at] = jnp.exp2(score - top).astype(BF16)
            tops[at] = jnp.broadcast_to(top, (CHUNK, LANES))

    def finish(d, mixed, top):
        total = jnp.where(block_lane < HEAD_DIM, mixed, pltpu.roll(mixed, HEAD_DIM, 1))
        level = top + jnp.log2(total)
        place = lax.broadcasted_iota(jnp.int32, (HALO, LANES), 0)
        levels = jnp.zeros((HALO, LANES), F32)
        for i in range(level_rows):
            few = level[i * LANES : (i + 1) * LANES]
            row = lax.broadcasted_iota(jnp.int32, few.shape, 0)
            column = lax.broadcasted_iota(jnp.int32, few.shape, 1)
            line = jnp.sum(jnp.where(row == column, few, 0.0), axis=0, keepdims=True)
            high = line.astype(BF16).astype(F32)
            levels = jnp.where(place == i, high, levels)
            levels = jnp.where(place == level_rows + i, line - high, levels)
        part_send[d] = jnp.concatenate(
            [folded(mixed / total), levels], axis=0
        ).astype(BF16)

    def chosen(step, order):
        return sum((step == i).astype(jnp.int32) * d for i, d in enumerate(order))

    steps = side // 2
    pairs = [tuple(slots[2 * step : 2 * step + 2]) for step in range(steps)]
    near_order = [2, 6, 1, 7, 0] if side == 8 else slots[:near_count]
    far_order = slots[near_count:]
    wait_for(q_line, slots[:near_count])
    lay_out_line(near_order, near_wide, near_keys)

    @pl.loop(0, max(steps // 2, 1))
    def _(turn):
        @pl.when(turn == steps // 4)
        def _():
            wait_for(q_line, far_order)

        ahead = min(2, steps)
        for i in range(ahead):
            step = ahead * turn + i
            query = [unfolded(chosen(2 * step + j, slots)) for j in range(2)]
            near_scores[i] = matmul(jnp.concatenate(query, axis=0), near_keys[...])
        for i in range(ahead):
            step = ahead * turn + i
            soften(near_scores.at[i], near_weights.at[i], first_tops.at[step])
            first_mixed[step] = matmul(near_weights[i], near_wide[...])

    lay_out_line(far_order, far_wide, far_keys)

    def part_copy(d):
        return pltpu.make_async_remote_copy(
            src_ref=part_send.at[d],
            dst_ref=part_recv.at[d],
            send_sem=part_ssem.at[d],
            recv_sem=part_rsem.at[d],
            device_id=query_peer(side - d),
            device_id_type=MESH,
        )

    def score_far(step):
        query = jnp.concatenate([unfolded(d) for d in pairs[step]], axis=0)
        far_scores[step] = matmul(query, far_keys[...])

    score_far(steps - 1)
    for step in range(steps - 1, -1, -1):
        if step > 0:
            score_far(step - 1)
        soften(far_scores.at[step], far_weights.at[step], far_tops.at[step], first_tops.at[step])
        top = far_tops[step]
        mixed = first_mixed[step] * jnp.exp2(first_tops[step] - top)
        mixed = mixed + matmul(far_weights[step], far_wide[...])
        for i in (1, 0):
            d = pairs[step][i]
            at = slice(i * block, (i + 1) * block)
            finish(d, mixed[at], top[at])
            if d > 0:
                part_copy(d).start()

    part_recv[0] = part_send[0]
    for d in range(1, side):
        part_copy(d).wait_recv()

    levels = []
    for i in range(level_rows):
        levels.append(
            [
                part_recv[d, half_block + i : half_block + i + 1].astype(F32)
                + part_recv[d, half_block + level_rows + i : half_block + level_rows + i + 1].astype(F32)
                for d in range(side)
            ]
        )
    shares = []
    for level in levels:
        level = jnp.concatenate(level, axis=0)
        fade = jnp.exp2(level - jnp.max(level, axis=0, keepdims=True))
        shares.append(fade / jnp.sum(fade, axis=0, keepdims=True))
    shares = jnp.concatenate(
        shares + [jnp.zeros((LANES - side * level_rows, LANES), F32)], axis=0
    ).T
    upper = []
    begin = half_block
    while begin < block:
        i = begin // LANES
        end = min(block, (i + 1) * LANES)
        few = shares[begin - i * LANES : end - i * LANES]
        upper.append(pltpu.roll(few, LANES - i * side, 1) if i else few)
        begin = end
    lower = shares[:half_block]
    upper = jnp.concatenate(upper, axis=0)
    pick = jnp.zeros((half_block, LANES), F32)
    for i, share in enumerate((lower, upper)):
        high = share.astype(BF16).astype(F32)
        for j, piece in enumerate((high, share - high)):
            begin = (2 * i + j) * side
            piece = pltpu.roll(piece, begin, 1) if begin else piece
            pick = jnp.where((half_lane >= begin) & (half_lane < begin + side), piece, pick)
    index = lax.broadcasted_iota(jnp.int32, (LANES, side * LANES), 0)
    lane = lax.broadcasted_iota(jnp.int32, (LANES, side * LANES), 1)
    spread = (
        (index % side == lane // LANES)
        & (index < 4 * side)
        & (index // (2 * side) == lane % LANES // HEAD_DIM)
    )
    spread = matmul(pick.astype(BF16), jnp.where(spread, 1.0, 0.0).astype(BF16))
    merged = jnp.zeros((half_block, LANES), F32)
    for d in range(side):
        part = part_recv[d].astype(F32)[:half_block]
        merged = merged + spread[:, d * LANES : (d + 1) * LANES] * part
    merged = jnp.concatenate([pltpu.roll(merged, HEAD_DIM, 1), merged], axis=0)

    edge_send[0] = folded(merged[: 2 * HALO]).astype(BF16)
    edge_send[1] = folded(merged[block - 2 * HALO :]).astype(BF16)
    framed = jnp.concatenate(
        [jnp.zeros((HALO, LANES), F32), merged, jnp.zeros((WINDOW - rows - HALO, LANES), F32)],
        axis=0,
    )
    for part in range(groups):
        ctx_send[part] = folded(framed[part * rows : part * rows + WINDOW]).astype(BF16)

    def edge_copy(i, head):
        return pltpu.make_async_remote_copy(
            src_ref=edge_send.at[i],
            dst_ref=edge_recv.at[head],
            send_sem=edge_ssem.at[i],
            recv_sem=edge_rsem.at[head],
            device_id=((earlier, groups - 1), (later, 0))[i],
            device_id_type=MESH,
        )

    for i in range(2):
        edge_copy(i, kv).start()
    ctx_copies = [
        pltpu.make_async_remote_copy(
            src_ref=ctx_send.at[(kv + d) & (groups - 1)],
            dst_ref=ctx_recv.at[kv],
            send_sem=ctx_ssem.at[d],
            recv_sem=ctx_rsem.at[d],
            device_id=kv_peer(d),
            device_id_type=MESH,
        )
        for d in far_first
    ]
    for copy in ctx_copies:
        copy.start()
    halo_copies = [
        pltpu.make_async_remote_copy(
            src_ref=halo_send.at[i],
            dst_ref=halo_recv.at[i],
            send_sem=halo_ssem.at[i],
            recv_sem=halo_rsem.at[i],
            device_id=target,
            device_id_type=MESH,
        )
        for i, target in enumerate((preceding, following))
    ]
    for copy in halo_copies:
        copy.start()
    ctx_recv[kv] = ctx_send[kv]
    for copy in head_copies:
        copy.wait_send()
    for line in (kv_line, q_line):
        for _, copy, onward in line:
            copy.wait_send()
            for _, relay in onward:
                relay.wait_send()
    for d in range(1, side):
        part_copy(d).wait_send()
    for copy in ctx_copies + halo_copies:
        copy.wait_send()
    for i in range(2):
        edge_copy(i, kv).wait_send()
    for load in loads[5:]:
        load.wait()
    for copy in halo_copies:
        copy.wait_recv()
    extent = rows + 2 * HALO
    nearby = jnp.concatenate([halo_recv[1].astype(F32), inputs, halo_recv[0].astype(F32)], axis=0)
    for copy in ctx_copies:
        copy.wait_recv()
    context[...] = all_heads(ctx_recv)[:extent]

    @pl.when(kv == 0)
    def _():
        for head in range(groups):
            edge_copy(1, head).wait_recv()
        context[:HALO] = all_heads(edge_recv)[HALO:]

    @pl.when(kv == groups - 1)
    def _():
        for head in range(groups):
            edge_copy(0, head).wait_recv()
        context[extent - HALO :] = all_heads(edge_recv)[:HALO]

    attended = matmul(context[...].astype(BF16), w_out[...]).astype(BF16).astype(F32)
    attended_ref[...] = attended[HALO : HALO + rows].astype(BF16)
    mid = nearby + attended
    conv_in = layer_norm(mid, gains_ref[1:2]).astype(BF16)
    expanded = matmul(conv_in, w_expand[...])
    gate = expanded[:, width:]
    glu = (expanded[:, :width] / (1.0 + jnp.exp(-gate))).astype(BF16).astype(F32)
    times = me * rows - HALO + lax.broadcasted_iota(jnp.int32, (extent, width), 0)
    padded[...] = jnp.where((times >= 0) & (times < devices * rows), glu, 0.0)

    depth = jnp.zeros((rows, width), F32)
    count = taps_ref.shape[0]
    for turn in range(8):
        shifted = None
        for tap in range(turn - 1, count, 8):
            if tap < 0:
                continue
            term = taps_ref[tap : tap + 1] * padded[tap + 1 - turn : tap + 9 - turn + rows]
            shifted = term if shifted is None else shifted + term
        depth = depth + shifted[turn : turn + rows]
    batch = depth * gains_ref[2:3] + gains_ref[3:4]
    act = (batch / (1.0 + jnp.exp(-batch))).astype(BF16)
    layer_ref[...] = (mid[HALO : HALO + rows] + matmul(act, w_project[...])).astype(BF16)


def copy_kernel(attended_in, layer_in, attended_out, layer_out, sem):
    copies = [
        pltpu.make_async_copy(attended_in, attended_out, sem.at[0]),
        pltpu.make_async_copy(layer_in, layer_out, sem.at[1]),
    ]
    for copy in copies:
        copy.start()
    for copy in copies:
        copy.wait()


def on_device(
    frames,
    attn_gain,
    w_query,
    w_key,
    w_value,
    w_out,
    conv_gain,
    w_expand,
    kernel,
    bn_scale,
    bn_shift,
    w_project,
):
    rows, width = frames.shape
    groups = lax.axis_size("kv")
    side = math.isqrt(lax.axis_size("tm"))
    block = rows * groups
    near_rows = (5 if side == 8 else side // 2) * block
    far_rows = side * block - near_rows
    vmem = pl.BlockSpec(memory_space=pltpu.VMEM)
    anywhere = pl.BlockSpec(memory_space=pl.ANY)
    dma = pltpu.SemaphoreType.DMA
    results = pl.pallas_call(
        functools.partial(layer_kernel, side),
        out_shape=(pltpu.VMEM((rows, width), BF16), pltpu.VMEM((rows, width), BF16)),
        in_specs=[anywhere] * 12,
        out_specs=(vmem, vmem),
        scratch_shapes=[
            pltpu.VMEM((rows, width), BF16),
            pltpu.VMEM((4, width), F32),
            pltpu.VMEM(kernel.shape, F32),
            pltpu.VMEM((width, width), BF16),
            pltpu.VMEM((width, width), BF16),
            pltpu.VMEM((width, width), BF16),
            pltpu.VMEM((width, width), BF16),
            pltpu.VMEM((width, 2 * width), BF16),
            pltpu.VMEM((width, width), BF16),
            pltpu.VMEM((groups, 2 * rows, LANES), BF16),
            pltpu.VMEM((groups, 2 * rows, LANES), BF16),
            pltpu.VMEM((side, block, LANES), BF16),
            pltpu.VMEM((near_rows, LANES), BF16),
            pltpu.VMEM((far_rows, LANES), BF16),
            pltpu.VMEM((LANES, near_rows), BF16),
            pltpu.VMEM((LANES, far_rows), BF16),
            pltpu.VMEM((side, block // 2, LANES), BF16),
            pltpu.VMEM((2, 2 * block, near_rows), F32),
            pltpu.VMEM((side // 2, 2 * block, far_rows), F32),
            pltpu.VMEM((2, 2 * block, near_rows), BF16),
            pltpu.VMEM((side // 2, 2 * block, far_rows), BF16),
            pltpu.VMEM((side // 2, 2 * block, LANES), F32),
            pltpu.VMEM((side // 2, 2 * block, LANES), F32),
            pltpu.VMEM((side // 2, 2 * block, LANES), F32),
            pltpu.VMEM((side, block // 2 + HALO, LANES), BF16),
            pltpu.VMEM((side, block // 2 + HALO, LANES), BF16),
            pltpu.VMEM((groups, WINDOW // 2, LANES), BF16),
            pltpu.VMEM((groups, WINDOW // 2, LANES), BF16),
            pltpu.VMEM((2, HALO, LANES), BF16),
            pltpu.VMEM((groups, HALO, LANES), BF16),
            pltpu.VMEM((rows + 2 * HALO, width), F32),
            pltpu.VMEM((2, HALO, width), BF16),
            pltpu.VMEM((2, HALO, width), BF16),
            pltpu.VMEM((rows + 2 * HALO, width), F32),
            dma((12,)),
            dma((groups,)),
            dma((groups,)),
            dma((2 * side,)),
            dma((2 * side,)),
            dma((side,)),
            dma((side,)),
            dma((side,)),
            dma((side,)),
            dma((groups,)),
            dma((groups,)),
            dma((2,)),
            dma((groups,)),
            dma((2,)),
            dma((2,)),
        ],
        compiler_params=pltpu.CompilerParams(
            collective_id=0, has_side_effects=True, vmem_limit_bytes=60 * 1024 * 1024
        ),
    )(
        frames,
        attn_gain.reshape(1, width),
        conv_gain.reshape(1, width),
        bn_scale.reshape(1, width),
        bn_shift.reshape(1, width),
        kernel,
        w_query,
        w_key,
        w_value,
        w_out,
        w_expand,
        w_project,
    )
    return pl.pallas_call(
        copy_kernel,
        out_shape=(jax.ShapeDtypeStruct((rows, width), BF16),) * 2,
        in_specs=[vmem] * 2,
        out_specs=(anywhere, anywhere),
        scratch_shapes=[dma((2,))],
        compiler_params=pltpu.CompilerParams(vmem_limit_bytes=4 * 1024 * 1024),
    )(*results)


def solution(mesh):
    rows = P(("tm", "kv"), None)
    return jax.shard_map(
        on_device,
        mesh=mesh,
        in_specs=(rows,) + (P(),) * 11,
        out_specs=(rows, rows),
        check_vma=False,
    )
```

```python
import functools
import math

import jax
import jax.numpy as jnp
from jax import lax
from jax.experimental import pallas as pl
from jax.experimental.pallas import tpu as pltpu
from jax.sharding import PartitionSpec as P

HEAD_DIM = 64
HALF = HEAD_DIM // 2
LANES = 128
HALO = 16
WINDOW = 64
CHUNK = 32
MESH = pl.DeviceIdType.MESH
BF16 = jnp.bfloat16
F32 = jnp.float32


def layer_norm(values, gain):
    mean = jnp.mean(values, axis=-1, keepdims=True)
    centered = values - mean
    var = jnp.mean(centered * centered, axis=-1, keepdims=True)
    return centered / jnp.sqrt(var + 1e-05) * gain


def matmul(a, b):
    return jnp.dot(a, b, preferred_element_type=F32)


def folded(rows):
    half = rows.shape[0] // 2
    lane = lax.broadcasted_iota(jnp.int32, (half, LANES), 1)
    return jnp.where(lane < HEAD_DIM, pltpu.roll(rows[:half], HEAD_DIM, 1), rows[half:])


def all_heads(ref):
    columns = []
    lane = lax.broadcasted_iota(jnp.int32, ref.shape[1:], 1)
    for pair in range(ref.shape[0] // 2):
        even = ref[2 * pair].astype(F32)
        odd = ref[2 * pair + 1].astype(F32)
        top = jnp.where(lane < HEAD_DIM, even, pltpu.roll(odd, HEAD_DIM, 1))
        bottom = jnp.where(lane < HEAD_DIM, pltpu.roll(even, HEAD_DIM, 1), odd)
        columns.append(jnp.concatenate([top, bottom], axis=0))
    return jnp.concatenate(columns, axis=1)


def layer_kernel(
    side,
    frames_hbm,
    attn_gain_hbm,
    conv_gain_hbm,
    scale_hbm,
    shift_hbm,
    taps_hbm,
    w_query_hbm,
    w_key_hbm,
    w_value_hbm,
    w_out_hbm,
    w_expand_hbm,
    w_project_hbm,
    attended_ref,
    layer_ref,
    frames_ref,
    gains_ref,
    taps_ref,
    w_query,
    w_key,
    w_value,
    w_out,
    w_expand,
    w_project,
    head_send,
    head_recv,
    kv_all,
    near_wide,
    far_wide,
    near_keys,
    far_keys,
    q_all,
    near_scores,
    far_scores,
    near_weights,
    far_weights,
    far_tops,
    first_mixed,
    first_tops,
    part_send,
    part_recv,
    ctx_send,
    ctx_recv,
    edge_send,
    edge_recv,
    context,
    halo_send,
    halo_recv,
    padded,
    load_sem,
    head_ssem,
    head_rsem,
    kv_ssem,
    kv_rsem,
    q_ssem,
    q_rsem,
    part_ssem,
    part_rsem,
    ctx_ssem,
    ctx_rsem,
    edge_ssem,
    edge_rsem,
    halo_ssem,
    halo_rsem,
):
    rows, width = frames_ref.shape
    groups = head_send.shape[0]
    block = rows * groups
    half_block = block // 2
    level_rows = -(-block // LANES)
    blocks = side * side
    tm = lax.axis_index("tm")
    kv = lax.axis_index("kv")
    bits = side.bit_length() - 1
    core = kv & 1
    slow = tm >> bits
    fast = tm & (side - 1)
    key_at = fast + core * (slow - fast)
    key_stride = 1 + core * (side - 1)
    query_at = slow + core * (fast - slow)
    query_stride = side - core * (side - 1)

    def kv_peer(d):
        return (tm, (kv + d) & (groups - 1))

    def key_peer(d):
        return (tm + (((key_at + d) & (side - 1)) - key_at) * key_stride, kv)

    def query_peer(d):
        return (tm + (((query_at + d) & (side - 1)) - query_at) * query_stride, kv)

    devices = groups * blocks
    me = tm * groups + kv
    following = (me + 1) & (devices - 1)
    preceding = (me - 1) & (devices - 1)
    group_bits = groups.bit_length() - 1
    following = (following >> group_bits, following & (groups - 1))
    preceding = (preceding >> group_bits, preceding & (groups - 1))
    later = (tm + 1) & (blocks - 1)
    earlier = (tm - 1) & (blocks - 1)
    far_first = sorted(range(1, groups), key=lambda d: -min(d, groups - d))
    near = sorted(range(1, side), key=lambda d: min(d, side - d))

    def greet(device):
        pl.semaphore_signal(barrier, inc=1, device_id=device, device_id_type=MESH)

    loads = [
        pltpu.make_async_copy(source, target, load_sem.at[i])
        for i, (source, target) in enumerate(
            (
                (frames_hbm, frames_ref),
                (attn_gain_hbm, gains_ref.at[0:1]),
                (w_key_hbm, w_key),
                (w_value_hbm, w_value),
                (w_query_hbm, w_query),
                (w_out_hbm, w_out),
                (w_expand_hbm, w_expand),
                (taps_hbm, taps_ref),
                (conv_gain_hbm, gains_ref.at[1:2]),
                (scale_hbm, gains_ref.at[2:3]),
                (shift_hbm, gains_ref.at[3:4]),
                (w_project_hbm, w_project),
            )
        )
    ]
    for load in loads[:5]:
        load.start()

    barrier = pltpu.get_barrier_semaphore()
    for d in range(1, groups):
        greet(kv_peer(d))
    for d in near[:4]:
        greet(key_peer(d))
        greet(query_peer(d))

    lane = lax.broadcasted_iota(jnp.int32, (rows, LANES), 1)
    low = lane < HEAD_DIM
    first_half = lane % HEAD_DIM < HALF
    which = lax.broadcasted_iota(jnp.int32, (1, LANES), 1) % HALF
    inverse = jnp.zeros((1, LANES), F32)
    for i in range(HALF):
        inverse = jnp.where(which == i, 10000.0 ** (-2.0 * i / HEAD_DIM), inverse)
    positions = me * rows + lax.broadcasted_iota(jnp.int32, (rows, LANES), 0)
    angle = positions.astype(F32) * inverse
    cosine = jnp.cos(angle)
    sine = jnp.sin(angle)
    sine = jnp.where(first_half, -sine, sine)

    def rotated(part):
        swapped = jnp.where(
            first_half, pltpu.roll(part, LANES - HALF, 1), pltpu.roll(part, HALF, 1)
        )
        return part * cosine + swapped * sine

    loads[0].wait()
    loads[1].wait()
    inputs = frames_ref[...].astype(F32)
    halo_send[0] = inputs[:HALO].astype(BF16)
    halo_send[1] = inputs[rows - HALO :].astype(BF16)
    normed = layer_norm(inputs, gains_ref[0:1]).astype(BF16)
    loads[2].wait()
    keys = matmul(normed, w_key[...])
    loads[3].wait()
    values = matmul(normed, w_value[...])
    loads[4].wait()
    queries = matmul(normed, w_query[...])
    to_log2 = 0.125 / math.log(2.0)
    for pair in range(groups // 2):
        at = slice(pair * LANES, (pair + 1) * LANES)
        key = rotated(keys[:, at])
        query = rotated(queries[:, at]) * to_log2
        value = values[:, at]
        key_value = jnp.where(low, key, pltpu.roll(value, HEAD_DIM, 1))
        head_send[2 * pair] = jnp.concatenate(
            [key_value, jnp.where(low, query, 0.0)], axis=0
        ).astype(BF16)
        key_value = jnp.where(low, pltpu.roll(key, HEAD_DIM, 1), value)
        head_send[2 * pair + 1] = jnp.concatenate(
            [key_value, jnp.where(low, pltpu.roll(query, HEAD_DIM, 1), 0.0)], axis=0
        ).astype(BF16)

    pl.semaphore_wait(barrier, groups - 1 + 2 * len(near[:4]))

    head_copies = [
        pltpu.make_async_remote_copy(
            src_ref=head_send.at[(kv + d) & (groups - 1)],
            dst_ref=head_recv.at[kv],
            send_sem=head_ssem.at[d],
            recv_sem=head_rsem.at[d],
            device_id=kv_peer(d),
            device_id_type=MESH,
        )
        for d in far_first
    ]
    for copy in head_copies:
        copy.start()
    for load in loads[5:]:
        load.start()
    head_recv[kv] = head_send[kv]
    for copy in head_copies:
        copy.wait_recv()
    pieces = [head_recv[head].astype(F32) for head in range(groups)]
    own_block = jnp.concatenate([piece[:rows] for piece in pieces], axis=0).astype(BF16)
    kv_all[0] = own_block

    def line_copies(ref, ssem, rsem, peer, halved):
        half = ref.shape[1] // 2
        lower, upper, whole = pl.ds(0, half), pl.ds(half, half), pl.ds(0, 2 * half)
        used = []

        def copy(source, target, rows, place):
            sem = len(used)
            used.append(sem)
            return pltpu.make_async_remote_copy(
                src_ref=ref.at[source, rows],
                dst_ref=ref.at[target, rows],
                send_sem=ssem.at[sem],
                recv_sem=rsem.at[sem],
                device_id=peer(place),
                device_id_type=MESH,
            )

        def entry(place, rows, onward=()):
            return place, copy(0, place, rows, place), [
                (target, copy(place, target, rows, step)) for target, rows, step in onward
            ]

        if side < 8:
            return [entry(d, whole) for d in near]
        if halved:
            return [
                entry(2, lower, [(4, lower, 2), (3, lower, 1)]),
                entry(6, upper, [(4, upper, 6), (5, upper, 7)]),
                entry(2, upper, [(3, upper, 1)]),
                entry(6, lower, [(5, lower, 7)]),
                entry(1, whole),
                entry(7, whole),
            ]
        return [
            entry(2, whole, [(4, lower, 2), (3, whole, 1)]),
            entry(6, whole, [(4, upper, 6), (5, whole, 7)]),
            entry(1, whole),
            entry(7, whole),
        ]

    kv_line = line_copies(kv_all, kv_ssem, kv_rsem, key_peer, True)
    q_line = line_copies(q_all, q_ssem, q_rsem, query_peer, False)
    for _, copy, _ in kv_line:
        copy.start()
    own_queries = jnp.concatenate([piece[rows:] for piece in pieces], axis=0)
    q_all[0] = (
        own_queries[:half_block] + pltpu.roll(own_queries[half_block:], HEAD_DIM, 1)
    ).astype(BF16)
    for _, copy, _ in q_line:
        copy.start()
    for line in (q_line, kv_line):
        for _, copy, onward in line:
            if onward:
                copy.wait_recv()
            for _, relay in onward:
                relay.start()

    slots = [0] + near
    near_count = near_wide.shape[0] // block

    def wait_for(line, wanted):
        for slot, copy, onward in line:
            if slot in wanted and not onward:
                copy.wait_recv()
            for target, relay in onward:
                if target in wanted:
                    relay.wait_recv()

    def lay_out(few, at, wide, keys):
        both = jnp.concatenate([kv_all[d] for d in few], axis=0).astype(F32)
        at = slice(at * block, (at + len(few)) * block)
        keys[:, at] = both.T.astype(BF16)
        lane = lax.broadcasted_iota(jnp.int32, both.shape, 1)
        wide[at] = jnp.where(lane < HEAD_DIM, 1.0, both).astype(BF16)

    def lay_out_line(kv_slots, wide, keys):
        for i in range(0, len(kv_slots), 2):
            wait_for(kv_line, kv_slots[i : i + 2])
            lay_out(kv_slots[i : i + 2], i, wide, keys)

    half_lane = lax.broadcasted_iota(jnp.int32, (half_block, LANES), 1)
    block_lane = lax.broadcasted_iota(jnp.int32, (block, LANES), 1)

    def unfolded(d):
        packed = q_all[d].astype(F32)
        return jnp.concatenate(
            [
                jnp.where(half_lane < HEAD_DIM, packed, 0.0),
                jnp.where(half_lane < HEAD_DIM, pltpu.roll(packed, HEAD_DIM, 1), 0.0),
            ],
            axis=0,
        ).astype(BF16)

    def soften(scores, weights, tops, floor=None):
        for begin in range(0, 2 * block, CHUNK):
            at = slice(begin, begin + CHUNK)
            score = scores[at]
            top = jnp.max(score, axis=1, keepdims=True)
            if floor is not None:
                top = jnp.maximum(top, floor[at, :1])
            weights[at] = jnp.exp2(score - top).astype(BF16)
            tops[at] = jnp.broadcast_to(top, (CHUNK, LANES))

    def finish(d, mixed, top):
        total = jnp.where(block_lane < HEAD_DIM, mixed, pltpu.roll(mixed, HEAD_DIM, 1))
        level = top + jnp.log2(total)
        place = lax.broadcasted_iota(jnp.int32, (part_send.shape[1] - half_block, LANES), 0)
        levels = jnp.zeros(place.shape, F32)
        for i in range(level_rows):
            few = level[i * LANES : (i + 1) * LANES]
            row = lax.broadcasted_iota(jnp.int32, few.shape, 0)
            column = lax.broadcasted_iota(jnp.int32, few.shape, 1)
            line = jnp.sum(jnp.where(row == column, few, 0.0), axis=0, keepdims=True)
            high = line.astype(BF16).astype(F32)
            levels = jnp.where(place == i * side + d, high, levels)
            levels = jnp.where(place == (level_rows + i) * side + d, line - high, levels)
        part = jnp.concatenate([folded(mixed / total), levels], axis=0).astype(BF16)
        if d > 0:
            part_send[d] = part
        else:
            part_recv[d] = part

    def chosen(step, order):
        return sum((step == i).astype(jnp.int32) * d for i, d in enumerate(order))

    steps = side // 2
    pairs = [tuple(slots[2 * step : 2 * step + 2]) for step in range(steps)]
    near_order = [2, 6, 1, 7, 0] if side == 8 else slots[:near_count]
    far_order = slots[near_count:]
    wait_for(q_line, slots[:near_count])
    lay_out_line(near_order, near_wide, near_keys)

    @pl.loop(0, max(steps // 2, 1))
    def _(turn):
        @pl.when(turn == steps // 4)
        def _():
            wait_for(q_line, far_order)

        ahead = min(2, steps)
        for i in range(ahead):
            step = ahead * turn + i
            query = [unfolded(chosen(2 * step + j, slots)) for j in range(2)]
            near_scores[i] = matmul(jnp.concatenate(query, axis=0), near_keys[...])
        for i in range(ahead):
            step = ahead * turn + i
            soften(near_scores.at[i], near_weights.at[i], first_tops.at[step])
            first_mixed[step] = matmul(near_weights[i], near_wide[...])

    lay_out_line(far_order, far_wide, far_keys)

    def part_copy(d):
        return pltpu.make_async_remote_copy(
            src_ref=part_send.at[d],
            dst_ref=part_recv.at[d],
            send_sem=part_ssem.at[d],
            recv_sem=part_rsem.at[d],
            device_id=query_peer(side - d),
            device_id_type=MESH,
        )

    def score_far(step):
        query = jnp.concatenate([unfolded(d) for d in pairs[step]], axis=0)
        far_scores[step] = matmul(query, far_keys[...])

    turns = [1, 3, 2, 0] if side == 8 else list(range(steps))[::-1]
    score_far(turns[0])
    for step, following_step in zip(turns, turns[1:] + [None]):
        if following_step is not None:
            score_far(following_step)
        soften(far_scores.at[step], far_weights.at[step], far_tops.at[step], first_tops.at[step])
        top = far_tops[step]
        mixed = first_mixed[step] * jnp.exp2(first_tops[step] - top)
        mixed = mixed + matmul(far_weights[step], far_wide[...])
        for i in (1, 0):
            d = pairs[step][i]
            at = slice(i * block, (i + 1) * block)
            finish(d, mixed[at], top[at])
            if d > 0:
                part_copy(d).start()

    for d in range(1, side):
        part_copy(d).wait_recv()

    levels = part_recv[0].astype(F32)[half_block:]
    for d in range(1, side):
        levels = levels + part_recv[d].astype(F32)[half_block:]
    shares = []
    for i in range(level_rows):
        high, low = [levels[(j * level_rows + i) * side : (j * level_rows + i + 1) * side] for j in range(2)]
        level = high + low
        fade = jnp.exp2(level - jnp.max(level, axis=0, keepdims=True))
        shares.append(fade / jnp.sum(fade, axis=0, keepdims=True))
    shares = jnp.concatenate(
        shares + [jnp.zeros((LANES - side * level_rows, LANES), F32)], axis=0
    ).T
    upper = []
    begin = half_block
    while begin < block:
        i = begin // LANES
        end = min(block, (i + 1) * LANES)
        few = shares[begin - i * LANES : end - i * LANES]
        upper.append(pltpu.roll(few, LANES - i * side, 1) if i else few)
        begin = end
    lower = shares[:half_block]
    upper = jnp.concatenate(upper, axis=0)
    pick = jnp.zeros((half_block, LANES), F32)
    for i, share in enumerate((lower, upper)):
        high = share.astype(BF16).astype(F32)
        for j, piece in enumerate((high, share - high)):
            begin = (2 * i + j) * side
            piece = pltpu.roll(piece, begin, 1) if begin else piece
            pick = jnp.where((half_lane >= begin) & (half_lane < begin + side), piece, pick)
    index = lax.broadcasted_iota(jnp.int32, (LANES, side * LANES), 0)
    lane = lax.broadcasted_iota(jnp.int32, (LANES, side * LANES), 1)
    spread = (
        (index % side == lane // LANES)
        & (index < 4 * side)
        & (index // (2 * side) == lane % LANES // HEAD_DIM)
    )
    spread = matmul(pick.astype(BF16), jnp.where(spread, 1.0, 0.0).astype(BF16))
    merged = jnp.zeros((half_block, LANES), F32)
    for d in range(side):
        part = part_recv[d].astype(F32)[:half_block]
        merged = merged + spread[:, d * LANES : (d + 1) * LANES] * part
    merged = jnp.concatenate([pltpu.roll(merged, HEAD_DIM, 1), merged], axis=0)

    edge_send[0] = folded(merged[: 2 * HALO]).astype(BF16)
    edge_send[1] = folded(merged[block - 2 * HALO :]).astype(BF16)
    framed = jnp.concatenate(
        [jnp.zeros((HALO, LANES), F32), merged, jnp.zeros((WINDOW - rows - HALO, LANES), F32)],
        axis=0,
    )
    for part in range(groups):
        ctx_send[part] = folded(framed[part * rows : part * rows + WINDOW]).astype(BF16)

    def edge_copy(i, head):
        return pltpu.make_async_remote_copy(
            src_ref=edge_send.at[i],
            dst_ref=edge_recv.at[head],
            send_sem=edge_ssem.at[i],
            recv_sem=edge_rsem.at[head],
            device_id=((earlier, groups - 1), (later, 0))[i],
            device_id_type=MESH,
        )

    for i in range(2):
        edge_copy(i, kv).start()
    ctx_copies = [
        pltpu.make_async_remote_copy(
            src_ref=ctx_send.at[(kv + d) & (groups - 1)],
            dst_ref=ctx_recv.at[kv],
            send_sem=ctx_ssem.at[d],
            recv_sem=ctx_rsem.at[d],
            device_id=kv_peer(d),
            device_id_type=MESH,
        )
        for d in far_first
    ]
    for copy in ctx_copies:
        copy.start()
    halo_copies = [
        pltpu.make_async_remote_copy(
            src_ref=halo_send.at[i],
            dst_ref=halo_recv.at[i],
            send_sem=halo_ssem.at[i],
            recv_sem=halo_rsem.at[i],
            device_id=target,
            device_id_type=MESH,
        )
        for i, target in enumerate((preceding, following))
    ]
    for copy in halo_copies:
        copy.start()
    ctx_recv[kv] = ctx_send[kv]
    for copy in head_copies:
        copy.wait_send()
    for line in (kv_line, q_line):
        for _, copy, onward in line:
            copy.wait_send()
            for _, relay in onward:
                relay.wait_send()
    for d in range(1, side):
        part_copy(d).wait_send()
    for copy in ctx_copies + halo_copies:
        copy.wait_send()
    for i in range(2):
        edge_copy(i, kv).wait_send()
    for load in loads[5:]:
        load.wait()
    for copy in halo_copies:
        copy.wait_recv()
    extent = rows + 2 * HALO
    nearby = jnp.concatenate([halo_recv[1].astype(F32), inputs, halo_recv[0].astype(F32)], axis=0)
    for copy in ctx_copies:
        copy.wait_recv()
    context[...] = all_heads(ctx_recv)[:extent]

    @pl.when(kv == 0)
    def _():
        for head in range(groups):
            edge_copy(1, head).wait_recv()
        context[:HALO] = all_heads(edge_recv)[HALO:]

    @pl.when(kv == groups - 1)
    def _():
        for head in range(groups):
            edge_copy(0, head).wait_recv()
        context[extent - HALO :] = all_heads(edge_recv)[:HALO]

    attended = matmul(context[...].astype(BF16), w_out[...]).astype(BF16).astype(F32)
    attended_ref[...] = attended[HALO : HALO + rows].astype(BF16)
    mid = nearby + attended
    conv_in = layer_norm(mid, gains_ref[1:2]).astype(BF16)
    expanded = matmul(conv_in, w_expand[...])
    gate = expanded[:, width:]
    glu = (expanded[:, :width] / (1.0 + jnp.exp(-gate))).astype(BF16).astype(F32)
    times = me * rows - HALO + lax.broadcasted_iota(jnp.int32, (extent, width), 0)
    padded[...] = jnp.where((times >= 0) & (times < devices * rows), glu, 0.0)

    depth = jnp.zeros((rows, width), F32)
    count = taps_ref.shape[0]
    for turn in range(8):
        shifted = None
        for tap in range(turn - 1, count, 8):
            if tap < 0:
                continue
            term = taps_ref[tap : tap + 1] * padded[tap + 1 - turn : tap + 9 - turn + rows]
            shifted = term if shifted is None else shifted + term
        depth = depth + shifted[turn : turn + rows]
    batch = depth * gains_ref[2:3] + gains_ref[3:4]
    act = (batch / (1.0 + jnp.exp(-batch))).astype(BF16)
    layer_ref[...] = (mid[HALO : HALO + rows] + matmul(act, w_project[...])).astype(BF16)


def copy_kernel(attended_in, layer_in, attended_out, layer_out, sem):
    copies = [
        pltpu.make_async_copy(attended_in, attended_out, sem.at[0]),
        pltpu.make_async_copy(layer_in, layer_out, sem.at[1]),
    ]
    for copy in copies:
        copy.start()
    for copy in copies:
        copy.wait()


def on_device(
    frames,
    attn_gain,
    w_query,
    w_key,
    w_value,
    w_out,
    conv_gain,
    w_expand,
    kernel,
    bn_scale,
    bn_shift,
    w_project,
):
    rows, width = frames.shape
    groups = lax.axis_size("kv")
    side = math.isqrt(lax.axis_size("tm"))
    block = rows * groups
    near_rows = (5 if side == 8 else side // 2) * block
    far_rows = side * block - near_rows
    part_rows = block // 2 + -(-2 * side * -(-block // LANES) // HALO) * HALO
    vmem = pl.BlockSpec(memory_space=pltpu.VMEM)
    anywhere = pl.BlockSpec(memory_space=pl.ANY)
    dma = pltpu.SemaphoreType.DMA
    results = pl.pallas_call(
        functools.partial(layer_kernel, side),
        out_shape=(pltpu.VMEM((rows, width), BF16), pltpu.VMEM((rows, width), BF16)),
        in_specs=[anywhere] * 12,
        out_specs=(vmem, vmem),
        scratch_shapes=[
            pltpu.VMEM((rows, width), BF16),
            pltpu.VMEM((4, width), F32),
            pltpu.VMEM(kernel.shape, F32),
            pltpu.VMEM((width, width), BF16),
            pltpu.VMEM((width, width), BF16),
            pltpu.VMEM((width, width), BF16),
            pltpu.VMEM((width, width), BF16),
            pltpu.VMEM((width, 2 * width), BF16),
            pltpu.VMEM((width, width), BF16),
            pltpu.VMEM((groups, 2 * rows, LANES), BF16),
            pltpu.VMEM((groups, 2 * rows, LANES), BF16),
            pltpu.VMEM((side, block, LANES), BF16),
            pltpu.VMEM((near_rows, LANES), BF16),
            pltpu.VMEM((far_rows, LANES), BF16),
            pltpu.VMEM((LANES, near_rows), BF16),
            pltpu.VMEM((LANES, far_rows), BF16),
            pltpu.VMEM((side, block // 2, LANES), BF16),
            pltpu.VMEM((2, 2 * block, near_rows), F32),
            pltpu.VMEM((side // 2, 2 * block, far_rows), F32),
            pltpu.VMEM((2, 2 * block, near_rows), BF16),
            pltpu.VMEM((side // 2, 2 * block, far_rows), BF16),
            pltpu.VMEM((side // 2, 2 * block, LANES), F32),
            pltpu.VMEM((side // 2, 2 * block, LANES), F32),
            pltpu.VMEM((side // 2, 2 * block, LANES), F32),
            pltpu.VMEM((side, part_rows, LANES), BF16),
            pltpu.VMEM((side, part_rows, LANES), BF16),
            pltpu.VMEM((groups, WINDOW // 2, LANES), BF16),
            pltpu.VMEM((groups, WINDOW // 2, LANES), BF16),
            pltpu.VMEM((2, HALO, LANES), BF16),
            pltpu.VMEM((groups, HALO, LANES), BF16),
            pltpu.VMEM((rows + 2 * HALO, width), F32),
            pltpu.VMEM((2, HALO, width), BF16),
            pltpu.VMEM((2, HALO, width), BF16),
            pltpu.VMEM((rows + 2 * HALO, width), F32),
            dma((12,)),
            dma((groups,)),
            dma((groups,)),
            dma((2 * side,)),
            dma((2 * side,)),
            dma((side,)),
            dma((side,)),
            dma((side,)),
            dma((side,)),
            dma((groups,)),
            dma((groups,)),
            dma((2,)),
            dma((groups,)),
            dma((2,)),
            dma((2,)),
        ],
        compiler_params=pltpu.CompilerParams(
            collective_id=0, has_side_effects=True, vmem_limit_bytes=60 * 1024 * 1024
        ),
    )(
        frames,
        attn_gain.reshape(1, width),
        conv_gain.reshape(1, width),
        bn_scale.reshape(1, width),
        bn_shift.reshape(1, width),
        kernel,
        w_query,
        w_key,
        w_value,
        w_out,
        w_expand,
        w_project,
    )
    return pl.pallas_call(
        copy_kernel,
        out_shape=(jax.ShapeDtypeStruct((rows, width), BF16),) * 2,
        in_specs=[vmem] * 2,
        out_specs=(anywhere, anywhere),
        scratch_shapes=[dma((2,))],
        compiler_params=pltpu.CompilerParams(vmem_limit_bytes=4 * 1024 * 1024),
    )(*results)


def solution(mesh):
    rows = P(("tm", "kv"), None)
    return jax.shard_map(
        on_device,
        mesh=mesh,
        in_specs=(rows,) + (P(),) * 11,
        out_specs=(rows, rows),
        check_vma=False,
    )
```

```python
import functools
import math

import jax
import jax.numpy as jnp
from jax import lax
from jax.experimental import pallas as pl
from jax.experimental.pallas import tpu as pltpu
from jax.sharding import PartitionSpec as P

HEAD_DIM = 64
HALF = HEAD_DIM // 2
LANES = 128
HALO = 16
WINDOW = 64
CHUNK = 32
MESH = pl.DeviceIdType.MESH
BF16 = jnp.bfloat16
F32 = jnp.float32


def layer_norm(values, gain):
    mean = jnp.mean(values, axis=-1, keepdims=True)
    centered = values - mean
    var = jnp.mean(centered * centered, axis=-1, keepdims=True)
    return centered / jnp.sqrt(var + 1e-05) * gain


def key_groups(side):
    return {8: ([2, 6, 0], [1, 7], [3, 5, 4]), 4: ([0], [1], [3, 2])}[side]


def matmul(a, b):
    return jnp.dot(a, b, preferred_element_type=F32)


def folded(rows):
    half = rows.shape[0] // 2
    lane = lax.broadcasted_iota(jnp.int32, (half, LANES), 1)
    return jnp.where(lane < HEAD_DIM, pltpu.roll(rows[:half], HEAD_DIM, 1), rows[half:])


def all_heads(ref):
    columns = []
    lane = lax.broadcasted_iota(jnp.int32, ref.shape[1:], 1)
    for pair in range(ref.shape[0] // 2):
        even = ref[2 * pair].astype(F32)
        odd = ref[2 * pair + 1].astype(F32)
        top = jnp.where(lane < HEAD_DIM, even, pltpu.roll(odd, HEAD_DIM, 1))
        bottom = jnp.where(lane < HEAD_DIM, pltpu.roll(even, HEAD_DIM, 1), odd)
        columns.append(jnp.concatenate([top, bottom], axis=0))
    return jnp.concatenate(columns, axis=1)


def layer_kernel(
    side,
    frames_hbm,
    attn_gain_hbm,
    conv_gain_hbm,
    scale_hbm,
    shift_hbm,
    taps_hbm,
    w_query_hbm,
    w_key_hbm,
    w_value_hbm,
    w_out_hbm,
    w_expand_hbm,
    w_project_hbm,
    attended_ref,
    layer_ref,
    frames_ref,
    gains_ref,
    taps_ref,
    w_query,
    w_key,
    w_value,
    w_out,
    w_expand,
    w_project,
    head_send,
    head_recv,
    kv_all,
    near_wide,
    next_wide,
    far_wide,
    near_keys,
    next_keys,
    far_keys,
    q_all,
    near_scores,
    next_scores,
    far_scores,
    near_weights,
    next_weights,
    far_weights,
    first_mixed,
    next_mixed,
    first_tops,
    next_tops,
    far_tops,
    part_send,
    part_recv,
    ctx_send,
    ctx_recv,
    edge_send,
    edge_recv,
    context,
    halo_send,
    halo_recv,
    padded,
    load_sem,
    head_ssem,
    head_rsem,
    kv_ssem,
    kv_rsem,
    q_ssem,
    q_rsem,
    part_ssem,
    part_rsem,
    ctx_ssem,
    ctx_rsem,
    edge_ssem,
    edge_rsem,
    halo_ssem,
    halo_rsem,
):
    rows, width = frames_ref.shape
    groups = head_send.shape[0]
    block = rows * groups
    half_block = block // 2
    level_rows = -(-block // LANES)
    blocks = side * side
    tm = lax.axis_index("tm")
    kv = lax.axis_index("kv")
    bits = side.bit_length() - 1
    core = kv & 1
    slow = tm >> bits
    fast = tm & (side - 1)
    key_at = fast + core * (slow - fast)
    key_stride = 1 + core * (side - 1)
    query_at = slow + core * (fast - slow)
    query_stride = side - core * (side - 1)

    def kv_peer(d):
        return (tm, (kv + d) & (groups - 1))

    def key_peer(d):
        return (tm + (((key_at + d) & (side - 1)) - key_at) * key_stride, kv)

    def query_peer(d):
        return (tm + (((query_at + d) & (side - 1)) - query_at) * query_stride, kv)

    devices = groups * blocks
    me = tm * groups + kv
    following = (me + 1) & (devices - 1)
    preceding = (me - 1) & (devices - 1)
    group_bits = groups.bit_length() - 1
    following = (following >> group_bits, following & (groups - 1))
    preceding = (preceding >> group_bits, preceding & (groups - 1))
    later = (tm + 1) & (blocks - 1)
    earlier = (tm - 1) & (blocks - 1)
    far_first = sorted(range(1, groups), key=lambda d: -min(d, groups - d))
    near = sorted(range(1, side), key=lambda d: min(d, side - d))

    def greet(device):
        pl.semaphore_signal(barrier, inc=1, device_id=device, device_id_type=MESH)

    loads = [
        pltpu.make_async_copy(source, target, load_sem.at[i])
        for i, (source, target) in enumerate(
            (
                (frames_hbm, frames_ref),
                (attn_gain_hbm, gains_ref.at[0:1]),
                (w_key_hbm, w_key),
                (w_value_hbm, w_value),
                (w_query_hbm, w_query),
                (w_out_hbm, w_out),
                (w_expand_hbm, w_expand),
                (taps_hbm, taps_ref),
                (conv_gain_hbm, gains_ref.at[1:2]),
                (scale_hbm, gains_ref.at[2:3]),
                (shift_hbm, gains_ref.at[3:4]),
                (w_project_hbm, w_project),
            )
        )
    ]
    for load in loads[:5]:
        load.start()

    barrier = pltpu.get_barrier_semaphore()
    for d in range(1, groups):
        greet(kv_peer(d))
    for d in near[:4]:
        greet(key_peer(d))
        greet(query_peer(d))

    lane = lax.broadcasted_iota(jnp.int32, (rows, LANES), 1)
    low = lane < HEAD_DIM
    first_half = lane % HEAD_DIM < HALF
    which = lax.broadcasted_iota(jnp.int32, (1, LANES), 1) % HALF
    inverse = jnp.zeros((1, LANES), F32)
    for i in range(HALF):
        inverse = jnp.where(which == i, 10000.0 ** (-2.0 * i / HEAD_DIM), inverse)
    positions = me * rows + lax.broadcasted_iota(jnp.int32, (rows, LANES), 0)
    angle = positions.astype(F32) * inverse
    cosine = jnp.cos(angle)
    sine = jnp.sin(angle)
    sine = jnp.where(first_half, -sine, sine)

    def rotated(part):
        swapped = jnp.where(
            first_half, pltpu.roll(part, LANES - HALF, 1), pltpu.roll(part, HALF, 1)
        )
        return part * cosine + swapped * sine

    loads[0].wait()
    loads[1].wait()
    inputs = frames_ref[...].astype(F32)
    halo_send[0] = inputs[:HALO].astype(BF16)
    halo_send[1] = inputs[rows - HALO :].astype(BF16)
    normed = layer_norm(inputs, gains_ref[0:1]).astype(BF16)
    loads[2].wait()
    keys = matmul(normed, w_key[...])
    loads[3].wait()
    values = matmul(normed, w_value[...])
    loads[4].wait()
    queries = matmul(normed, w_query[...])
    to_log2 = 0.125 / math.log(2.0)
    for pair in range(groups // 2):
        at = slice(pair * LANES, (pair + 1) * LANES)
        key = rotated(keys[:, at])
        query = rotated(queries[:, at]) * to_log2
        value = values[:, at]
        key_value = jnp.where(low, key, pltpu.roll(value, HEAD_DIM, 1))
        head_send[2 * pair] = jnp.concatenate(
            [key_value, jnp.where(low, query, 0.0)], axis=0
        ).astype(BF16)
        key_value = jnp.where(low, pltpu.roll(key, HEAD_DIM, 1), value)
        head_send[2 * pair + 1] = jnp.concatenate(
            [key_value, jnp.where(low, pltpu.roll(query, HEAD_DIM, 1), 0.0)], axis=0
        ).astype(BF16)

    pl.semaphore_wait(barrier, groups - 1 + 2 * len(near[:4]))

    head_copies = [
        pltpu.make_async_remote_copy(
            src_ref=head_send.at[(kv + d) & (groups - 1)],
            dst_ref=head_recv.at[kv],
            send_sem=head_ssem.at[d],
            recv_sem=head_rsem.at[d],
            device_id=kv_peer(d),
            device_id_type=MESH,
        )
        for d in far_first
    ]
    for copy in head_copies:
        copy.start()
    for load in loads[5:]:
        load.start()
    head_recv[kv] = head_send[kv]
    for copy in head_copies:
        copy.wait_recv()
    pieces = [head_recv[head].astype(F32) for head in range(groups)]
    own_block = jnp.concatenate([piece[:rows] for piece in pieces], axis=0).astype(BF16)
    kv_all[0] = own_block

    def line_copies(ref, ssem, rsem, peer, halved):
        half = ref.shape[1] // 2
        lower, upper, whole = pl.ds(0, half), pl.ds(half, half), pl.ds(0, 2 * half)
        used = []

        def copy(source, target, rows, place):
            sem = len(used)
            used.append(sem)
            return pltpu.make_async_remote_copy(
                src_ref=ref.at[source, rows],
                dst_ref=ref.at[target, rows],
                send_sem=ssem.at[sem],
                recv_sem=rsem.at[sem],
                device_id=peer(place),
                device_id_type=MESH,
            )

        def entry(place, rows, onward=()):
            return place, copy(0, place, rows, place), [
                (target, copy(place, target, rows, step)) for target, rows, step in onward
            ]

        if side < 8:
            return [entry(d, whole) for d in near]
        if halved:
            return [
                entry(2, lower, [(4, lower, 2), (3, lower, 1)]),
                entry(6, upper, [(4, upper, 6), (5, upper, 7)]),
                entry(2, upper, [(3, upper, 1)]),
                entry(6, lower, [(5, lower, 7)]),
                entry(1, whole),
                entry(7, whole),
            ]
        return [
            entry(2, whole, [(4, lower, 2), (3, whole, 1)]),
            entry(6, whole, [(4, upper, 6), (5, whole, 7)]),
            entry(1, whole),
            entry(7, whole),
        ]

    kv_line = line_copies(kv_all, kv_ssem, kv_rsem, key_peer, True)
    q_line = line_copies(q_all, q_ssem, q_rsem, query_peer, False)
    for _, copy, _ in kv_line:
        copy.start()
    own_queries = jnp.concatenate([piece[rows:] for piece in pieces], axis=0)
    q_all[0] = (
        own_queries[:half_block] + pltpu.roll(own_queries[half_block:], HEAD_DIM, 1)
    ).astype(BF16)
    for _, copy, _ in q_line:
        copy.start()
    for line in (q_line, kv_line):
        for _, copy, onward in line:
            if onward:
                copy.wait_recv()
            for _, relay in onward:
                relay.start()

    slots = [0] + near
    near_count = side // 2 + 1

    def wait_for(line, wanted):
        for slot, copy, onward in line:
            if slot in wanted and not onward:
                copy.wait_recv()
            for target, relay in onward:
                if target in wanted:
                    relay.wait_recv()

    def lay_out(few, at, wide, keys):
        both = jnp.concatenate([kv_all[d] for d in few], axis=0).astype(F32)
        at = slice(at * block, (at + len(few)) * block)
        keys[:, at] = both.T.astype(BF16)
        lane = lax.broadcasted_iota(jnp.int32, both.shape, 1)
        wide[at] = jnp.where(lane < HEAD_DIM, 1.0, both).astype(BF16)

    def lay_out_line(kv_slots, wide, keys):
        for i in range(0, len(kv_slots), 2):
            wait_for(kv_line, kv_slots[i : i + 2])
            lay_out(kv_slots[i : i + 2], i, wide, keys)

    half_lane = lax.broadcasted_iota(jnp.int32, (half_block, LANES), 1)
    block_lane = lax.broadcasted_iota(jnp.int32, (block, LANES), 1)

    def unfolded(d):
        packed = q_all[d].astype(F32)
        return jnp.concatenate(
            [
                jnp.where(half_lane < HEAD_DIM, packed, 0.0),
                jnp.where(half_lane < HEAD_DIM, pltpu.roll(packed, HEAD_DIM, 1), 0.0),
            ],
            axis=0,
        ).astype(BF16)

    def soften(scores, weights, tops, floor=None):
        for begin in range(0, 2 * block, CHUNK):
            at = slice(begin, begin + CHUNK)
            score = scores[at]
            top = jnp.max(score, axis=1, keepdims=True)
            if floor is not None:
                top = jnp.maximum(top, floor[at, :1])
            weights[at] = jnp.exp2(score - top).astype(BF16)
            tops[at] = jnp.broadcast_to(top, (CHUNK, LANES))

    def finish(d, mixed, top):
        total = jnp.where(block_lane < HEAD_DIM, mixed, pltpu.roll(mixed, HEAD_DIM, 1))
        level = top + jnp.log2(total)
        place = lax.broadcasted_iota(jnp.int32, (part_send.shape[1] - half_block, LANES), 0)
        levels = jnp.zeros(place.shape, F32)
        for i in range(level_rows):
            few = level[i * LANES : (i + 1) * LANES]
            row = lax.broadcasted_iota(jnp.int32, few.shape, 0)
            column = lax.broadcasted_iota(jnp.int32, few.shape, 1)
            line = jnp.sum(jnp.where(row == column, few, 0.0), axis=0, keepdims=True)
            high = line.astype(BF16).astype(F32)
            levels = jnp.where(place == i * side + d, high, levels)
            levels = jnp.where(place == (level_rows + i) * side + d, line - high, levels)
        part = jnp.concatenate([folded(mixed / total), levels], axis=0).astype(BF16)
        if d > 0:
            part_send[d] = part
        else:
            part_recv[d] = part

    def chosen(step, order):
        return sum((step == i).astype(jnp.int32) * d for i, d in enumerate(order))

    steps = side // 2
    pairs = [tuple(slots[2 * step : 2 * step + 2]) for step in range(steps)]
    near_order, next_order, far_order = key_groups(side)
    ahead = min(2, steps)
    wait_for(q_line, slots[:near_count])
    lay_out_line(near_order, near_wide, near_keys)

    def scored(step, keys):
        query = [unfolded(chosen(2 * step + j, slots)) for j in range(2)]
        return matmul(jnp.concatenate(query, axis=0), keys[...])

    @pl.loop(0, steps // ahead)
    def _(turn):
        @pl.when(turn == steps // 4)
        def _():
            wait_for(q_line, slots[near_count:])

        for i in range(ahead):
            near_scores[i] = scored(ahead * turn + i, near_keys)
        for i in range(ahead):
            step = ahead * turn + i
            soften(near_scores.at[i], near_weights.at[i], first_tops.at[step])
            first_mixed[step] = matmul(near_weights[i], near_wide[...])

    lay_out_line(next_order, next_wide, next_keys)

    @pl.loop(0, steps // ahead)
    def _(turn):
        for i in range(ahead):
            next_scores[i] = scored(ahead * turn + i, next_keys)
        for i in range(ahead):
            step = ahead * turn + i
            soften(next_scores.at[i], next_weights.at[i], next_tops.at[step], first_tops.at[step])
            mixed = first_mixed[step] * jnp.exp2(first_tops[step] - next_tops[step])
            next_mixed[step] = mixed + matmul(next_weights[i], next_wide[...])

    lay_out_line(far_order, far_wide, far_keys)

    def part_copy(d):
        return pltpu.make_async_remote_copy(
            src_ref=part_send.at[d],
            dst_ref=part_recv.at[d],
            send_sem=part_ssem.at[d],
            recv_sem=part_rsem.at[d],
            device_id=query_peer(side - d),
            device_id_type=MESH,
        )

    def score_far(step):
        query = jnp.concatenate([unfolded(d) for d in pairs[step]], axis=0)
        far_scores[step] = matmul(query, far_keys[...])

    turns = list(range(steps))[::-1]
    score_far(turns[0])
    for step, following_step in zip(turns, turns[1:] + [None]):
        if following_step is not None:
            score_far(following_step)
        soften(far_scores.at[step], far_weights.at[step], far_tops.at[step], next_tops.at[step])
        top = far_tops[step]
        mixed = next_mixed[step] * jnp.exp2(next_tops[step] - top)
        mixed = mixed + matmul(far_weights[step], far_wide[...])
        for i in (1, 0):
            d = pairs[step][i]
            at = slice(i * block, (i + 1) * block)
            finish(d, mixed[at], top[at])
            if d > 0:
                part_copy(d).start()

    for d in range(1, side):
        part_copy(d).wait_recv()

    levels = part_recv[0].astype(F32)[half_block:]
    for d in range(1, side):
        levels = levels + part_recv[d].astype(F32)[half_block:]
    shares = []
    for i in range(level_rows):
        high, low = [levels[(j * level_rows + i) * side : (j * level_rows + i + 1) * side] for j in range(2)]
        level = high + low
        fade = jnp.exp2(level - jnp.max(level, axis=0, keepdims=True))
        shares.append(fade / jnp.sum(fade, axis=0, keepdims=True))
    shares = jnp.concatenate(
        shares + [jnp.zeros((LANES - side * level_rows, LANES), F32)], axis=0
    ).T
    upper = []
    begin = half_block
    while begin < block:
        i = begin // LANES
        end = min(block, (i + 1) * LANES)
        few = shares[begin - i * LANES : end - i * LANES]
        upper.append(pltpu.roll(few, LANES - i * side, 1) if i else few)
        begin = end
    lower = shares[:half_block]
    upper = jnp.concatenate(upper, axis=0)
    pick = jnp.zeros((half_block, LANES), F32)
    for i, share in enumerate((lower, upper)):
        high = share.astype(BF16).astype(F32)
        for j, piece in enumerate((high, share - high)):
            begin = (2 * i + j) * side
            piece = pltpu.roll(piece, begin, 1) if begin else piece
            pick = jnp.where((half_lane >= begin) & (half_lane < begin + side), piece, pick)
    index = lax.broadcasted_iota(jnp.int32, (LANES, side * LANES), 0)
    lane = lax.broadcasted_iota(jnp.int32, (LANES, side * LANES), 1)
    spread = (
        (index % side == lane // LANES)
        & (index < 4 * side)
        & (index // (2 * side) == lane % LANES // HEAD_DIM)
    )
    spread = matmul(pick.astype(BF16), jnp.where(spread, 1.0, 0.0).astype(BF16))
    merged = jnp.zeros((half_block, LANES), F32)
    for d in range(side):
        part = part_recv[d].astype(F32)[:half_block]
        merged = merged + spread[:, d * LANES : (d + 1) * LANES] * part
    merged = jnp.concatenate([pltpu.roll(merged, HEAD_DIM, 1), merged], axis=0)

    edge_send[0] = folded(merged[: 2 * HALO]).astype(BF16)
    edge_send[1] = folded(merged[block - 2 * HALO :]).astype(BF16)
    framed = jnp.concatenate(
        [jnp.zeros((HALO, LANES), F32), merged, jnp.zeros((WINDOW - rows - HALO, LANES), F32)],
        axis=0,
    )
    for part in range(groups):
        ctx_send[part] = folded(framed[part * rows : part * rows + WINDOW]).astype(BF16)

    def edge_copy(i, head):
        return pltpu.make_async_remote_copy(
            src_ref=edge_send.at[i],
            dst_ref=edge_recv.at[head],
            send_sem=edge_ssem.at[i],
            recv_sem=edge_rsem.at[head],
            device_id=((earlier, groups - 1), (later, 0))[i],
            device_id_type=MESH,
        )

    for i in range(2):
        edge_copy(i, kv).start()
    ctx_copies = [
        pltpu.make_async_remote_copy(
            src_ref=ctx_send.at[(kv + d) & (groups - 1)],
            dst_ref=ctx_recv.at[kv],
            send_sem=ctx_ssem.at[d],
            recv_sem=ctx_rsem.at[d],
            device_id=kv_peer(d),
            device_id_type=MESH,
        )
        for d in far_first
    ]
    for copy in ctx_copies:
        copy.start()
    halo_copies = [
        pltpu.make_async_remote_copy(
            src_ref=halo_send.at[i],
            dst_ref=halo_recv.at[i],
            send_sem=halo_ssem.at[i],
            recv_sem=halo_rsem.at[i],
            device_id=target,
            device_id_type=MESH,
        )
        for i, target in enumerate((preceding, following))
    ]
    for copy in halo_copies:
        copy.start()
    ctx_recv[kv] = ctx_send[kv]
    for copy in head_copies:
        copy.wait_send()
    for line in (kv_line, q_line):
        for _, copy, onward in line:
            copy.wait_send()
            for _, relay in onward:
                relay.wait_send()
    for d in range(1, side):
        part_copy(d).wait_send()
    for copy in ctx_copies + halo_copies:
        copy.wait_send()
    for i in range(2):
        edge_copy(i, kv).wait_send()
    for load in loads[5:]:
        load.wait()
    for copy in halo_copies:
        copy.wait_recv()
    extent = rows + 2 * HALO
    nearby = jnp.concatenate([halo_recv[1].astype(F32), inputs, halo_recv[0].astype(F32)], axis=0)
    for copy in ctx_copies:
        copy.wait_recv()
    context[...] = all_heads(ctx_recv)[:extent]

    @pl.when(kv == 0)
    def _():
        for head in range(groups):
            edge_copy(1, head).wait_recv()
        context[:HALO] = all_heads(edge_recv)[HALO:]

    @pl.when(kv == groups - 1)
    def _():
        for head in range(groups):
            edge_copy(0, head).wait_recv()
        context[extent - HALO :] = all_heads(edge_recv)[:HALO]

    attended = matmul(context[...].astype(BF16), w_out[...]).astype(BF16).astype(F32)
    attended_ref[...] = attended[HALO : HALO + rows].astype(BF16)
    mid = nearby + attended
    conv_in = layer_norm(mid, gains_ref[1:2]).astype(BF16)
    expanded = matmul(conv_in, w_expand[...])
    gate = expanded[:, width:]
    glu = (expanded[:, :width] / (1.0 + jnp.exp(-gate))).astype(BF16).astype(F32)
    times = me * rows - HALO + lax.broadcasted_iota(jnp.int32, (extent, width), 0)
    padded[...] = jnp.where((times >= 0) & (times < devices * rows), glu, 0.0)

    depth = jnp.zeros((rows, width), F32)
    count = taps_ref.shape[0]
    for turn in range(8):
        shifted = None
        for tap in range(turn - 1, count, 8):
            if tap < 0:
                continue
            term = taps_ref[tap : tap + 1] * padded[tap + 1 - turn : tap + 9 - turn + rows]
            shifted = term if shifted is None else shifted + term
        depth = depth + shifted[turn : turn + rows]
    batch = depth * gains_ref[2:3] + gains_ref[3:4]
    act = (batch / (1.0 + jnp.exp(-batch))).astype(BF16)
    layer_ref[...] = (mid[HALO : HALO + rows] + matmul(act, w_project[...])).astype(BF16)


def copy_kernel(attended_in, layer_in, attended_out, layer_out, sem):
    copies = [
        pltpu.make_async_copy(attended_in, attended_out, sem.at[0]),
        pltpu.make_async_copy(layer_in, layer_out, sem.at[1]),
    ]
    for copy in copies:
        copy.start()
    for copy in copies:
        copy.wait()


def on_device(
    frames,
    attn_gain,
    w_query,
    w_key,
    w_value,
    w_out,
    conv_gain,
    w_expand,
    kernel,
    bn_scale,
    bn_shift,
    w_project,
):
    rows, width = frames.shape
    groups = lax.axis_size("kv")
    side = math.isqrt(lax.axis_size("tm"))
    block = rows * groups
    near_rows, next_rows, far_rows = [len(group) * block for group in key_groups(side)]
    part_rows = block // 2 + -(-2 * side * -(-block // LANES) // HALO) * HALO
    vmem = pl.BlockSpec(memory_space=pltpu.VMEM)
    anywhere = pl.BlockSpec(memory_space=pl.ANY)
    dma = pltpu.SemaphoreType.DMA
    results = pl.pallas_call(
        functools.partial(layer_kernel, side),
        out_shape=(pltpu.VMEM((rows, width), BF16), pltpu.VMEM((rows, width), BF16)),
        in_specs=[anywhere] * 12,
        out_specs=(vmem, vmem),
        scratch_shapes=[
            pltpu.VMEM((rows, width), BF16),
            pltpu.VMEM((4, width), F32),
            pltpu.VMEM(kernel.shape, F32),
            pltpu.VMEM((width, width), BF16),
            pltpu.VMEM((width, width), BF16),
            pltpu.VMEM((width, width), BF16),
            pltpu.VMEM((width, width), BF16),
            pltpu.VMEM((width, 2 * width), BF16),
            pltpu.VMEM((width, width), BF16),
            pltpu.VMEM((groups, 2 * rows, LANES), BF16),
            pltpu.VMEM((groups, 2 * rows, LANES), BF16),
            pltpu.VMEM((side, block, LANES), BF16),
            pltpu.VMEM((near_rows, LANES), BF16),
            pltpu.VMEM((next_rows, LANES), BF16),
            pltpu.VMEM((far_rows, LANES), BF16),
            pltpu.VMEM((LANES, near_rows), BF16),
            pltpu.VMEM((LANES, next_rows), BF16),
            pltpu.VMEM((LANES, far_rows), BF16),
            pltpu.VMEM((side, block // 2, LANES), BF16),
            pltpu.VMEM((2, 2 * block, near_rows), F32),
            pltpu.VMEM((2, 2 * block, next_rows), F32),
            pltpu.VMEM((side // 2, 2 * block, far_rows), F32),
            pltpu.VMEM((2, 2 * block, near_rows), BF16),
            pltpu.VMEM((2, 2 * block, next_rows), BF16),
            pltpu.VMEM((side // 2, 2 * block, far_rows), BF16),
            pltpu.VMEM((side // 2, 2 * block, LANES), F32),
            pltpu.VMEM((side // 2, 2 * block, LANES), F32),
            pltpu.VMEM((side // 2, 2 * block, LANES), F32),
            pltpu.VMEM((side // 2, 2 * block, LANES), F32),
            pltpu.VMEM((side // 2, 2 * block, LANES), F32),
            pltpu.VMEM((side, part_rows, LANES), BF16),
            pltpu.VMEM((side, part_rows, LANES), BF16),
            pltpu.VMEM((groups, WINDOW // 2, LANES), BF16),
            pltpu.VMEM((groups, WINDOW // 2, LANES), BF16),
            pltpu.VMEM((2, HALO, LANES), BF16),
            pltpu.VMEM((groups, HALO, LANES), BF16),
            pltpu.VMEM((rows + 2 * HALO, width), F32),
            pltpu.VMEM((2, HALO, width), BF16),
            pltpu.VMEM((2, HALO, width), BF16),
            pltpu.VMEM((rows + 2 * HALO, width), F32),
            dma((12,)),
            dma((groups,)),
            dma((groups,)),
            dma((2 * side,)),
            dma((2 * side,)),
            dma((side,)),
            dma((side,)),
            dma((side,)),
            dma((side,)),
            dma((groups,)),
            dma((groups,)),
            dma((2,)),
            dma((groups,)),
            dma((2,)),
            dma((2,)),
        ],
        compiler_params=pltpu.CompilerParams(
            collective_id=0, has_side_effects=True, vmem_limit_bytes=60 * 1024 * 1024
        ),
    )(
        frames,
        attn_gain.reshape(1, width),
        conv_gain.reshape(1, width),
        bn_scale.reshape(1, width),
        bn_shift.reshape(1, width),
        kernel,
        w_query,
        w_key,
        w_value,
        w_out,
        w_expand,
        w_project,
    )
    return pl.pallas_call(
        copy_kernel,
        out_shape=(jax.ShapeDtypeStruct((rows, width), BF16),) * 2,
        in_specs=[vmem] * 2,
        out_specs=(anywhere, anywhere),
        scratch_shapes=[dma((2,))],
        compiler_params=pltpu.CompilerParams(vmem_limit_bytes=4 * 1024 * 1024),
    )(*results)


def solution(mesh):
    rows = P(("tm", "kv"), None)
    return jax.shard_map(
        on_device,
        mesh=mesh,
        in_specs=(rows,) + (P(),) * 11,
        out_specs=(rows, rows),
        check_vma=False,
    )
```

```python
import functools
import math

import jax
import jax.numpy as jnp
from jax import lax
from jax.experimental import pallas as pl
from jax.experimental.pallas import tpu as pltpu
from jax.sharding import PartitionSpec as P

HEAD_DIM = 64
HALF = HEAD_DIM // 2
LANES = 128
HALO = 16
WINDOW = 64
CHUNK = 32
MESH = pl.DeviceIdType.MESH
BF16 = jnp.bfloat16
F32 = jnp.float32


def layer_norm(values, gain):
    mean = jnp.mean(values, axis=-1, keepdims=True)
    centered = values - mean
    var = jnp.mean(centered * centered, axis=-1, keepdims=True)
    return centered / jnp.sqrt(var + 1e-05) * gain


def matmul(a, b):
    return jnp.dot(a, b, preferred_element_type=F32)


def folded(rows):
    half = rows.shape[0] // 2
    lane = lax.broadcasted_iota(jnp.int32, (half, LANES), 1)
    return jnp.where(lane < HEAD_DIM, pltpu.roll(rows[:half], HEAD_DIM, 1), rows[half:])


def all_heads(ref):
    columns = []
    lane = lax.broadcasted_iota(jnp.int32, ref.shape[1:], 1)
    for pair in range(ref.shape[0] // 2):
        even = ref[2 * pair].astype(F32)
        odd = ref[2 * pair + 1].astype(F32)
        top = jnp.where(lane < HEAD_DIM, even, pltpu.roll(odd, HEAD_DIM, 1))
        bottom = jnp.where(lane < HEAD_DIM, pltpu.roll(even, HEAD_DIM, 1), odd)
        columns.append(jnp.concatenate([top, bottom], axis=0))
    return jnp.concatenate(columns, axis=1)


def layer_kernel(
    side,
    frames_hbm,
    attn_gain_hbm,
    conv_gain_hbm,
    scale_hbm,
    shift_hbm,
    taps_hbm,
    w_query_hbm,
    w_key_hbm,
    w_value_hbm,
    w_out_hbm,
    w_expand_hbm,
    w_project_hbm,
    attended_ref,
    layer_ref,
    frames_ref,
    gains_ref,
    taps_ref,
    w_query,
    w_key,
    w_value,
    w_out,
    w_expand,
    w_project,
    head_send,
    head_recv,
    kv_all,
    near_wide,
    far_wide,
    near_keys,
    far_keys,
    q_all,
    near_scores,
    far_scores,
    near_weights,
    far_weights,
    far_tops,
    first_mixed,
    first_tops,
    part_send,
    part_recv,
    ctx_send,
    ctx_recv,
    edge_send,
    edge_recv,
    context,
    halo_send,
    halo_recv,
    padded,
    load_sem,
    head_ssem,
    head_rsem,
    kv_ssem,
    kv_rsem,
    q_ssem,
    q_rsem,
    part_ssem,
    part_rsem,
    ctx_ssem,
    ctx_rsem,
    edge_ssem,
    edge_rsem,
    halo_ssem,
    halo_rsem,
):
    rows, width = frames_ref.shape
    groups = head_send.shape[0]
    block = rows * groups
    half_block = block // 2
    level_rows = -(-block // LANES)
    blocks = side * side
    tm = lax.axis_index("tm")
    kv = lax.axis_index("kv")
    bits = side.bit_length() - 1
    core = kv & 1
    slow = tm >> bits
    fast = tm & (side - 1)
    key_at = fast + core * (slow - fast)
    key_stride = 1 + core * (side - 1)
    query_at = slow + core * (fast - slow)
    query_stride = side - core * (side - 1)

    def kv_peer(d):
        return (tm, (kv + d) & (groups - 1))

    def key_peer(d):
        return (tm + (((key_at + d) & (side - 1)) - key_at) * key_stride, kv)

    def query_peer(d):
        return (tm + (((query_at + d) & (side - 1)) - query_at) * query_stride, kv)

    devices = groups * blocks
    me = tm * groups + kv
    following = (me + 1) & (devices - 1)
    preceding = (me - 1) & (devices - 1)
    group_bits = groups.bit_length() - 1
    following = (following >> group_bits, following & (groups - 1))
    preceding = (preceding >> group_bits, preceding & (groups - 1))
    later = (tm + 1) & (blocks - 1)
    earlier = (tm - 1) & (blocks - 1)
    far_first = sorted(range(1, groups), key=lambda d: -min(d, groups - d))
    near = sorted(range(1, side), key=lambda d: min(d, side - d))

    def greet(device):
        pl.semaphore_signal(barrier, inc=1, device_id=device, device_id_type=MESH)

    loads = [
        pltpu.make_async_copy(source, target, load_sem.at[i])
        for i, (source, target) in enumerate(
            (
                (frames_hbm, frames_ref),
                (attn_gain_hbm, gains_ref.at[0:1]),
                (w_key_hbm, w_key),
                (w_value_hbm, w_value),
                (w_query_hbm, w_query),
                (w_out_hbm, w_out),
                (w_expand_hbm, w_expand),
                (taps_hbm, taps_ref),
                (conv_gain_hbm, gains_ref.at[1:2]),
                (scale_hbm, gains_ref.at[2:3]),
                (shift_hbm, gains_ref.at[3:4]),
                (w_project_hbm, w_project),
            )
        )
    ]
    for load in loads[:5]:
        load.start()

    barrier = pltpu.get_barrier_semaphore()
    for d in range(1, groups):
        greet(kv_peer(d))
    for d in near[:4]:
        greet(key_peer(d))
        greet(query_peer(d))

    lane = lax.broadcasted_iota(jnp.int32, (rows, LANES), 1)
    low = lane < HEAD_DIM
    first_half = lane % HEAD_DIM < HALF
    which = lax.broadcasted_iota(jnp.int32, (1, LANES), 1) % HALF
    inverse = jnp.zeros((1, LANES), F32)
    for i in range(HALF):
        inverse = jnp.where(which == i, 10000.0 ** (-2.0 * i / HEAD_DIM), inverse)
    positions = me * rows + lax.broadcasted_iota(jnp.int32, (rows, LANES), 0)
    angle = positions.astype(F32) * inverse
    cosine = jnp.cos(angle)
    sine = jnp.sin(angle)
    sine = jnp.where(first_half, -sine, sine)

    def rotated(part):
        swapped = jnp.where(
            first_half, pltpu.roll(part, LANES - HALF, 1), pltpu.roll(part, HALF, 1)
        )
        return part * cosine + swapped * sine

    loads[0].wait()
    loads[1].wait()
    inputs = frames_ref[...].astype(F32)
    halo_send[0] = inputs[:HALO].astype(BF16)
    halo_send[1] = inputs[rows - HALO :].astype(BF16)
    normed = layer_norm(inputs, gains_ref[0:1]).astype(BF16)
    loads[2].wait()
    keys = matmul(normed, w_key[...])
    loads[3].wait()
    values = matmul(normed, w_value[...])
    loads[4].wait()
    queries = matmul(normed, w_query[...])
    to_log2 = 0.125 / math.log(2.0)
    for pair in range(groups // 2):
        at = slice(pair * LANES, (pair + 1) * LANES)
        key = rotated(keys[:, at])
        query = rotated(queries[:, at]) * to_log2
        value = values[:, at]
        key_value = jnp.where(low, key, pltpu.roll(value, HEAD_DIM, 1))
        head_send[2 * pair] = jnp.concatenate(
            [key_value, jnp.where(low, query, 0.0)], axis=0
        ).astype(BF16)
        key_value = jnp.where(low, pltpu.roll(key, HEAD_DIM, 1), value)
        head_send[2 * pair + 1] = jnp.concatenate(
            [key_value, jnp.where(low, pltpu.roll(query, HEAD_DIM, 1), 0.0)], axis=0
        ).astype(BF16)

    pl.semaphore_wait(barrier, groups - 1 + 2 * len(near[:4]))

    head_copies = [
        pltpu.make_async_remote_copy(
            src_ref=head_send.at[(kv + d) & (groups - 1)],
            dst_ref=head_recv.at[kv],
            send_sem=head_ssem.at[d],
            recv_sem=head_rsem.at[d],
            device_id=kv_peer(d),
            device_id_type=MESH,
        )
        for d in far_first
    ]
    for copy in head_copies:
        copy.start()
    for load in loads[5:]:
        load.start()
    head_recv[kv] = head_send[kv]
    for copy in head_copies:
        copy.wait_recv()
    pieces = [head_recv[head].astype(F32) for head in range(groups)]
    own_block = jnp.concatenate([piece[:rows] for piece in pieces], axis=0).astype(BF16)
    kv_all[0] = own_block

    def line_copies(ref, ssem, rsem, peer, halved):
        half = ref.shape[1] // 2
        lower, upper, whole = pl.ds(0, half), pl.ds(half, half), pl.ds(0, 2 * half)
        used = []

        def copy(source, target, rows, place):
            sem = len(used)
            used.append(sem)
            return pltpu.make_async_remote_copy(
                src_ref=ref.at[source, rows],
                dst_ref=ref.at[target, rows],
                send_sem=ssem.at[sem],
                recv_sem=rsem.at[sem],
                device_id=peer(place),
                device_id_type=MESH,
            )

        def entry(place, rows, onward=()):
            return place, copy(0, place, rows, place), [
                (target, copy(place, target, rows, step)) for target, rows, step in onward
            ]

        if side < 8:
            return [entry(d, whole) for d in near]
        if halved:
            return [
                entry(1, whole),
                entry(7, whole),
                entry(2, lower, [(4, lower, 2), (3, lower, 1)]),
                entry(6, upper, [(4, upper, 6), (5, upper, 7)]),
                entry(2, upper, [(3, upper, 1)]),
                entry(6, lower, [(5, lower, 7)]),
            ]
        return [
            entry(1, whole),
            entry(7, whole),
            entry(2, whole, [(4, lower, 2), (3, whole, 1)]),
            entry(6, whole, [(4, upper, 6), (5, whole, 7)]),
        ]

    kv_line = line_copies(kv_all, kv_ssem, kv_rsem, key_peer, True)
    q_line = line_copies(q_all, q_ssem, q_rsem, query_peer, False)
    for _, copy, _ in kv_line:
        copy.start()
    own_queries = jnp.concatenate([piece[rows:] for piece in pieces], axis=0)
    q_all[0] = (
        own_queries[:half_block] + pltpu.roll(own_queries[half_block:], HEAD_DIM, 1)
    ).astype(BF16)
    for _, copy, _ in q_line:
        copy.start()
    for line in (q_line, kv_line):
        for _, copy, onward in line:
            if onward:
                copy.wait_recv()
            for _, relay in onward:
                relay.start()

    slots = [0] + near
    near_count = near_wide.shape[0] // block

    def wait_for(line, wanted):
        for slot, copy, onward in line:
            if slot in wanted and not onward:
                copy.wait_recv()
            for target, relay in onward:
                if target in wanted:
                    relay.wait_recv()

    def lay_out(few, at, wide, keys):
        both = jnp.concatenate([kv_all[d] for d in few], axis=0).astype(F32)
        at = slice(at * block, (at + len(few)) * block)
        keys[:, at] = both.T.astype(BF16)
        lane = lax.broadcasted_iota(jnp.int32, both.shape, 1)
        wide[at] = jnp.where(lane < HEAD_DIM, 1.0, both).astype(BF16)

    def lay_out_line(kv_slots, wide, keys):
        for i in range(0, len(kv_slots), 2):
            wait_for(kv_line, kv_slots[i : i + 2])
            lay_out(kv_slots[i : i + 2], i, wide, keys)

    half_lane = lax.broadcasted_iota(jnp.int32, (half_block, LANES), 1)
    block_lane = lax.broadcasted_iota(jnp.int32, (block, LANES), 1)

    def unfolded(d):
        packed = q_all[d].astype(F32)
        return jnp.concatenate(
            [
                jnp.where(half_lane < HEAD_DIM, packed, 0.0),
                jnp.where(half_lane < HEAD_DIM, pltpu.roll(packed, HEAD_DIM, 1), 0.0),
            ],
            axis=0,
        ).astype(BF16)

    def soften(scores, weights, tops, floor=None):
        for begin in range(0, 2 * block, CHUNK):
            at = slice(begin, begin + CHUNK)
            score = scores[at]
            top = jnp.max(score, axis=1, keepdims=True)
            if floor is not None:
                top = jnp.maximum(top, floor[at, :1])
            weights[at] = jnp.exp2(score - top).astype(BF16)
            tops[at] = jnp.broadcast_to(top, (CHUNK, LANES))

    def finish(d, mixed, top):
        total = jnp.where(block_lane < HEAD_DIM, mixed, pltpu.roll(mixed, HEAD_DIM, 1))
        level = top + jnp.log2(total)
        place = lax.broadcasted_iota(jnp.int32, (HALO, LANES), 0)
        levels = jnp.zeros((HALO, LANES), F32)
        for i in range(level_rows):
            few = level[i * LANES : (i + 1) * LANES]
            row = lax.broadcasted_iota(jnp.int32, few.shape, 0)
            column = lax.broadcasted_iota(jnp.int32, few.shape, 1)
            line = jnp.sum(jnp.where(row == column, few, 0.0), axis=0, keepdims=True)
            high = line.astype(BF16).astype(F32)
            levels = jnp.where(place == i, high, levels)
            levels = jnp.where(place == level_rows + i, line - high, levels)
        part = jnp.concatenate([folded(mixed / total), levels], axis=0).astype(BF16)
        if d > 0:
            part_send[d] = part
        else:
            part_recv[d] = part

    steps = side // 2
    pairs = [tuple(slots[2 * step : 2 * step + 2]) for step in range(steps)]
    near_order = [2, 6, 1, 7, 0] if side == 8 else slots[:near_count]
    far_order = slots[near_count:]
    wait_for(q_line, slots[:near_count])
    lay_out_line(near_order, near_wide, near_keys)

    def score_near(step):
        if step == near_count // 2:
            wait_for(q_line, far_order)
        query = jnp.concatenate([unfolded(d) for d in pairs[step]], axis=0)
        near_scores[step & 1] = matmul(query, near_keys[...])

    score_near(0)
    for step in range(steps):
        if step + 1 < steps:
            score_near(step + 1)
        i = step & 1
        soften(near_scores.at[i], near_weights.at[i], first_tops.at[step])
        first_mixed[step] = matmul(near_weights[i], near_wide[...])

    lay_out_line(far_order, far_wide, far_keys)

    def part_copy(d):
        return pltpu.make_async_remote_copy(
            src_ref=part_send.at[d],
            dst_ref=part_recv.at[d],
            send_sem=part_ssem.at[d],
            recv_sem=part_rsem.at[d],
            device_id=query_peer(side - d),
            device_id_type=MESH,
        )

    def score_far(step):
        query = jnp.concatenate([unfolded(d) for d in pairs[step]], axis=0)
        far_scores[step] = matmul(query, far_keys[...])

    score_far(steps - 1)
    for step in range(steps - 1, -1, -1):
        if step > 0:
            score_far(step - 1)
        soften(far_scores.at[step], far_weights.at[step], far_tops.at[step], first_tops.at[step])
        top = far_tops[step]
        mixed = first_mixed[step] * jnp.exp2(first_tops[step] - top)
        mixed = mixed + matmul(far_weights[step], far_wide[...])
        for i in (1, 0):
            d = pairs[step][i]
            at = slice(i * block, (i + 1) * block)
            finish(d, mixed[at], top[at])
            if d > 0:
                part_copy(d).start()

    for d in range(1, side):
        part_copy(d).wait_recv()

    levels = []
    for i in range(level_rows):
        levels.append(
            [
                part_recv[d, half_block + i : half_block + i + 1].astype(F32)
                + part_recv[d, half_block + level_rows + i : half_block + level_rows + i + 1].astype(F32)
                for d in range(side)
            ]
        )
    shares = []
    for level in levels:
        level = jnp.concatenate(level, axis=0)
        fade = jnp.exp2(level - jnp.max(level, axis=0, keepdims=True))
        shares.append(fade / jnp.sum(fade, axis=0, keepdims=True))
    shares = jnp.concatenate(
        shares + [jnp.zeros((LANES - side * level_rows, LANES), F32)], axis=0
    ).T
    upper = []
    begin = half_block
    while begin < block:
        i = begin // LANES
        end = min(block, (i + 1) * LANES)
        few = shares[begin - i * LANES : end - i * LANES]
        upper.append(pltpu.roll(few, LANES - i * side, 1) if i else few)
        begin = end
    lower = shares[:half_block]
    upper = jnp.concatenate(upper, axis=0)
    pick = jnp.zeros((half_block, LANES), F32)
    for i, share in enumerate((lower, upper)):
        high = share.astype(BF16).astype(F32)
        for j, piece in enumerate((high, share - high)):
            begin = (2 * i + j) * side
            piece = pltpu.roll(piece, begin, 1) if begin else piece
            pick = jnp.where((half_lane >= begin) & (half_lane < begin + side), piece, pick)
    index = lax.broadcasted_iota(jnp.int32, (LANES, side * LANES), 0)
    lane = lax.broadcasted_iota(jnp.int32, (LANES, side * LANES), 1)
    spread = (
        (index % side == lane // LANES)
        & (index < 4 * side)
        & (index // (2 * side) == lane % LANES // HEAD_DIM)
    )
    spread = matmul(pick.astype(BF16), jnp.where(spread, 1.0, 0.0).astype(BF16))
    merged = jnp.zeros((half_block, LANES), F32)
    for d in range(side):
        part = part_recv[d].astype(F32)[:half_block]
        merged = merged + spread[:, d * LANES : (d + 1) * LANES] * part
    merged = jnp.concatenate([pltpu.roll(merged, HEAD_DIM, 1), merged], axis=0)

    edge_send[0] = folded(merged[: 2 * HALO]).astype(BF16)
    edge_send[1] = folded(merged[block - 2 * HALO :]).astype(BF16)
    framed = jnp.concatenate(
        [jnp.zeros((HALO, LANES), F32), merged, jnp.zeros((WINDOW - rows - HALO, LANES), F32)],
        axis=0,
    )
    for part in range(groups):
        ctx_send[part] = folded(framed[part * rows : part * rows + WINDOW]).astype(BF16)

    def edge_copy(i, head):
        return pltpu.make_async_remote_copy(
            src_ref=edge_send.at[i],
            dst_ref=edge_recv.at[head],
            send_sem=edge_ssem.at[i],
            recv_sem=edge_rsem.at[head],
            device_id=((earlier, groups - 1), (later, 0))[i],
            device_id_type=MESH,
        )

    for i in range(2):
        edge_copy(i, kv).start()
    ctx_copies = [
        pltpu.make_async_remote_copy(
            src_ref=ctx_send.at[(kv + d) & (groups - 1)],
            dst_ref=ctx_recv.at[kv],
            send_sem=ctx_ssem.at[d],
            recv_sem=ctx_rsem.at[d],
            device_id=kv_peer(d),
            device_id_type=MESH,
        )
        for d in far_first
    ]
    for copy in ctx_copies:
        copy.start()
    halo_copies = [
        pltpu.make_async_remote_copy(
            src_ref=halo_send.at[i],
            dst_ref=halo_recv.at[i],
            send_sem=halo_ssem.at[i],
            recv_sem=halo_rsem.at[i],
            device_id=target,
            device_id_type=MESH,
        )
        for i, target in enumerate((preceding, following))
    ]
    for copy in halo_copies:
        copy.start()
    ctx_recv[kv] = ctx_send[kv]
    for copy in head_copies:
        copy.wait_send()
    for line in (kv_line, q_line):
        for _, copy, onward in line:
            copy.wait_send()
            for _, relay in onward:
                relay.wait_send()
    for d in range(1, side):
        part_copy(d).wait_send()
    for copy in ctx_copies + halo_copies:
        copy.wait_send()
    for i in range(2):
        edge_copy(i, kv).wait_send()
    for load in loads[5:]:
        load.wait()
    for copy in halo_copies:
        copy.wait_recv()
    extent = rows + 2 * HALO
    nearby = jnp.concatenate([halo_recv[1].astype(F32), inputs, halo_recv[0].astype(F32)], axis=0)
    for copy in ctx_copies:
        copy.wait_recv()
    context[...] = all_heads(ctx_recv)[:extent]

    @pl.when(kv == 0)
    def _():
        for head in range(groups):
            edge_copy(1, head).wait_recv()
        context[:HALO] = all_heads(edge_recv)[HALO:]

    @pl.when(kv == groups - 1)
    def _():
        for head in range(groups):
            edge_copy(0, head).wait_recv()
        context[extent - HALO :] = all_heads(edge_recv)[:HALO]

    attended = matmul(context[...].astype(BF16), w_out[...]).astype(BF16).astype(F32)
    attended_ref[...] = attended[HALO : HALO + rows].astype(BF16)
    mid = nearby + attended
    conv_in = layer_norm(mid, gains_ref[1:2]).astype(BF16)
    expanded = matmul(conv_in, w_expand[...])
    gate = expanded[:, width:]
    glu = (expanded[:, :width] / (1.0 + jnp.exp(-gate))).astype(BF16).astype(F32)
    times = me * rows - HALO + lax.broadcasted_iota(jnp.int32, (extent, width), 0)
    padded[...] = jnp.where((times >= 0) & (times < devices * rows), glu, 0.0)

    depth = jnp.zeros((rows, width), F32)
    count = taps_ref.shape[0]
    for turn in range(8):
        shifted = None
        for tap in range(turn - 1, count, 8):
            if tap < 0:
                continue
            term = taps_ref[tap : tap + 1] * padded[tap + 1 - turn : tap + 9 - turn + rows]
            shifted = term if shifted is None else shifted + term
        depth = depth + shifted[turn : turn + rows]
    batch = depth * gains_ref[2:3] + gains_ref[3:4]
    act = (batch / (1.0 + jnp.exp(-batch))).astype(BF16)
    layer_ref[...] = (mid[HALO : HALO + rows] + matmul(act, w_project[...])).astype(BF16)


def copy_kernel(attended_in, layer_in, attended_out, layer_out, sem):
    copies = [
        pltpu.make_async_copy(attended_in, attended_out, sem.at[0]),
        pltpu.make_async_copy(layer_in, layer_out, sem.at[1]),
    ]
    for copy in copies:
        copy.start()
    for copy in copies:
        copy.wait()


def on_device(
    frames,
    attn_gain,
    w_query,
    w_key,
    w_value,
    w_out,
    conv_gain,
    w_expand,
    kernel,
    bn_scale,
    bn_shift,
    w_project,
):
    rows, width = frames.shape
    groups = lax.axis_size("kv")
    side = math.isqrt(lax.axis_size("tm"))
    block = rows * groups
    near_rows = (5 if side == 8 else side // 2) * block
    far_rows = side * block - near_rows
    vmem = pl.BlockSpec(memory_space=pltpu.VMEM)
    anywhere = pl.BlockSpec(memory_space=pl.ANY)
    dma = pltpu.SemaphoreType.DMA
    results = pl.pallas_call(
        functools.partial(layer_kernel, side),
        out_shape=(pltpu.VMEM((rows, width), BF16), pltpu.VMEM((rows, width), BF16)),
        in_specs=[anywhere] * 12,
        out_specs=(vmem, vmem),
        scratch_shapes=[
            pltpu.VMEM((rows, width), BF16),
            pltpu.VMEM((4, width), F32),
            pltpu.VMEM(kernel.shape, F32),
            pltpu.VMEM((width, width), BF16),
            pltpu.VMEM((width, width), BF16),
            pltpu.VMEM((width, width), BF16),
            pltpu.VMEM((width, width), BF16),
            pltpu.VMEM((width, 2 * width), BF16),
            pltpu.VMEM((width, width), BF16),
            pltpu.VMEM((groups, 2 * rows, LANES), BF16),
            pltpu.VMEM((groups, 2 * rows, LANES), BF16),
            pltpu.VMEM((side, block, LANES), BF16),
            pltpu.VMEM((near_rows, LANES), BF16),
            pltpu.VMEM((far_rows, LANES), BF16),
            pltpu.VMEM((LANES, near_rows), BF16),
            pltpu.VMEM((LANES, far_rows), BF16),
            pltpu.VMEM((side, block // 2, LANES), BF16),
            pltpu.VMEM((2, 2 * block, near_rows), F32),
            pltpu.VMEM((side // 2, 2 * block, far_rows), F32),
            pltpu.VMEM((2, 2 * block, near_rows), BF16),
            pltpu.VMEM((side // 2, 2 * block, far_rows), BF16),
            pltpu.VMEM((side // 2, 2 * block, LANES), F32),
            pltpu.VMEM((side // 2, 2 * block, LANES), F32),
            pltpu.VMEM((side // 2, 2 * block, LANES), F32),
            pltpu.VMEM((side, block // 2 + HALO, LANES), BF16),
            pltpu.VMEM((side, block // 2 + HALO, LANES), BF16),
            pltpu.VMEM((groups, WINDOW // 2, LANES), BF16),
            pltpu.VMEM((groups, WINDOW // 2, LANES), BF16),
            pltpu.VMEM((2, HALO, LANES), BF16),
            pltpu.VMEM((groups, HALO, LANES), BF16),
            pltpu.VMEM((rows + 2 * HALO, width), F32),
            pltpu.VMEM((2, HALO, width), BF16),
            pltpu.VMEM((2, HALO, width), BF16),
            pltpu.VMEM((rows + 2 * HALO, width), F32),
            dma((12,)),
            dma((groups,)),
            dma((groups,)),
            dma((2 * side,)),
            dma((2 * side,)),
            dma((side,)),
            dma((side,)),
            dma((side,)),
            dma((side,)),
            dma((groups,)),
            dma((groups,)),
            dma((2,)),
            dma((groups,)),
            dma((2,)),
            dma((2,)),
        ],
        compiler_params=pltpu.CompilerParams(
            collective_id=0, has_side_effects=True, vmem_limit_bytes=60 * 1024 * 1024
        ),
    )(
        frames,
        attn_gain.reshape(1, width),
        conv_gain.reshape(1, width),
        bn_scale.reshape(1, width),
        bn_shift.reshape(1, width),
        kernel,
        w_query,
        w_key,
        w_value,
        w_out,
        w_expand,
        w_project,
    )
    return pl.pallas_call(
        copy_kernel,
        out_shape=(jax.ShapeDtypeStruct((rows, width), BF16),) * 2,
        in_specs=[vmem] * 2,
        out_specs=(anywhere, anywhere),
        scratch_shapes=[dma((2,))],
        compiler_params=pltpu.CompilerParams(vmem_limit_bytes=4 * 1024 * 1024),
    )(*results)


def solution(mesh):
    rows = P(("tm", "kv"), None)
    return jax.shard_map(
        on_device,
        mesh=mesh,
        in_specs=(rows,) + (P(),) * 11,
        out_specs=(rows, rows),
        check_vma=False,
    )
```

```python
import functools
import math

import jax
import jax.numpy as jnp
from jax import lax
from jax.experimental import pallas as pl
from jax.experimental.pallas import tpu as pltpu
from jax.sharding import PartitionSpec as P

HEAD_DIM = 64
HALF = HEAD_DIM // 2
LANES = 128
HALO = 16
WINDOW = 64
CHUNK = 32
MESH = pl.DeviceIdType.MESH
BF16 = jnp.bfloat16
F32 = jnp.float32


def layer_norm(values, gain):
    mean = jnp.mean(values, axis=-1, keepdims=True)
    centered = values - mean
    var = jnp.mean(centered * centered, axis=-1, keepdims=True)
    return centered / jnp.sqrt(var + 1e-05) * gain


def matmul(a, b):
    return jnp.dot(a, b, preferred_element_type=F32)


def folded(rows):
    half = rows.shape[0] // 2
    lane = lax.broadcasted_iota(jnp.int32, (half, LANES), 1)
    return jnp.where(lane < HEAD_DIM, pltpu.roll(rows[:half], HEAD_DIM, 1), rows[half:])


def all_heads(ref):
    columns = []
    lane = lax.broadcasted_iota(jnp.int32, ref.shape[1:], 1)
    for pair in range(ref.shape[0] // 2):
        even = ref[2 * pair].astype(F32)
        odd = ref[2 * pair + 1].astype(F32)
        top = jnp.where(lane < HEAD_DIM, even, pltpu.roll(odd, HEAD_DIM, 1))
        bottom = jnp.where(lane < HEAD_DIM, pltpu.roll(even, HEAD_DIM, 1), odd)
        columns.append(jnp.concatenate([top, bottom], axis=0))
    return jnp.concatenate(columns, axis=1)


def layer_kernel(
    side,
    frames_hbm,
    attn_gain_hbm,
    conv_gain_hbm,
    scale_hbm,
    shift_hbm,
    taps_hbm,
    w_query_hbm,
    w_key_hbm,
    w_value_hbm,
    w_out_hbm,
    w_expand_hbm,
    w_project_hbm,
    attended_ref,
    layer_ref,
    frames_ref,
    gains_ref,
    taps_ref,
    w_query,
    w_key,
    w_value,
    w_out,
    w_expand,
    w_project,
    head_send,
    head_recv,
    kv_all,
    near_wide,
    far_wide,
    near_keys,
    far_keys,
    q_all,
    near_scores,
    far_scores,
    near_weights,
    far_weights,
    far_tops,
    first_mixed,
    first_tops,
    part_send,
    part_recv,
    ctx_send,
    ctx_recv,
    edge_send,
    edge_recv,
    context,
    halo_send,
    halo_recv,
    padded,
    load_sem,
    head_ssem,
    head_rsem,
    kv_ssem,
    kv_rsem,
    q_ssem,
    q_rsem,
    part_ssem,
    part_rsem,
    ctx_ssem,
    ctx_rsem,
    edge_ssem,
    edge_rsem,
    halo_ssem,
    halo_rsem,
):
    rows, width = frames_ref.shape
    groups = head_send.shape[0]
    block = rows * groups
    half_block = block // 2
    level_rows = -(-block // LANES)
    blocks = side * side
    tm = lax.axis_index("tm")
    kv = lax.axis_index("kv")
    bits = side.bit_length() - 1
    core = kv & 1
    slow = tm >> bits
    fast = tm & (side - 1)
    key_at = fast + core * (slow - fast)
    key_stride = 1 + core * (side - 1)
    query_at = slow + core * (fast - slow)
    query_stride = side - core * (side - 1)

    def kv_peer(d):
        return (tm, (kv + d) & (groups - 1))

    def key_peer(d):
        return (tm + (((key_at + d) & (side - 1)) - key_at) * key_stride, kv)

    def query_peer(d):
        return (tm + (((query_at + d) & (side - 1)) - query_at) * query_stride, kv)

    devices = groups * blocks
    me = tm * groups + kv
    following = (me + 1) & (devices - 1)
    preceding = (me - 1) & (devices - 1)
    group_bits = groups.bit_length() - 1
    following = (following >> group_bits, following & (groups - 1))
    preceding = (preceding >> group_bits, preceding & (groups - 1))
    later = (tm + 1) & (blocks - 1)
    earlier = (tm - 1) & (blocks - 1)
    far_first = sorted(range(1, groups), key=lambda d: -min(d, groups - d))
    near = sorted(range(1, side), key=lambda d: min(d, side - d))

    def greet(device):
        pl.semaphore_signal(barrier, inc=1, device_id=device, device_id_type=MESH)

    loads = [
        pltpu.make_async_copy(source, target, load_sem.at[i])
        for i, (source, target) in enumerate(
            (
                (frames_hbm, frames_ref),
                (attn_gain_hbm, gains_ref.at[0:1]),
                (w_key_hbm, w_key),
                (w_value_hbm, w_value),
                (w_query_hbm, w_query),
                (w_out_hbm, w_out),
                (w_expand_hbm, w_expand),
                (taps_hbm, taps_ref),
                (conv_gain_hbm, gains_ref.at[1:2]),
                (scale_hbm, gains_ref.at[2:3]),
                (shift_hbm, gains_ref.at[3:4]),
                (w_project_hbm, w_project),
            )
        )
    ]
    for load in loads[:5]:
        load.start()

    barrier = pltpu.get_barrier_semaphore()
    for d in range(1, groups):
        greet(kv_peer(d))
    for d in near[:4]:
        greet(key_peer(d))
        greet(query_peer(d))

    lane = lax.broadcasted_iota(jnp.int32, (rows, LANES), 1)
    low = lane < HEAD_DIM
    first_half = lane % HEAD_DIM < HALF
    which = lax.broadcasted_iota(jnp.int32, (1, LANES), 1) % HALF
    inverse = jnp.zeros((1, LANES), F32)
    for i in range(HALF):
        inverse = jnp.where(which == i, 10000.0 ** (-2.0 * i / HEAD_DIM), inverse)
    positions = me * rows + lax.broadcasted_iota(jnp.int32, (rows, LANES), 0)
    angle = positions.astype(F32) * inverse
    cosine = jnp.cos(angle)
    sine = jnp.sin(angle)
    sine = jnp.where(first_half, -sine, sine)

    def rotated(part):
        swapped = jnp.where(
            first_half, pltpu.roll(part, LANES - HALF, 1), pltpu.roll(part, HALF, 1)
        )
        return part * cosine + swapped * sine

    loads[0].wait()
    loads[1].wait()
    inputs = frames_ref[...].astype(F32)
    halo_send[0] = inputs[:HALO].astype(BF16)
    halo_send[1] = inputs[rows - HALO :].astype(BF16)
    normed = layer_norm(inputs, gains_ref[0:1]).astype(BF16)
    loads[2].wait()
    keys = matmul(normed, w_key[...])
    loads[3].wait()
    values = matmul(normed, w_value[...])
    loads[4].wait()
    queries = matmul(normed, w_query[...])
    to_log2 = 0.125 / math.log(2.0)
    for pair in range(groups // 2):
        at = slice(pair * LANES, (pair + 1) * LANES)
        key = rotated(keys[:, at])
        query = rotated(queries[:, at]) * to_log2
        value = values[:, at]
        key_value = jnp.where(low, key, pltpu.roll(value, HEAD_DIM, 1))
        head_send[2 * pair] = jnp.concatenate(
            [key_value, jnp.where(low, query, 0.0)], axis=0
        ).astype(BF16)
        key_value = jnp.where(low, pltpu.roll(key, HEAD_DIM, 1), value)
        head_send[2 * pair + 1] = jnp.concatenate(
            [key_value, jnp.where(low, pltpu.roll(query, HEAD_DIM, 1), 0.0)], axis=0
        ).astype(BF16)

    pl.semaphore_wait(barrier, groups - 1 + 2 * len(near[:4]))

    head_copies = [
        pltpu.make_async_remote_copy(
            src_ref=head_send.at[(kv + d) & (groups - 1)],
            dst_ref=head_recv.at[kv],
            send_sem=head_ssem.at[d],
            recv_sem=head_rsem.at[d],
            device_id=kv_peer(d),
            device_id_type=MESH,
        )
        for d in far_first
    ]
    for copy in head_copies:
        copy.start()
    for load in loads[5:]:
        load.start()
    head_recv[kv] = head_send[kv]
    for copy in head_copies:
        copy.wait_recv()
    pieces = [head_recv[head].astype(F32) for head in range(groups)]
    own_block = jnp.concatenate([piece[:rows] for piece in pieces], axis=0).astype(BF16)
    kv_all[0] = own_block

    def line_copies(ref, ssem, rsem, peer, halved):
        half = ref.shape[1] // 2
        lower, upper, whole = pl.ds(0, half), pl.ds(half, half), pl.ds(0, 2 * half)
        used = []

        def copy(source, target, rows, place):
            sem = len(used)
            used.append(sem)
            return pltpu.make_async_remote_copy(
                src_ref=ref.at[source, rows],
                dst_ref=ref.at[target, rows],
                send_sem=ssem.at[sem],
                recv_sem=rsem.at[sem],
                device_id=peer(place),
                device_id_type=MESH,
            )

        def entry(place, rows, onward=()):
            return place, copy(0, place, rows, place), [
                (target, copy(place, target, rows, step)) for target, rows, step in onward
            ]

        if side < 8:
            return [entry(d, whole) for d in near]
        if halved:
            return [
                entry(2, lower, [(4, lower, 2), (3, lower, 1)]),
                entry(6, upper, [(4, upper, 6), (5, upper, 7)]),
                entry(2, upper, [(3, upper, 1)]),
                entry(6, lower, [(5, lower, 7)]),
                entry(1, whole),
                entry(7, whole),
            ]
        return [
            entry(2, whole, [(4, lower, 2), (3, whole, 1)]),
            entry(6, whole, [(4, upper, 6), (5, whole, 7)]),
            entry(1, whole),
            entry(7, whole),
        ]

    kv_line = line_copies(kv_all, kv_ssem, kv_rsem, key_peer, True)
    q_line = line_copies(q_all, q_ssem, q_rsem, query_peer, False)
    for _, copy, _ in kv_line:
        copy.start()
    own_queries = jnp.concatenate([piece[rows:] for piece in pieces], axis=0)
    q_all[0] = (
        own_queries[:half_block] + pltpu.roll(own_queries[half_block:], HEAD_DIM, 1)
    ).astype(BF16)
    for _, copy, _ in q_line:
        copy.start()
    for _, copy, onward in kv_line[:2] + q_line + kv_line[2:]:
        if onward:
            copy.wait_recv()
        for _, relay in onward:
            relay.start()

    slots = [0] + near
    near_count = near_wide.shape[0] // block

    def wait_for(line, wanted):
        for slot, copy, onward in line:
            if slot in wanted and not onward:
                copy.wait_recv()
            for target, relay in onward:
                if target in wanted:
                    relay.wait_recv()

    def lay_out(few, at, wide, keys):
        both = jnp.concatenate([kv_all[d] for d in few], axis=0).astype(F32)
        at = slice(at * block, (at + len(few)) * block)
        keys[:, at] = both.T.astype(BF16)
        lane = lax.broadcasted_iota(jnp.int32, both.shape, 1)
        wide[at] = jnp.where(lane < HEAD_DIM, 1.0, both).astype(BF16)

    def lay_out_line(kv_slots, wide, keys):
        for i in range(0, len(kv_slots), 2):
            wait_for(kv_line, kv_slots[i : i + 2])
            lay_out(kv_slots[i : i + 2], i, wide, keys)

    half_lane = lax.broadcasted_iota(jnp.int32, (half_block, LANES), 1)
    block_lane = lax.broadcasted_iota(jnp.int32, (block, LANES), 1)

    def unfolded(d):
        packed = q_all[d].astype(F32)
        return jnp.concatenate(
            [
                jnp.where(half_lane < HEAD_DIM, packed, 0.0),
                jnp.where(half_lane < HEAD_DIM, pltpu.roll(packed, HEAD_DIM, 1), 0.0),
            ],
            axis=0,
        ).astype(BF16)

    def soften(scores, weights, tops, floor=None):
        for begin in range(0, 2 * block, CHUNK):
            at = slice(begin, begin + CHUNK)
            score = scores[at]
            top = jnp.max(score, axis=1, keepdims=True)
            if floor is not None:
                top = jnp.maximum(top, floor[at, :1])
            weights[at] = jnp.exp2(score - top).astype(BF16)
            tops[at] = jnp.broadcast_to(top, (CHUNK, LANES))

    def finish(d, mixed, top):
        total = jnp.where(block_lane < HEAD_DIM, mixed, pltpu.roll(mixed, HEAD_DIM, 1))
        level = top + jnp.log2(total)
        place = lax.broadcasted_iota(jnp.int32, (HALO, LANES), 0)
        levels = jnp.zeros((HALO, LANES), F32)
        for i in range(level_rows):
            few = level[i * LANES : (i + 1) * LANES]
            row = lax.broadcasted_iota(jnp.int32, few.shape, 0)
            column = lax.broadcasted_iota(jnp.int32, few.shape, 1)
            line = jnp.sum(jnp.where(row == column, few, 0.0), axis=0, keepdims=True)
            high = line.astype(BF16).astype(F32)
            levels = jnp.where(place == i, high, levels)
            levels = jnp.where(place == level_rows + i, line - high, levels)
        part_send[d] = jnp.concatenate(
            [folded(mixed / total), levels], axis=0
        ).astype(BF16)

    def chosen(step, order):
        return sum((step == i).astype(jnp.int32) * d for i, d in enumerate(order))

    steps = side // 2
    pairs = [tuple(slots[2 * step : 2 * step + 2]) for step in range(steps)]
    near_order = [2, 6, 1, 7, 0] if side == 8 else slots[:near_count]
    far_order = slots[near_count:]
    wait_for(q_line, slots[:near_count])
    lay_out_line(near_order, near_wide, near_keys)

    @pl.loop(0, max(steps // 2, 1))
    def _(turn):
        @pl.when(turn == steps // 4)
        def _():
            wait_for(q_line, far_order)

        ahead = min(2, steps)
        for i in range(ahead):
            step = ahead * turn + i
            query = [unfolded(chosen(2 * step + j, slots)) for j in range(2)]
            near_scores[i] = matmul(jnp.concatenate(query, axis=0), near_keys[...])
        for i in range(ahead):
            step = ahead * turn + i
            soften(near_scores.at[i], near_weights.at[i], first_tops.at[step])
            first_mixed[step] = matmul(near_weights[i], near_wide[...])

    lay_out_line(far_order, far_wide, far_keys)

    def part_copy(d):
        return pltpu.make_async_remote_copy(
            src_ref=part_send.at[d],
            dst_ref=part_recv.at[d],
            send_sem=part_ssem.at[d],
            recv_sem=part_rsem.at[d],
            device_id=query_peer(side - d),
            device_id_type=MESH,
        )

    def score_far(step):
        query = jnp.concatenate([unfolded(d) for d in pairs[step]], axis=0)
        far_scores[step] = matmul(query, far_keys[...])

    score_far(steps - 1)
    for step in range(steps - 1, -1, -1):
        if step > 0:
            score_far(step - 1)
        soften(far_scores.at[step], far_weights.at[step], far_tops.at[step], first_tops.at[step])
        top = far_tops[step]
        mixed = first_mixed[step] * jnp.exp2(first_tops[step] - top)
        mixed = mixed + matmul(far_weights[step], far_wide[...])
        for i in (1, 0):
            d = pairs[step][i]
            at = slice(i * block, (i + 1) * block)
            finish(d, mixed[at], top[at])
            if d > 0:
                part_copy(d).start()

    part_recv[0] = part_send[0]
    for d in range(1, side):
        part_copy(d).wait_recv()

    levels = []
    for i in range(level_rows):
        levels.append(
            [
                part_recv[d, half_block + i : half_block + i + 1].astype(F32)
                + part_recv[d, half_block + level_rows + i : half_block + level_rows + i + 1].astype(F32)
                for d in range(side)
            ]
        )
    shares = []
    for level in levels:
        level = jnp.concatenate(level, axis=0)
        fade = jnp.exp2(level - jnp.max(level, axis=0, keepdims=True))
        shares.append(fade / jnp.sum(fade, axis=0, keepdims=True))
    shares = jnp.concatenate(
        shares + [jnp.zeros((LANES - side * level_rows, LANES), F32)], axis=0
    ).T
    upper = []
    begin = half_block
    while begin < block:
        i = begin // LANES
        end = min(block, (i + 1) * LANES)
        few = shares[begin - i * LANES : end - i * LANES]
        upper.append(pltpu.roll(few, LANES - i * side, 1) if i else few)
        begin = end
    lower = shares[:half_block]
    upper = jnp.concatenate(upper, axis=0)
    pick = jnp.zeros((half_block, LANES), F32)
    for i, share in enumerate((lower, upper)):
        high = share.astype(BF16).astype(F32)
        for j, piece in enumerate((high, share - high)):
            begin = (2 * i + j) * side
            piece = pltpu.roll(piece, begin, 1) if begin else piece
            pick = jnp.where((half_lane >= begin) & (half_lane < begin + side), piece, pick)
    index = lax.broadcasted_iota(jnp.int32, (LANES, side * LANES), 0)
    lane = lax.broadcasted_iota(jnp.int32, (LANES, side * LANES), 1)
    spread = (
        (index % side == lane // LANES)
        & (index < 4 * side)
        & (index // (2 * side) == lane % LANES // HEAD_DIM)
    )
    spread = matmul(pick.astype(BF16), jnp.where(spread, 1.0, 0.0).astype(BF16))
    merged = jnp.zeros((half_block, LANES), F32)
    for d in range(side):
        part = part_recv[d].astype(F32)[:half_block]
        merged = merged + spread[:, d * LANES : (d + 1) * LANES] * part
    merged = jnp.concatenate([pltpu.roll(merged, HEAD_DIM, 1), merged], axis=0)

    edge_send[0] = folded(merged[: 2 * HALO]).astype(BF16)
    edge_send[1] = folded(merged[block - 2 * HALO :]).astype(BF16)
    framed = jnp.concatenate(
        [jnp.zeros((HALO, LANES), F32), merged, jnp.zeros((WINDOW - rows - HALO, LANES), F32)],
        axis=0,
    )
    for part in range(groups):
        ctx_send[part] = folded(framed[part * rows : part * rows + WINDOW]).astype(BF16)

    def edge_copy(i, head):
        return pltpu.make_async_remote_copy(
            src_ref=edge_send.at[i],
            dst_ref=edge_recv.at[head],
            send_sem=edge_ssem.at[i],
            recv_sem=edge_rsem.at[head],
            device_id=((earlier, groups - 1), (later, 0))[i],
            device_id_type=MESH,
        )

    for i in range(2):
        edge_copy(i, kv).start()
    ctx_copies = [
        pltpu.make_async_remote_copy(
            src_ref=ctx_send.at[(kv + d) & (groups - 1)],
            dst_ref=ctx_recv.at[kv],
            send_sem=ctx_ssem.at[d],
            recv_sem=ctx_rsem.at[d],
            device_id=kv_peer(d),
            device_id_type=MESH,
        )
        for d in far_first
    ]
    for copy in ctx_copies:
        copy.start()
    halo_copies = [
        pltpu.make_async_remote_copy(
            src_ref=halo_send.at[i],
            dst_ref=halo_recv.at[i],
            send_sem=halo_ssem.at[i],
            recv_sem=halo_rsem.at[i],
            device_id=target,
            device_id_type=MESH,
        )
        for i, target in enumerate((preceding, following))
    ]
    for copy in halo_copies:
        copy.start()
    ctx_recv[kv] = ctx_send[kv]
    for copy in head_copies:
        copy.wait_send()
    for line in (kv_line, q_line):
        for _, copy, onward in line:
            copy.wait_send()
            for _, relay in onward:
                relay.wait_send()
    for d in range(1, side):
        part_copy(d).wait_send()
    for copy in ctx_copies + halo_copies:
        copy.wait_send()
    for i in range(2):
        edge_copy(i, kv).wait_send()
    for load in loads[5:]:
        load.wait()
    for copy in halo_copies:
        copy.wait_recv()
    extent = rows + 2 * HALO
    nearby = jnp.concatenate([halo_recv[1].astype(F32), inputs, halo_recv[0].astype(F32)], axis=0)
    for copy in ctx_copies:
        copy.wait_recv()
    context[...] = all_heads(ctx_recv)[:extent]

    @pl.when(kv == 0)
    def _():
        for head in range(groups):
            edge_copy(1, head).wait_recv()
        context[:HALO] = all_heads(edge_recv)[HALO:]

    @pl.when(kv == groups - 1)
    def _():
        for head in range(groups):
            edge_copy(0, head).wait_recv()
        context[extent - HALO :] = all_heads(edge_recv)[:HALO]

    attended = matmul(context[...].astype(BF16), w_out[...]).astype(BF16).astype(F32)
    attended_ref[...] = attended[HALO : HALO + rows].astype(BF16)
    mid = nearby + attended
    conv_in = layer_norm(mid, gains_ref[1:2]).astype(BF16)
    expanded = matmul(conv_in, w_expand[...])
    gate = expanded[:, width:]
    glu = (expanded[:, :width] / (1.0 + jnp.exp(-gate))).astype(BF16).astype(F32)
    times = me * rows - HALO + lax.broadcasted_iota(jnp.int32, (extent, width), 0)
    padded[...] = jnp.where((times >= 0) & (times < devices * rows), glu, 0.0)

    depth = jnp.zeros((rows, width), F32)
    count = taps_ref.shape[0]
    for turn in range(8):
        shifted = None
        for tap in range(turn - 1, count, 8):
            if tap < 0:
                continue
            term = taps_ref[tap : tap + 1] * padded[tap + 1 - turn : tap + 9 - turn + rows]
            shifted = term if shifted is None else shifted + term
        depth = depth + shifted[turn : turn + rows]
    batch = depth * gains_ref[2:3] + gains_ref[3:4]
    act = (batch / (1.0 + jnp.exp(-batch))).astype(BF16)
    layer_ref[...] = (mid[HALO : HALO + rows] + matmul(act, w_project[...])).astype(BF16)


def copy_kernel(attended_in, layer_in, attended_out, layer_out, sem):
    copies = [
        pltpu.make_async_copy(attended_in, attended_out, sem.at[0]),
        pltpu.make_async_copy(layer_in, layer_out, sem.at[1]),
    ]
    for copy in copies:
        copy.start()
    for copy in copies:
        copy.wait()


def on_device(
    frames,
    attn_gain,
    w_query,
    w_key,
    w_value,
    w_out,
    conv_gain,
    w_expand,
    kernel,
    bn_scale,
    bn_shift,
    w_project,
):
    rows, width = frames.shape
    groups = lax.axis_size("kv")
    side = math.isqrt(lax.axis_size("tm"))
    block = rows * groups
    near_rows = (5 if side == 8 else side // 2) * block
    far_rows = side * block - near_rows
    vmem = pl.BlockSpec(memory_space=pltpu.VMEM)
    anywhere = pl.BlockSpec(memory_space=pl.ANY)
    dma = pltpu.SemaphoreType.DMA
    results = pl.pallas_call(
        functools.partial(layer_kernel, side),
        out_shape=(pltpu.VMEM((rows, width), BF16), pltpu.VMEM((rows, width), BF16)),
        in_specs=[anywhere] * 12,
        out_specs=(vmem, vmem),
        scratch_shapes=[
            pltpu.VMEM((rows, width), BF16),
            pltpu.VMEM((4, width), F32),
            pltpu.VMEM(kernel.shape, F32),
            pltpu.VMEM((width, width), BF16),
            pltpu.VMEM((width, width), BF16),
            pltpu.VMEM((width, width), BF16),
            pltpu.VMEM((width, width), BF16),
            pltpu.VMEM((width, 2 * width), BF16),
            pltpu.VMEM((width, width), BF16),
            pltpu.VMEM((groups, 2 * rows, LANES), BF16),
            pltpu.VMEM((groups, 2 * rows, LANES), BF16),
            pltpu.VMEM((side, block, LANES), BF16),
            pltpu.VMEM((near_rows, LANES), BF16),
            pltpu.VMEM((far_rows, LANES), BF16),
            pltpu.VMEM((LANES, near_rows), BF16),
            pltpu.VMEM((LANES, far_rows), BF16),
            pltpu.VMEM((side, block // 2, LANES), BF16),
            pltpu.VMEM((2, 2 * block, near_rows), F32),
            pltpu.VMEM((side // 2, 2 * block, far_rows), F32),
            pltpu.VMEM((2, 2 * block, near_rows), BF16),
            pltpu.VMEM((side // 2, 2 * block, far_rows), BF16),
            pltpu.VMEM((side // 2, 2 * block, LANES), F32),
            pltpu.VMEM((side // 2, 2 * block, LANES), F32),
            pltpu.VMEM((side // 2, 2 * block, LANES), F32),
            pltpu.VMEM((side, block // 2 + HALO, LANES), BF16),
            pltpu.VMEM((side, block // 2 + HALO, LANES), BF16),
            pltpu.VMEM((groups, WINDOW // 2, LANES), BF16),
            pltpu.VMEM((groups, WINDOW // 2, LANES), BF16),
            pltpu.VMEM((2, HALO, LANES), BF16),
            pltpu.VMEM((groups, HALO, LANES), BF16),
            pltpu.VMEM((rows + 2 * HALO, width), F32),
            pltpu.VMEM((2, HALO, width), BF16),
            pltpu.VMEM((2, HALO, width), BF16),
            pltpu.VMEM((rows + 2 * HALO, width), F32),
            dma((12,)),
            dma((groups,)),
            dma((groups,)),
            dma((2 * side,)),
            dma((2 * side,)),
            dma((side,)),
            dma((side,)),
            dma((side,)),
            dma((side,)),
            dma((groups,)),
            dma((groups,)),
            dma((2,)),
            dma((groups,)),
            dma((2,)),
            dma((2,)),
        ],
        compiler_params=pltpu.CompilerParams(
            collective_id=0, has_side_effects=True, vmem_limit_bytes=60 * 1024 * 1024
        ),
    )(
        frames,
        attn_gain.reshape(1, width),
        conv_gain.reshape(1, width),
        bn_scale.reshape(1, width),
        bn_shift.reshape(1, width),
        kernel,
        w_query,
        w_key,
        w_value,
        w_out,
        w_expand,
        w_project,
    )
    return pl.pallas_call(
        copy_kernel,
        out_shape=(jax.ShapeDtypeStruct((rows, width), BF16),) * 2,
        in_specs=[vmem] * 2,
        out_specs=(anywhere, anywhere),
        scratch_shapes=[dma((2,))],
        compiler_params=pltpu.CompilerParams(vmem_limit_bytes=4 * 1024 * 1024),
    )(*results)


def solution(mesh):
    rows = P(("tm", "kv"), None)
    return jax.shard_map(
        on_device,
        mesh=mesh,
        in_specs=(rows,) + (P(),) * 11,
        out_specs=(rows, rows),
        check_vma=False,
    )
```

```python
import functools
import math

import jax
import jax.numpy as jnp
from jax import lax
from jax.experimental import pallas as pl
from jax.experimental.pallas import tpu as pltpu
from jax.sharding import PartitionSpec as P

HEAD_DIM = 64
HALF = HEAD_DIM // 2
LANES = 128
HALO = 16
WINDOW = 64
CHUNK = 32
MESH = pl.DeviceIdType.MESH
BF16 = jnp.bfloat16
F32 = jnp.float32


def layer_norm(values, gain):
    mean = jnp.mean(values, axis=-1, keepdims=True)
    centered = values - mean
    var = jnp.mean(centered * centered, axis=-1, keepdims=True)
    return centered / jnp.sqrt(var + 1e-05) * gain


def matmul(a, b):
    return jnp.dot(a, b, preferred_element_type=F32)


def folded(rows):
    half = rows.shape[0] // 2
    lane = lax.broadcasted_iota(jnp.int32, (half, LANES), 1)
    return jnp.where(lane < HEAD_DIM, pltpu.roll(rows[:half], HEAD_DIM, 1), rows[half:])


def all_heads(ref):
    columns = []
    lane = lax.broadcasted_iota(jnp.int32, ref.shape[1:], 1)
    for pair in range(ref.shape[0] // 2):
        even = ref[2 * pair].astype(F32)
        odd = ref[2 * pair + 1].astype(F32)
        top = jnp.where(lane < HEAD_DIM, even, pltpu.roll(odd, HEAD_DIM, 1))
        bottom = jnp.where(lane < HEAD_DIM, pltpu.roll(even, HEAD_DIM, 1), odd)
        columns.append(jnp.concatenate([top, bottom], axis=0))
    return jnp.concatenate(columns, axis=1)


def layer_kernel(
    side,
    frames_hbm,
    attn_gain_hbm,
    conv_gain_hbm,
    scale_hbm,
    shift_hbm,
    taps_hbm,
    w_query_hbm,
    w_key_hbm,
    w_value_hbm,
    w_out_hbm,
    w_expand_hbm,
    w_project_hbm,
    attended_ref,
    layer_ref,
    frames_ref,
    gains_ref,
    taps_ref,
    w_query,
    w_key,
    w_value,
    w_out,
    w_expand,
    w_project,
    head_send,
    head_recv,
    kv_all,
    near_wide,
    far_wide,
    near_keys,
    far_keys,
    q_all,
    near_scores,
    far_scores,
    near_weights,
    far_weights,
    far_tops,
    first_mixed,
    first_tops,
    part_send,
    part_recv,
    ctx_send,
    ctx_recv,
    edge_send,
    edge_recv,
    context,
    halo_send,
    halo_recv,
    padded,
    load_sem,
    head_ssem,
    head_rsem,
    kv_ssem,
    kv_rsem,
    q_ssem,
    q_rsem,
    part_ssem,
    part_rsem,
    ctx_ssem,
    ctx_rsem,
    edge_ssem,
    edge_rsem,
    halo_ssem,
    halo_rsem,
):
    rows, width = frames_ref.shape
    groups = head_send.shape[0]
    block = rows * groups
    half_block = block // 2
    level_rows = -(-block // LANES)
    blocks = side * side
    tm = lax.axis_index("tm")
    kv = lax.axis_index("kv")
    bits = side.bit_length() - 1
    core = kv & 1
    slow = tm >> bits
    fast = tm & (side - 1)
    key_at = fast + core * (slow - fast)
    key_stride = 1 + core * (side - 1)
    query_at = slow + core * (fast - slow)
    query_stride = side - core * (side - 1)

    def kv_peer(d):
        return (tm, (kv + d) & (groups - 1))

    def key_peer(d):
        return (tm + (((key_at + d) & (side - 1)) - key_at) * key_stride, kv)

    def query_peer(d):
        return (tm + (((query_at + d) & (side - 1)) - query_at) * query_stride, kv)

    devices = groups * blocks
    me = tm * groups + kv
    following = (me + 1) & (devices - 1)
    preceding = (me - 1) & (devices - 1)
    group_bits = groups.bit_length() - 1
    following = (following >> group_bits, following & (groups - 1))
    preceding = (preceding >> group_bits, preceding & (groups - 1))
    later = (tm + 1) & (blocks - 1)
    earlier = (tm - 1) & (blocks - 1)
    far_first = sorted(range(1, groups), key=lambda d: -min(d, groups - d))
    near = sorted(range(1, side), key=lambda d: min(d, side - d))

    def greet(device):
        pl.semaphore_signal(barrier, inc=1, device_id=device, device_id_type=MESH)

    loads = [
        pltpu.make_async_copy(source, target, load_sem.at[i])
        for i, (source, target) in enumerate(
            (
                (frames_hbm, frames_ref),
                (attn_gain_hbm, gains_ref.at[0:1]),
                (w_key_hbm, w_key),
                (w_value_hbm, w_value),
                (w_query_hbm, w_query),
                (w_out_hbm, w_out),
                (w_expand_hbm, w_expand),
                (taps_hbm, taps_ref),
                (conv_gain_hbm, gains_ref.at[1:2]),
                (scale_hbm, gains_ref.at[2:3]),
                (shift_hbm, gains_ref.at[3:4]),
                (w_project_hbm, w_project),
            )
        )
    ]
    for load in loads[:5]:
        load.start()

    barrier = pltpu.get_barrier_semaphore()
    for d in range(1, groups):
        greet(kv_peer(d))
    for d in near[:4]:
        greet(key_peer(d))
        greet(query_peer(d))

    lane = lax.broadcasted_iota(jnp.int32, (rows, LANES), 1)
    low = lane < HEAD_DIM
    first_half = lane % HEAD_DIM < HALF
    which = lax.broadcasted_iota(jnp.int32, (1, LANES), 1) % HALF
    inverse = jnp.zeros((1, LANES), F32)
    for i in range(HALF):
        inverse = jnp.where(which == i, 10000.0 ** (-2.0 * i / HEAD_DIM), inverse)
    positions = me * rows + lax.broadcasted_iota(jnp.int32, (rows, LANES), 0)
    angle = positions.astype(F32) * inverse
    cosine = jnp.cos(angle)
    sine = jnp.sin(angle)
    sine = jnp.where(first_half, -sine, sine)

    def rotated(part):
        swapped = jnp.where(
            first_half, pltpu.roll(part, LANES - HALF, 1), pltpu.roll(part, HALF, 1)
        )
        return part * cosine + swapped * sine

    loads[0].wait()
    loads[1].wait()
    inputs = frames_ref[...].astype(F32)
    halo_send[0] = inputs[:HALO].astype(BF16)
    halo_send[1] = inputs[rows - HALO :].astype(BF16)
    normed = layer_norm(inputs, gains_ref[0:1]).astype(BF16)
    loads[2].wait()
    keys = matmul(normed, w_key[...])
    loads[3].wait()
    values = matmul(normed, w_value[...])
    loads[4].wait()
    queries = matmul(normed, w_query[...])
    to_log2 = 0.125 / math.log(2.0)
    for pair in range(groups // 2):
        at = slice(pair * LANES, (pair + 1) * LANES)
        key = rotated(keys[:, at])
        query = rotated(queries[:, at]) * to_log2
        value = values[:, at]
        key_value = jnp.where(low, key, pltpu.roll(value, HEAD_DIM, 1))
        head_send[2 * pair] = jnp.concatenate(
            [key_value, jnp.where(low, query, 0.0)], axis=0
        ).astype(BF16)
        key_value = jnp.where(low, pltpu.roll(key, HEAD_DIM, 1), value)
        head_send[2 * pair + 1] = jnp.concatenate(
            [key_value, jnp.where(low, pltpu.roll(query, HEAD_DIM, 1), 0.0)], axis=0
        ).astype(BF16)

    pl.semaphore_wait(barrier, groups - 1 + 2 * len(near[:4]))

    head_copies = [
        pltpu.make_async_remote_copy(
            src_ref=head_send.at[(kv + d) & (groups - 1)],
            dst_ref=head_recv.at[kv],
            send_sem=head_ssem.at[d],
            recv_sem=head_rsem.at[d],
            device_id=kv_peer(d),
            device_id_type=MESH,
        )
        for d in far_first
    ]
    for copy in head_copies:
        copy.start()
    for load in loads[5:]:
        load.start()
    head_recv[kv] = head_send[kv]
    for copy in head_copies:
        copy.wait_recv()
    pieces = [head_recv[head].astype(F32) for head in range(groups)]
    own_block = jnp.concatenate([piece[:rows] for piece in pieces], axis=0).astype(BF16)
    kv_all[0] = own_block

    def line_copies(ref, ssem, rsem, peer, halved):
        half = ref.shape[1] // 2
        lower, upper, whole = pl.ds(0, half), pl.ds(half, half), pl.ds(0, 2 * half)
        used = []

        def copy(source, target, rows, place):
            sem = len(used)
            used.append(sem)
            return pltpu.make_async_remote_copy(
                src_ref=ref.at[source, rows],
                dst_ref=ref.at[target, rows],
                send_sem=ssem.at[sem],
                recv_sem=rsem.at[sem],
                device_id=peer(place),
                device_id_type=MESH,
            )

        def entry(place, rows, onward=()):
            return place, copy(0, place, rows, place), [
                (target, copy(place, target, rows, step)) for target, rows, step in onward
            ]

        if side < 8:
            return [entry(d, whole) for d in near]
        if halved:
            return [
                entry(2, lower, [(4, lower, 2), (3, lower, 1)]),
                entry(6, upper, [(4, upper, 6), (5, upper, 7)]),
                entry(2, upper, [(3, upper, 1)]),
                entry(6, lower, [(5, lower, 7)]),
                entry(1, whole),
                entry(7, whole),
            ]
        return [
            entry(2, whole, [(4, lower, 2), (3, whole, 1)]),
            entry(6, whole, [(4, upper, 6), (5, whole, 7)]),
            entry(1, whole),
            entry(7, whole),
        ]

    kv_line = line_copies(kv_all, kv_ssem, kv_rsem, key_peer, True)
    q_line = line_copies(q_all, q_ssem, q_rsem, query_peer, False)
    for _, copy, _ in kv_line:
        copy.start()
    own_queries = jnp.concatenate([piece[rows:] for piece in pieces], axis=0)
    q_all[0] = (
        own_queries[:half_block] + pltpu.roll(own_queries[half_block:], HEAD_DIM, 1)
    ).astype(BF16)
    for _, copy, _ in q_line:
        copy.start()
    for line in (q_line, kv_line):
        for _, copy, onward in line:
            if onward:
                copy.wait_recv()
            for _, relay in onward:
                relay.start()

    slots = [0] + near
    near_count = near_wide.shape[0] // block

    def wait_for(line, wanted):
        for slot, copy, onward in line:
            if slot in wanted and not onward:
                copy.wait_recv()
            for target, relay in onward:
                if target in wanted:
                    relay.wait_recv()

    def lay_out(few, at, wide, keys):
        both = jnp.concatenate([kv_all[d] for d in few], axis=0).astype(F32)
        at = slice(at * block, (at + len(few)) * block)
        keys[:, at] = both.T.astype(BF16)
        lane = lax.broadcasted_iota(jnp.int32, both.shape, 1)
        wide[at] = jnp.where(lane < HEAD_DIM, 1.0, both).astype(BF16)

    def lay_out_line(kv_slots, wide, keys):
        for i in range(0, len(kv_slots), 2):
            wait_for(kv_line, kv_slots[i : i + 2])
            lay_out(kv_slots[i : i + 2], i, wide, keys)

    half_lane = lax.broadcasted_iota(jnp.int32, (half_block, LANES), 1)
    block_lane = lax.broadcasted_iota(jnp.int32, (block, LANES), 1)

    def unfolded(d):
        packed = q_all[d].astype(F32)
        return jnp.concatenate(
            [
                jnp.where(half_lane < HEAD_DIM, packed, 0.0),
                jnp.where(half_lane < HEAD_DIM, pltpu.roll(packed, HEAD_DIM, 1), 0.0),
            ],
            axis=0,
        ).astype(BF16)

    def soften(scores, weights, tops, floor=None):
        for begin in range(0, 2 * block, CHUNK):
            at = slice(begin, begin + CHUNK)
            score = scores[at]
            top = jnp.max(score, axis=1, keepdims=True)
            if floor is not None:
                top = jnp.maximum(top, floor[at, :1])
            weights[at] = jnp.exp2(score - top).astype(BF16)
            tops[at] = jnp.broadcast_to(top, (CHUNK, LANES))

    def finish(d, mixed, top):
        total = jnp.where(block_lane < HEAD_DIM, mixed, pltpu.roll(mixed, HEAD_DIM, 1))
        level = top + jnp.log2(total)
        place = lax.broadcasted_iota(jnp.int32, (HALO, LANES), 0)
        levels = jnp.zeros((HALO, LANES), F32)
        for i in range(level_rows):
            few = level[i * LANES : (i + 1) * LANES]
            row = lax.broadcasted_iota(jnp.int32, few.shape, 0)
            column = lax.broadcasted_iota(jnp.int32, few.shape, 1)
            line = jnp.sum(jnp.where(row == column, few, 0.0), axis=0, keepdims=True)
            high = line.astype(BF16).astype(F32)
            levels = jnp.where(place == i, high, levels)
            levels = jnp.where(place == level_rows + i, line - high, levels)
        part_send[d] = jnp.concatenate(
            [folded(mixed / total), levels], axis=0
        ).astype(BF16)

    def chosen(step, order):
        return sum((step == i).astype(jnp.int32) * d for i, d in enumerate(order))

    steps = side // 2
    pairs = [tuple(slots[2 * step : 2 * step + 2]) for step in range(steps)]
    near_order = [2, 6, 1, 7, 0] if side == 8 else slots[:near_count]
    far_order = slots[near_count:]
    lay_out_line(near_order, near_wide, near_keys)
    wait_for(q_line, slots[:near_count])

    @pl.loop(0, max(steps // 2, 1))
    def _(turn):
        @pl.when(turn == steps // 4)
        def _():
            wait_for(q_line, far_order)

        ahead = min(2, steps)
        for i in range(ahead):
            step = ahead * turn + i
            query = [unfolded(chosen(2 * step + j, slots)) for j in range(2)]
            near_scores[i] = matmul(jnp.concatenate(query, axis=0), near_keys[...])
        for i in range(ahead):
            step = ahead * turn + i
            soften(near_scores.at[i], near_weights.at[i], first_tops.at[step])
            first_mixed[step] = matmul(near_weights[i], near_wide[...])

    lay_out_line(far_order, far_wide, far_keys)

    def part_copy(d):
        return pltpu.make_async_remote_copy(
            src_ref=part_send.at[d],
            dst_ref=part_recv.at[d],
            send_sem=part_ssem.at[d],
            recv_sem=part_rsem.at[d],
            device_id=query_peer(side - d),
            device_id_type=MESH,
        )

    def score_far(step):
        query = jnp.concatenate([unfolded(d) for d in pairs[step]], axis=0)
        far_scores[step] = matmul(query, far_keys[...])

    score_far(steps - 1)
    for step in range(steps - 1, -1, -1):
        if step > 0:
            score_far(step - 1)
        soften(far_scores.at[step], far_weights.at[step], far_tops.at[step], first_tops.at[step])
        top = far_tops[step]
        mixed = first_mixed[step] * jnp.exp2(first_tops[step] - top)
        mixed = mixed + matmul(far_weights[step], far_wide[...])
        for i in (1, 0):
            d = pairs[step][i]
            at = slice(i * block, (i + 1) * block)
            finish(d, mixed[at], top[at])
            if d > 0:
                part_copy(d).start()

    part_recv[0] = part_send[0]
    for d in range(1, side):
        part_copy(d).wait_recv()

    levels = []
    for i in range(level_rows):
        levels.append(
            [
                part_recv[d, half_block + i : half_block + i + 1].astype(F32)
                + part_recv[d, half_block + level_rows + i : half_block + level_rows + i + 1].astype(F32)
                for d in range(side)
            ]
        )
    shares = []
    for level in levels:
        level = jnp.concatenate(level, axis=0)
        fade = jnp.exp2(level - jnp.max(level, axis=0, keepdims=True))
        shares.append(fade / jnp.sum(fade, axis=0, keepdims=True))
    shares = jnp.concatenate(
        shares + [jnp.zeros((LANES - side * level_rows, LANES), F32)], axis=0
    ).T
    upper = []
    begin = half_block
    while begin < block:
        i = begin // LANES
        end = min(block, (i + 1) * LANES)
        few = shares[begin - i * LANES : end - i * LANES]
        upper.append(pltpu.roll(few, LANES - i * side, 1) if i else few)
        begin = end
    lower = shares[:half_block]
    upper = jnp.concatenate(upper, axis=0)
    pick = jnp.zeros((half_block, LANES), F32)
    for i, share in enumerate((lower, upper)):
        high = share.astype(BF16).astype(F32)
        for j, piece in enumerate((high, share - high)):
            begin = (2 * i + j) * side
            piece = pltpu.roll(piece, begin, 1) if begin else piece
            pick = jnp.where((half_lane >= begin) & (half_lane < begin + side), piece, pick)
    index = lax.broadcasted_iota(jnp.int32, (LANES, side * LANES), 0)
    lane = lax.broadcasted_iota(jnp.int32, (LANES, side * LANES), 1)
    spread = (
        (index % side == lane // LANES)
        & (index < 4 * side)
        & (index // (2 * side) == lane % LANES // HEAD_DIM)
    )
    spread = matmul(pick.astype(BF16), jnp.where(spread, 1.0, 0.0).astype(BF16))
    merged = jnp.zeros((half_block, LANES), F32)
    for d in range(side):
        part = part_recv[d].astype(F32)[:half_block]
        merged = merged + spread[:, d * LANES : (d + 1) * LANES] * part
    merged = jnp.concatenate([pltpu.roll(merged, HEAD_DIM, 1), merged], axis=0)

    edge_send[0] = folded(merged[: 2 * HALO]).astype(BF16)
    edge_send[1] = folded(merged[block - 2 * HALO :]).astype(BF16)
    framed = jnp.concatenate(
        [jnp.zeros((HALO, LANES), F32), merged, jnp.zeros((WINDOW - rows - HALO, LANES), F32)],
        axis=0,
    )
    for part in range(groups):
        ctx_send[part] = folded(framed[part * rows : part * rows + WINDOW]).astype(BF16)

    def edge_copy(i, head):
        return pltpu.make_async_remote_copy(
            src_ref=edge_send.at[i],
            dst_ref=edge_recv.at[head],
            send_sem=edge_ssem.at[i],
            recv_sem=edge_rsem.at[head],
            device_id=((earlier, groups - 1), (later, 0))[i],
            device_id_type=MESH,
        )

    for i in range(2):
        edge_copy(i, kv).start()
    ctx_copies = [
        pltpu.make_async_remote_copy(
            src_ref=ctx_send.at[(kv + d) & (groups - 1)],
            dst_ref=ctx_recv.at[kv],
            send_sem=ctx_ssem.at[d],
            recv_sem=ctx_rsem.at[d],
            device_id=kv_peer(d),
            device_id_type=MESH,
        )
        for d in far_first
    ]
    for copy in ctx_copies:
        copy.start()
    halo_copies = [
        pltpu.make_async_remote_copy(
            src_ref=halo_send.at[i],
            dst_ref=halo_recv.at[i],
            send_sem=halo_ssem.at[i],
            recv_sem=halo_rsem.at[i],
            device_id=target,
            device_id_type=MESH,
        )
        for i, target in enumerate((preceding, following))
    ]
    for copy in halo_copies:
        copy.start()
    ctx_recv[kv] = ctx_send[kv]
    for copy in head_copies:
        copy.wait_send()
    for line in (kv_line, q_line):
        for _, copy, onward in line:
            copy.wait_send()
            for _, relay in onward:
                relay.wait_send()
    for d in range(1, side):
        part_copy(d).wait_send()
    for copy in ctx_copies + halo_copies:
        copy.wait_send()
    for i in range(2):
        edge_copy(i, kv).wait_send()
    for load in loads[5:]:
        load.wait()
    for copy in halo_copies:
        copy.wait_recv()
    extent = rows + 2 * HALO
    nearby = jnp.concatenate([halo_recv[1].astype(F32), inputs, halo_recv[0].astype(F32)], axis=0)
    for copy in ctx_copies:
        copy.wait_recv()
    context[...] = all_heads(ctx_recv)[:extent]

    @pl.when(kv == 0)
    def _():
        for head in range(groups):
            edge_copy(1, head).wait_recv()
        context[:HALO] = all_heads(edge_recv)[HALO:]

    @pl.when(kv == groups - 1)
    def _():
        for head in range(groups):
            edge_copy(0, head).wait_recv()
        context[extent - HALO :] = all_heads(edge_recv)[:HALO]

    attended = matmul(context[...].astype(BF16), w_out[...]).astype(BF16).astype(F32)
    attended_ref[...] = attended[HALO : HALO + rows].astype(BF16)
    mid = nearby + attended
    conv_in = layer_norm(mid, gains_ref[1:2]).astype(BF16)
    expanded = matmul(conv_in, w_expand[...])
    gate = expanded[:, width:]
    glu = (expanded[:, :width] / (1.0 + jnp.exp(-gate))).astype(BF16).astype(F32)
    times = me * rows - HALO + lax.broadcasted_iota(jnp.int32, (extent, width), 0)
    padded[...] = jnp.where((times >= 0) & (times < devices * rows), glu, 0.0)

    depth = jnp.zeros((rows, width), F32)
    count = taps_ref.shape[0]
    for turn in range(8):
        shifted = None
        for tap in range(turn - 1, count, 8):
            if tap < 0:
                continue
            term = taps_ref[tap : tap + 1] * padded[tap + 1 - turn : tap + 9 - turn + rows]
            shifted = term if shifted is None else shifted + term
        depth = depth + shifted[turn : turn + rows]
    batch = depth * gains_ref[2:3] + gains_ref[3:4]
    act = (batch / (1.0 + jnp.exp(-batch))).astype(BF16)
    layer_ref[...] = (mid[HALO : HALO + rows] + matmul(act, w_project[...])).astype(BF16)


def copy_kernel(attended_in, layer_in, attended_out, layer_out, sem):
    copies = [
        pltpu.make_async_copy(attended_in, attended_out, sem.at[0]),
        pltpu.make_async_copy(layer_in, layer_out, sem.at[1]),
    ]
    for copy in copies:
        copy.start()
    for copy in copies:
        copy.wait()


def on_device(
    frames,
    attn_gain,
    w_query,
    w_key,
    w_value,
    w_out,
    conv_gain,
    w_expand,
    kernel,
    bn_scale,
    bn_shift,
    w_project,
):
    rows, width = frames.shape
    groups = lax.axis_size("kv")
    side = math.isqrt(lax.axis_size("tm"))
    block = rows * groups
    near_rows = (5 if side == 8 else side // 2) * block
    far_rows = side * block - near_rows
    vmem = pl.BlockSpec(memory_space=pltpu.VMEM)
    anywhere = pl.BlockSpec(memory_space=pl.ANY)
    dma = pltpu.SemaphoreType.DMA
    results = pl.pallas_call(
        functools.partial(layer_kernel, side),
        out_shape=(pltpu.VMEM((rows, width), BF16), pltpu.VMEM((rows, width), BF16)),
        in_specs=[anywhere] * 12,
        out_specs=(vmem, vmem),
        scratch_shapes=[
            pltpu.VMEM((rows, width), BF16),
            pltpu.VMEM((4, width), F32),
            pltpu.VMEM(kernel.shape, F32),
            pltpu.VMEM((width, width), BF16),
            pltpu.VMEM((width, width), BF16),
            pltpu.VMEM((width, width), BF16),
            pltpu.VMEM((width, width), BF16),
            pltpu.VMEM((width, 2 * width), BF16),
            pltpu.VMEM((width, width), BF16),
            pltpu.VMEM((groups, 2 * rows, LANES), BF16),
            pltpu.VMEM((groups, 2 * rows, LANES), BF16),
            pltpu.VMEM((side, block, LANES), BF16),
            pltpu.VMEM((near_rows, LANES), BF16),
            pltpu.VMEM((far_rows, LANES), BF16),
            pltpu.VMEM((LANES, near_rows), BF16),
            pltpu.VMEM((LANES, far_rows), BF16),
            pltpu.VMEM((side, block // 2, LANES), BF16),
            pltpu.VMEM((2, 2 * block, near_rows), F32),
            pltpu.VMEM((side // 2, 2 * block, far_rows), F32),
            pltpu.VMEM((2, 2 * block, near_rows), BF16),
            pltpu.VMEM((side // 2, 2 * block, far_rows), BF16),
            pltpu.VMEM((side // 2, 2 * block, LANES), F32),
            pltpu.VMEM((side // 2, 2 * block, LANES), F32),
            pltpu.VMEM((side // 2, 2 * block, LANES), F32),
            pltpu.VMEM((side, block // 2 + HALO, LANES), BF16),
            pltpu.VMEM((side, block // 2 + HALO, LANES), BF16),
            pltpu.VMEM((groups, WINDOW // 2, LANES), BF16),
            pltpu.VMEM((groups, WINDOW // 2, LANES), BF16),
            pltpu.VMEM((2, HALO, LANES), BF16),
            pltpu.VMEM((groups, HALO, LANES), BF16),
            pltpu.VMEM((rows + 2 * HALO, width), F32),
            pltpu.VMEM((2, HALO, width), BF16),
            pltpu.VMEM((2, HALO, width), BF16),
            pltpu.VMEM((rows + 2 * HALO, width), F32),
            dma((12,)),
            dma((groups,)),
            dma((groups,)),
            dma((2 * side,)),
            dma((2 * side,)),
            dma((side,)),
            dma((side,)),
            dma((side,)),
            dma((side,)),
            dma((groups,)),
            dma((groups,)),
            dma((2,)),
            dma((groups,)),
            dma((2,)),
            dma((2,)),
        ],
        compiler_params=pltpu.CompilerParams(
            collective_id=0, has_side_effects=True, vmem_limit_bytes=60 * 1024 * 1024
        ),
    )(
        frames,
        attn_gain.reshape(1, width),
        conv_gain.reshape(1, width),
        bn_scale.reshape(1, width),
        bn_shift.reshape(1, width),
        kernel,
        w_query,
        w_key,
        w_value,
        w_out,
        w_expand,
        w_project,
    )
    return pl.pallas_call(
        copy_kernel,
        out_shape=(jax.ShapeDtypeStruct((rows, width), BF16),) * 2,
        in_specs=[vmem] * 2,
        out_specs=(anywhere, anywhere),
        scratch_shapes=[dma((2,))],
        compiler_params=pltpu.CompilerParams(vmem_limit_bytes=4 * 1024 * 1024),
    )(*results)


def solution(mesh):
    rows = P(("tm", "kv"), None)
    return jax.shard_map(
        on_device,
        mesh=mesh,
        in_specs=(rows,) + (P(),) * 11,
        out_specs=(rows, rows),
        check_vma=False,
    )
```
